32 devices in a mesh: dp: 2 (over y), row: 4 (over z), col: 4 (over x, core).
Axes of the slice: x: 2, y: 2, z: 4, core: 2. Of those that a mesh axis runs over, the one named last changes fastest.
Arguments:
- hidden_in: bfloat16 [16384, 1088], P(('dp', 'row', 'col')), may hold values from -6 to 6
- cotangent: bfloat16 [16384, 1088], P(('dp', 'row', 'col')), may hold values from -6 to 6
- segments: int32 [16, 1024], P(('dp', 'row')), may hold values from 0 to 3, never falling along the last dimension, each value on 1 to 800 neighbouring positions
- qkv_weight: float32 [1088, 3, 1088], P(('dp', 'row'), None, 'col'), may hold values from -0.1875 to 0.1875
- out_weight: float32 [1088, 1088], P('col', ('dp', 'row')), may hold values from -1.5 to 1.5
- up_weight: float32 [1088, 4352], P(('dp', 'row'), 'col'), may hold values from -0.1875 to 0.1875
- down_weight: float32 [4352, 1088], P('col', ('dp', 'row')), may hold values from -0.09375 to 0.09375
- vectors: float32 [12, 1088], P('col', ('dp', 'row')), may hold values from -1.2 to 1.4, as said below
- qkv_first: float32 [1088, 3, 1088], P(('dp', 'row'), None, 'col'), may hold values from -128 to 128
- out_first: float32 [1088, 1088], P('col', ('dp', 'row')), may hold values from -20 to 20
- up_first: float32 [1088, 4352], P(('dp', 'row'), 'col'), may hold values from -24 to 24
- down_first: float32 [4352, 1088], P('col', ('dp', 'row')), may hold values from -56 to 56
- vectors_first: float32 [12, 1088], P('col', ('dp', 'row')), may hold values from -64 to 64
- qkv_second: float32 [1088, 3, 1088], P(('dp', 'row'), None, 'col'), may hold values from 18.0224 to 294.912
- out_second: float32 [1088, 1088], P('col', ('dp', 'row')), may hold values from 0.49152 to 8.192
- up_second: float32 [1088, 4352], P(('dp', 'row'), 'col'), may hold values from 0.73728 to 11.79648
- down_second: float32 [4352, 1088], P('col', ('dp', 'row')), may hold values from 3.2768 to 55.7056
- vectors_second: float32 [12, 1088], P('col', ('dp', 'row')), may hold values from 4.096 to 65.536
Outputs:
- layer_out: bfloat16 [16384, 1088], P(('dp', 'row', 'col'))
- input_grad: float32 [16384, 1088], P(('dp', 'row', 'col'))
- qkv_first_new: float32 [1088, 3, 1088], P(('dp', 'row'), None, 'col')
- qkv_second_new: float32 [1088, 3, 1088], P(('dp', 'row'), None, 'col')
- qkv_weight_new: float32 [1088, 3, 1088], P(('dp', 'row'), None, 'col')
- out_first_new: float32 [1088, 1088], P('col', ('dp', 'row'))
- out_second_new: float32 [1088, 1088], P('col', ('dp', 'row'))
- out_weight_new: float32 [1088, 1088], P('col', ('dp', 'row'))
- up_first_new: float32 [1088, 4352], P(('dp', 'row'), 'col')
- up_second_new: float32 [1088, 4352], P(('dp', 'row'), 'col')
- up_weight_new: float32 [1088, 4352], P(('dp', 'row'), 'col')
- down_first_new: float32 [4352, 1088], P('col', ('dp', 'row'))
- down_second_new: float32 [4352, 1088], P('col', ('dp', 'row'))
- down_weight_new: float32 [4352, 1088], P('col', ('dp', 'row'))
- vectors_first_new: float32 [12, 1088], P('col', ('dp', 'row'))
- vectors_second_new: float32 [12, 1088], P('col', ('dp', 'row'))
- vectors_new: float32 [12, 1088], P('col', ('dp', 'row'))
The draws below stay inside these ranges and needn't reach their ends.
Inputs may be any that keep to these rules, and one draw needn't show every extreme that they name: `segments`: within each sequence the numbers start at 0 and never fall; each number covers 1 to 800 consecutive tokens, one of them exactly 800. `vectors`: rows 0 and 5 lie within 0.6 to 1.4; the other rows within -1.2 to 1.2.
All inputs are finite; a program needn't handle non-finite values.
Results may differ from the reference program's by a relative error of at most 0.015.
Values may be sent and summed in bfloat16 or wider, within the bound.
No kernel may reach another device: no remote copies, remote signals or barrier semaphores. Data moves between devices by JAX's collectives and lax.ppermute only.
A program may use at most 256 MiB of HBM per device.

```python
import math
import jax
import jax.numpy as jnp
import numpy as np
from jax import lax

D = 1088
HEADS = 17
HEAD_DIM = 64
FF = 4352
SEQ = 1024
DOCS = 4
SEG_MOST = 800
STEP = 5
VROWS = 12
TOKENS = 16384
NSEQ = 16


def draw_vectors(key, part):
    key = jax.random.fold_in(key, 7)
    key_one, key_two = jax.random.split(key)
    row_ids = jnp.arange(VROWS)[:, None]
    noise = jax.random.normal(key_one, (VROWS, D), jnp.float32)
    spread = jax.random.uniform(key_two, (VROWS, D), jnp.float32, -1.0, 1.0)
    gain_rows = (row_ids == 0) | (row_ids == 5)
    return jnp.where(gain_rows, 1.0 + 0.4 * spread, 0.3 * jnp.clip(noise, -4.0, 4.0))


def shard_levels(rng, dims, pieces, low, high):
    def one(dim, shards_of):
        draws = jax.random.uniform(jax.random.fold_in(jax.random.fold_in(rng, 6), dim), (shards_of,), jnp.float32, low / len(pieces), high / len(pieces))
        return jnp.repeat(jnp.exp(draws), dims[dim] // shards_of).reshape((-1,) + (1,) * (len(dims) - dim - 1))

    factor_of = one(*pieces[0])
    for cut in pieces[1:]:
        factor_of = factor_of * one(*cut)
    return factor_of


def split_up(count, total, bound, slope):
    loads = [(1 << 20) // math.isqrt(standing ** slope) + 1 for standing in range(2, count + 1)]
    surplus, holding = total - bound - (count - 1), [1] * (count - 1)
    while surplus > 0:
        candidates = [i for i in range(count - 1) if holding[i] < bound]
        whole, left = sum([loads[i] for i in candidates]), surplus
        for i in candidates:
            extra = min(bound - holding[i], max(1, left * loads[i] // whole), surplus)
            holding[i] = holding[i] + extra
            surplus = surplus - extra
    return np.array([bound] + holding)


def uneven_parts(stream_key, count, total, bound, lean):
    if count == 2:
        one = jax.random.randint(stream_key, (), max(1, total - bound), min(bound, total - 1) + 1)
        return jnp.stack([one, total - one])
    sizes = jnp.asarray(split_up(count, total, bound, lean), jnp.int32)
    pairs = (count - 1) // 2
    giver, receiver = sizes[1:1 + 2 * pairs:2], sizes[2:2 + 2 * pairs:2]
    room = jnp.minimum(giver - 1, bound - receiver)
    passed = jax.random.randint(jax.random.fold_in(stream_key, 1), (pairs,), 0, 1 << 20) % (room + 1)
    sizes = sizes.at[1:1 + 2 * pairs:2].set(giver - passed).at[2:2 + 2 * pairs:2].set(receiver + passed)
    return sizes[jax.random.permutation(jax.random.fold_in(stream_key, 2), count)]


def scatter_about(key, extent, scale, limit, cuts=(), dtype=jnp.bfloat16):
    array = jax.random.normal(key, extent, jnp.float32) * scale
    if len(cuts) > 0:
        array = shard_levels(key, extent, cuts, -0.22, 0.18) * array
    return jnp.clip(array, min=-limit, max=limit).astype(dtype)


def setup_inputs(seed: int = 0) -> dict:
    keys = jax.random.split(jax.random.key(seed), 19)
    hidden_in = scatter_about(keys[0], (TOKENS, D), 1.0, 6.0, ((0, 32),))
    cotangent = scatter_about(keys[1], (TOKENS, D), 1.0, 6.0, ((0, 32),))
    segments = jax.vmap(lambda own: jnp.searchsorted(jnp.cumsum(uneven_parts(own, DOCS, SEQ, SEG_MOST, 0)), jnp.arange(SEQ), side="right"))(jax.random.split(keys[2], NSEQ)).reshape((NSEQ, SEQ)).astype(jnp.int32)
    qkv_weight = scatter_about(keys[3], (D, 3, D), D ** -0.5, 0.1875, ((0, 8), (2, 4)), jnp.float32)
    out_weight = scatter_about(keys[4], (D, D), (D // 64) ** -0.5, 1.5, ((0, 4), (1, 8)), jnp.float32)
    up_weight = scatter_about(keys[5], (D, FF), D ** -0.5, 0.1875, ((0, 8), (1, 4)), jnp.float32)
    down_weight = scatter_about(keys[6], (FF, D), FF ** -0.5, 0.09375, ((0, 4), (1, 8)), jnp.float32)
    vectors = draw_vectors(jax.random.fold_in(keys[18], 71), 0)
    qkv_first = scatter_about(keys[8], (D, 3, D), (0.16 * TOKENS ** 0.5), 128.0, ((0, 8), (2, 4)), jnp.float32)
    out_first = scatter_about(keys[9], (D, D), (0.028 * TOKENS ** 0.5), 20.0, ((0, 4), (1, 8)), jnp.float32)
    up_first = scatter_about(keys[10], (D, FF), (0.033 * TOKENS ** 0.5), 24.0, ((0, 8), (1, 4)), jnp.float32)
    down_first = scatter_about(keys[11], (FF, D), (0.07 * TOKENS ** 0.5), 56.0, ((0, 4), (1, 8)), jnp.float32)
    vectors_first = scatter_about(keys[12], (VROWS, D), (0.077 * TOKENS ** 0.5), 64.0, ((0, 4), (1, 8)), jnp.float32)
    qkv_second = jnp.clip(jnp.exp(math.log(294.912) - 2.7950615 * jax.random.uniform(keys[13], (D, 3, D), jnp.float32) ** shard_levels(keys[13], (D, 3, D), ((0, 8), (2, 4)), -0.2, 0.2)), 18.0224, 294.912)
    out_second = jnp.clip(jnp.exp(math.log(8.192) - 2.8134108 * jax.random.uniform(keys[14], (D, D), jnp.float32) ** shard_levels(keys[14], (D, D), ((0, 4), (1, 8)), -0.2, 0.2)), 0.49152, 8.192)
    up_second = jnp.clip(jnp.exp(math.log(11.79648) - 2.7725887 * jax.random.uniform(keys[15], (D, FF), jnp.float32) ** shard_levels(keys[15], (D, FF), ((0, 8), (1, 4)), -0.2, 0.2)), 0.73728, 11.79648)
    down_second = jnp.clip(jnp.exp(math.log(55.7056) - 2.8332134 * jax.random.uniform(keys[16], (FF, D), jnp.float32) ** shard_levels(keys[16], (FF, D), ((0, 4), (1, 8)), -0.2, 0.2)), 3.2768, 55.7056)
    vectors_second = jnp.clip(jnp.exp(math.log(65.536) - 2.7725887 * jax.random.uniform(keys[17], (VROWS, D), jnp.float32) ** shard_levels(keys[17], (VROWS, D), ((0, 4), (1, 8)), -0.2, 0.2)), 4.096, 65.536)
    return dict(hidden_in=hidden_in, cotangent=cotangent, segments=segments, qkv_weight=qkv_weight, out_weight=out_weight, up_weight=up_weight, down_weight=down_weight, vectors=vectors, qkv_first=qkv_first, out_first=out_first, up_first=up_first, down_first=down_first, vectors_first=vectors_first, qkv_second=qkv_second, out_second=out_second, up_second=up_second, down_second=down_second, vectors_second=vectors_second)


@jax.custom_vjp
def low(v):
    return lax.optimization_barrier(v.astype(jnp.bfloat16)).astype(jnp.float32)

@jax.custom_vjp
def low_back(v):
    return v

def low_keep(v):
    return (low(v), None)

def low_pass(kept, grad):
    return (grad,)

def back_keep(v):
    return (v, None)

def back_low(kept, grad):
    return (low(grad),)
low.defvjp(low_keep, low_pass)
low_back.defvjp(back_keep, back_low)
highest = lax.Precision.HIGHEST
beta_one = 0.9
beta_two = 0.999
epsilon = 1e-08
decay_rate = 0.1

def matmul(left, right):
    return jnp.dot(left, right, precision=highest, preferred_element_type=jnp.float32)

def normalize(rows, gain, shift):
    row_mean = lax.optimization_barrier(jnp.mean(rows, -1, keepdims=True))
    centred = rows - row_mean
    inverse = lax.rsqrt(lax.optimization_barrier(jnp.mean(centred * centred, -1, keepdims=True)) + 1e-05)
    return centred * inverse * gain + shift

def attend(queries, key_rows, values, labels):
    length = queries.shape[0]
    query_heads = queries.reshape(length, HEADS, HEAD_DIM)
    key_heads = key_rows.reshape(length, HEADS, HEAD_DIM)
    value_heads = values.reshape(length, HEADS, HEAD_DIM)
    raw_scores = jnp.einsum('qhd,khd->hqk', query_heads, key_heads, precision=highest) * HEAD_DIM ** (-0.5)
    places = jnp.arange(length)
    allowed = (places[None, :] <= places[:, None]) & (labels[None, :] == labels[:, None])
    scores = jnp.where(allowed[None], low_back(raw_scores), -1000000000.0)
    row_max = lax.optimization_barrier(jnp.max(scores, -1, keepdims=True))
    row_total = lax.optimization_barrier(jnp.sum(jnp.exp(scores - row_max), -1, keepdims=True))
    attn_probs = low(jnp.exp(scores - (row_max + jnp.log(row_total))))
    attn_mixed = jnp.einsum('hqk,khd->qhd', attn_probs, value_heads, precision=highest)
    return low(low_back(attn_mixed.reshape(length, HEADS * HEAD_DIM)))

def layer(seq_rows, qkv_weight, out_weight, up_weight, down_weight, vectors, labels):
    vector_rows = low(vectors)
    normed = low(normalize(seq_rows, vector_rows[0], vector_rows[1]))
    linear = low_back(matmul(normed, low(qkv_weight).reshape(D, 3 * D)))
    bias_rows = jnp.stack([vector_rows[2], jnp.zeros_like(vector_rows[2]), vector_rows[3]])
    projected = low(linear.reshape(-1, 3, D) + bias_rows)
    attn_mixed = attend(projected[:, 0], projected[:, 1], projected[:, 2], labels)
    residual = seq_rows + low_back(matmul(attn_mixed, low(out_weight))) + vector_rows[4]
    normed_two = low(normalize(residual, vector_rows[5], vector_rows[6]))
    up_linear = low_back(matmul(normed_two, low(up_weight))) + vector_rows[8:].reshape(FF)
    active = low(jax.nn.gelu(up_linear, approximate=True))
    return residual + low_back(matmul(active, low(down_weight))) + vector_rows[7]

def adamw(weight, gradient, moment_one, moment_two, step_rate, shrink):
    moment_one = beta_one * moment_one + (1.0 - beta_one) * gradient
    moment_two = beta_two * moment_two + (1.0 - beta_two) * gradient * gradient
    update = moment_one / (1.0 - beta_one ** STEP) / (jnp.sqrt(moment_two / (1.0 - beta_two ** STEP)) + epsilon)
    return (moment_one, moment_two, weight - step_rate * (update + shrink * weight))

def reference(hidden_in, cotangent, segments, qkv_weight, out_weight, up_weight, down_weight, vectors, qkv_first, out_first, up_first, down_first, vectors_first, qkv_second, out_second, up_second, down_second, vectors_second):
    params = (qkv_weight, out_weight, up_weight, down_weight, vectors)
    inputs = hidden_in.astype(jnp.float32).reshape(NSEQ, SEQ, D)
    cotangents = cotangent.astype(jnp.float32).reshape(NSEQ, SEQ, D)

    def one_sequence(grad_sums, sequence_item):
        seq_in, seq_cot, labels = sequence_item

        def forward(seq_rows, *weights):
            return layer(seq_rows, *weights, labels)
        result, pullback = jax.vjp(forward, seq_in, *params)
        gradients = pullback(seq_cot)
        grad_sums = tuple((running + fresh for running, fresh in zip(grad_sums, gradients[1:])))
        return (grad_sums, (result.astype(jnp.bfloat16), gradients[0]))
    zero_grads = tuple((jnp.zeros_like(weight) for weight in params))
    totals, (outputs, input_grads) = lax.scan(one_sequence, zero_grads, (inputs, cotangents, segments))
    qkv_m, qkv_v, qkv_w = adamw(qkv_weight, totals[0], qkv_first, qkv_second, 1.5 * D ** (-0.5), decay_rate)
    out_m, out_v, out_w = adamw(out_weight, totals[1], out_first, out_second, 1.5 * (D // 64) ** (-0.5), decay_rate)
    up_m, up_v, up_w = adamw(up_weight, totals[2], up_first, up_second, 1.5 * D ** (-0.5), decay_rate)
    down_m, down_v, down_w = adamw(down_weight, totals[3], down_first, down_second, 1.5 * FF ** (-0.5), decay_rate)
    vec_m, vec_v, vec_w = adamw(vectors, totals[4], vectors_first, vectors_second, 0.5, 0.0)
    return (outputs.reshape(TOKENS, D), input_grads.reshape(TOKENS, D), qkv_m, qkv_v, qkv_w, out_m, out_v, out_w, up_m, up_v, up_w, down_m, down_v, down_w, vec_m, vec_v, vec_w)
```

```python
import functools

import jax
import jax.numpy as jnp
from jax import lax
from jax.experimental import pallas as pl
from jax.experimental.pallas import tpu as pltpu
from jax.sharding import PartitionSpec as P

D = 1088
HEAD_DIM = 64
FF = 4352
SEQ = 1024
STEP = 5

LANES = 128
VEC_ROWS = 8


beta_one = 0.9
beta_two = 0.999
epsilon = 1e-08
decay_rate = 0.1
masked_score = -1000000000.0

f32 = jnp.float32
bf16 = jnp.bfloat16


def contract(left, right, left_dim, right_dim):
    return lax.dot_general(
        left, right, (((left_dim,), (right_dim,)), ((), ())), preferred_element_type=f32
    )


def contract_first(left, right):
    return contract(left, right, 0, 0)


def contract_last(left, right):
    return contract(left, right, 1, 1)


def normalize(rows, gain, shift):
    row_mean = jnp.mean(rows, -1, keepdims=True)
    centred = rows - row_mean
    inverse = lax.rsqrt(jnp.mean(centred * centred, -1, keepdims=True) + 1e-05)
    scaled = centred * inverse
    return (scaled * gain + shift, scaled, inverse)


def norm_back(grad_out, scaled, inverse, gain):
    grad_scaled = grad_out * gain
    return inverse * (
        grad_scaled
        - jnp.mean(grad_scaled, -1, keepdims=True)
        - scaled * jnp.mean(grad_scaled * scaled, -1, keepdims=True)
    )


def gelu_tanh(values):
    return jax.nn.gelu(values, approximate=True)


def adamw(weight, gradient, moment_one, moment_two, step_rate, shrink):
    moment_one = beta_one * moment_one + (1.0 - beta_one) * gradient
    moment_two = beta_two * moment_two + (1.0 - beta_two) * gradient * gradient
    update = (
        moment_one
        / (1.0 - beta_one**STEP)
        / (jnp.sqrt(moment_two / (1.0 - beta_two**STEP)) + epsilon)
    )
    return (moment_one, moment_two, weight - step_rate * (update + shrink * weight))


def mask_tables(kseg_own, kseg_oth, qseg, bias_own, bias_oth):
    count = bias_own.shape[0]
    key_place = lax.broadcasted_iota(jnp.int32, (count, count), 0)
    query_place = lax.broadcasted_iota(jnp.int32, (count, count), 1)
    same = kseg_own[...] == qseg[...]
    bias_own[...] = jnp.where(same & (key_place <= query_place), 0.0, masked_score)
    bias_oth[...] = jnp.where(kseg_oth[...] == qseg[...], 0.0, masked_score)


def head_lanes(block, half):
    lane = lax.broadcasted_iota(jnp.int32, block.shape, 1)
    return jnp.where((lane // HEAD_DIM) == half, block, jnp.zeros_like(block))


def attention_forward(
    later, qseg, kseg_own, kseg_oth, q, k_own, v_own, k_oth, v_oth, out, lse, bias_own, bias_oth
):
    pair = pl.program_id(0)
    count = q.shape[0]
    step = count // 2

    @pl.when(pair == 0)
    def _():
        mask_tables(kseg_own, kseg_oth, qseg, bias_own, bias_oth)

    def body(with_other):
        queries = q[...] * jnp.asarray(HEAD_DIM**-0.5, bf16)
        values_own = v_own[...].astype(f32).T.astype(bf16)
        values_oth = v_oth[...].astype(f32).T.astype(bf16) if with_other else None
        for part in range(2):
            cols = slice(part * step, (part + 1) * step)
            seen = (part + 1) * step
            pieces = []
            for half in range(2):
                q_head = head_lanes(queries[cols], half)
                rows = slice(half * HEAD_DIM, (half + 1) * HEAD_DIM)
                s_own = contract_last(k_own[:seen], q_head) + bias_own[:seen, cols]
                top = jnp.max(s_own, 0, keepdims=True)
                if with_other:
                    s_oth = contract_last(k_oth[...], q_head) + bias_oth[:, cols]
                    top = jnp.maximum(top, jnp.max(s_oth, 0, keepdims=True))
                e_own = jnp.exp(s_own - top)
                total = jnp.sum(e_own, 0, keepdims=True)
                mixed = jnp.dot(
                    values_own[rows, :seen], e_own.astype(bf16), preferred_element_type=f32
                )
                if with_other:
                    e_oth = jnp.exp(s_oth - top)
                    total = total + jnp.sum(e_oth, 0, keepdims=True)
                    mixed = mixed + jnp.dot(
                        values_oth[rows], e_oth.astype(bf16), preferred_element_type=f32
                    )
                lse[0, half : half + 1, cols] = top + jnp.log(total)
                pieces.append(mixed / total)
            out[cols] = jnp.concatenate(pieces, 0).T.astype(bf16)

    @pl.when(later[0] == 1)
    def _():
        body(True)

    @pl.when(later[0] == 0)
    def _():
        body(False)


def attention_backward(
    later, qseg, kseg_own, kseg_oth, q, k_own, v_own, k_oth, v_oth, grad, out, lse,
    dq, dk_own, dv_own, dk_oth, dv_oth, bias_own, bias_oth,
):
    pair = pl.program_id(0)
    count = q.shape[0]
    step = count // 2

    @pl.when(pair == 0)
    def _():
        mask_tables(kseg_own, kseg_oth, qseg, bias_own, bias_oth)

    def body(with_other):
        scale = jnp.asarray(HEAD_DIM**-0.5, bf16)
        queries = q[...] * scale
        keys_own = k_own[...].astype(f32).T.astype(bf16)
        keys_oth = k_oth[...].astype(f32).T.astype(bf16) if with_other else None
        products = (grad[...].astype(f32) * out[...].astype(f32)).T
        dk_a = [jnp.zeros((step, LANES), f32) for _ in range(2)]
        dv_a = [jnp.zeros((step, LANES), f32) for _ in range(2)]
        dk_b = jnp.zeros((count, LANES), f32)
        dv_b = jnp.zeros((count, LANES), f32)
        for part in range(2):
            cols = slice(part * step, (part + 1) * step)
            pieces = []
            for half in range(2):
                q_head = head_lanes(queries[cols], half)
                g_head = head_lanes(grad[cols], half)
                rows = slice(half * HEAD_DIM, (half + 1) * HEAD_DIM)
                delta = jnp.sum(products[rows, cols], 0, keepdims=True)
                log_total = lse[0, half : half + 1, cols]

                def block(keys, values, bias):
                    probs = jnp.exp(contract_last(keys, q_head) + bias - log_total)
                    d_probs = contract_last(values, g_head)
                    d_scores = (probs * (d_probs - delta)).astype(bf16)
                    dk = jnp.dot(d_scores, q_head, preferred_element_type=f32)
                    dv = jnp.dot(probs.astype(bf16), g_head, preferred_element_type=f32)
                    return (d_scores, dk, dv)

                d_query = jnp.zeros((HEAD_DIM, step), f32)
                for chunk in range(part + 1):
                    span = slice(chunk * step, (chunk + 1) * step)
                    d_scores, dk, dv = block(k_own[span], v_own[span], bias_own[span, cols])
                    dk_a[chunk] = dk_a[chunk] + dk
                    dv_a[chunk] = dv_a[chunk] + dv
                    d_query = d_query + jnp.dot(
                        keys_own[rows, span], d_scores, preferred_element_type=f32
                    )
                if with_other:
                    d_scores, dk, dv = block(k_oth[...], v_oth[...], bias_oth[:, cols])
                    dk_b = dk_b + dk
                    dv_b = dv_b + dv
                    d_query = d_query + jnp.dot(
                        keys_oth[rows], d_scores, preferred_element_type=f32
                    )
                pieces.append(d_query)
            dq[cols] = (jnp.concatenate(pieces, 0).T * HEAD_DIM**-0.5).astype(bf16)
        for chunk in range(2):
            span = slice(chunk * step, (chunk + 1) * step)
            dk_own[span] = dk_a[chunk].astype(bf16)
            dv_own[span] = dv_a[chunk].astype(bf16)
        dk_oth[...] = dk_b.astype(bf16)
        dv_oth[...] = dv_b.astype(bf16)

    @pl.when(later[0] == 1)
    def _():
        body(True)

    @pl.when(later[0] == 0)
    def _():
        body(False)


def attention_specs(count, pairs):
    def whole(shape):
        return pl.BlockSpec(shape, lambda p, later: (0,) * len(shape))

    def lanes(start):
        return pl.BlockSpec((count, LANES), lambda p, later: (0, start + p))

    segments = [whole((1, count)), whole((count, 1)), whole((count, 1))]
    projected = [lanes(0), lanes(pairs), lanes(2 * pairs), lanes(0), lanes(pairs)]
    totals = pl.BlockSpec((1, 2, count), lambda p, later: (p, 0, 0))
    return segments, projected, lanes(0), totals


def attend(later, labels, projected, others):
    count = projected.shape[0]
    pairs = projected.shape[1] // (3 * LANES)
    segments, blocks, wide, totals = attention_specs(count, pairs)
    work = count * count * LANES * pairs * 2
    return pl.pallas_call(
        attention_forward,
        grid_spec=pltpu.PrefetchScalarGridSpec(
            num_scalar_prefetch=1,
            grid=(pairs,),
            in_specs=segments + blocks,
            out_specs=[wide, totals],
            scratch_shapes=[pltpu.VMEM((count, count), f32), pltpu.VMEM((count, count), f32)],
        ),
        out_shape=[
            jax.ShapeDtypeStruct((count, pairs * LANES), bf16),
            jax.ShapeDtypeStruct((pairs, 2, count), f32),
        ],
        compiler_params=pltpu.CompilerParams(vmem_limit_bytes=48 << 20),
        cost_estimate=pl.CostEstimate(
            flops=4 * work, bytes_accessed=6 * count * pairs * LANES * 2, transcendentals=0
        ),
        name="attention_forward",
    )(later, *labels, projected, projected, projected, others, others)


def attend_back(later, labels, projected, others, grad, mixed, log_totals):
    count = projected.shape[0]
    pairs = projected.shape[1] // (3 * LANES)
    segments, blocks, wide, totals = attention_specs(count, pairs)
    work = count * count * LANES * pairs * 2
    return pl.pallas_call(
        attention_backward,
        grid_spec=pltpu.PrefetchScalarGridSpec(
            num_scalar_prefetch=1,
            grid=(pairs,),
            in_specs=segments + blocks + [wide, wide, totals],
            out_specs=[wide] * 5,
            scratch_shapes=[pltpu.VMEM((count, count), f32), pltpu.VMEM((count, count), f32)],
        ),
        out_shape=[jax.ShapeDtypeStruct((count, pairs * LANES), bf16)] * 5,
        compiler_params=pltpu.CompilerParams(vmem_limit_bytes=48 << 20),
        cost_estimate=pl.CostEstimate(
            flops=10 * work, bytes_accessed=12 * count * pairs * LANES * 2, transcendentals=0
        ),
        name="attention_backward",
    )(later, *labels, projected, projected, projected, others, others, grad, mixed, log_totals)


AXES = ("col", "dp", "row")


def gather_blocks(block):
    cols = lax.axis_size("col")
    whole = lax.all_gather(block, AXES, axis=0, tiled=False)
    return whole.reshape(cols, -1, *block.shape)


def scatter_blocks(blocks):
    flat = blocks.reshape(-1, blocks.shape[-1])
    return lax.psum_scatter(flat, AXES, scatter_dimension=0, tiled=True)


def local(
    hidden_in,
    cotangent,
    segments,
    qkv_weight,
    out_weight,
    up_weight,
    down_weight,
    vectors,
    qkv_first,
    out_first,
    up_first,
    down_first,
    vectors_first,
    qkv_second,
    out_second,
    up_second,
    down_second,
    vectors_second,
):
    column = lax.axis_index("col")
    cols = lax.axis_size("col")
    here, width = hidden_in.shape
    rows_own = qkv_weight.shape[0]
    owners = lax.axis_size("dp") * lax.axis_size("row")
    piece = qkv_weight.shape[2]
    halves = SEQ // here
    later = lax.rem(column, halves).reshape(1).astype(jnp.int32)
    padded = -(-width // LANES) * LANES

    vec_shape = vectors.shape
    vec_count = vec_shape[0] * vec_shape[1]
    attn_block = jnp.concatenate(
        [
            jnp.concatenate(
                [qkv_weight.reshape(rows_own, 3 * piece), out_weight.T], 1
            ).astype(bf16),
            jnp.pad(
                vectors.reshape(1, vec_count).astype(bf16),
                ((0, VEC_ROWS - 1), (0, 4 * piece - vec_count)),
            ),
        ],
        0,
    )
    attn_all = gather_blocks(attn_block)
    up_all = gather_blocks(up_weight.astype(bf16)).reshape(cols, width, -1)
    down_all = gather_blocks(down_weight.T.astype(bf16)).reshape(cols, width, -1)

    vec = (
        attn_all[:, :, rows_own, :vec_count]
        .reshape(cols, owners, *vec_shape)
        .transpose(0, 2, 1, 3)
        .reshape(cols * vec_shape[0], width)
        .astype(f32)
    )
    attn_weights = (
        attn_all[:, :, :rows_own]
        .reshape(cols, width, 4, piece)
        .transpose(1, 2, 0, 3)
        .reshape(width, 4, width)
    )
    attn_weights = jnp.pad(attn_weights, ((0, 0), (0, 0), (0, padded - width)))
    qkv_flat = attn_weights[:, :3].reshape(width, 3 * padded)
    out_turned = attn_weights[:, 3]

    def widen(row):
        return jnp.pad(row, (0, padded - width))

    inputs = hidden_in.astype(f32)
    normed_one, scaled_one, inverse_one = normalize(inputs, vec[0], vec[1])
    normed_low = normed_one.astype(bf16)
    bias = jnp.concatenate([widen(vec[2]), jnp.zeros((padded,), f32), widen(vec[3])])
    projected = (jnp.dot(normed_low, qkv_flat, preferred_element_type=f32) + bias).astype(bf16)
    ahead = [(c, c + 1) for c in range(cols - 1) if c % halves + 1 < halves]
    behind = [(b, a) for a, b in ahead]
    others = lax.ppermute(projected[:, padded:], "col", ahead)

    own_half = lax.dynamic_slice_in_dim(segments.reshape(-1), column * here, here, 0)
    first_half = lax.dynamic_slice_in_dim(
        segments.reshape(-1), (column - lax.rem(column, halves)) * here, here, 0
    )
    labels = (own_half.reshape(1, here), own_half.reshape(here, 1), first_half.reshape(here, 1))
    mixed, log_totals = attend(later, labels, projected, others)
    residual = inputs + contract_last(mixed, out_turned) + vec[4]
    normed_two, scaled_two, inverse_two = normalize(residual, vec[5], vec[6])
    normed_two_low = normed_two.astype(bf16)

    branch = jnp.zeros((here, width), f32)
    grad_normed_two = jnp.zeros((here, width), f32)
    grad_up, grad_down, grad_up_bias = [], [], []
    for c in range(cols):
        up_linear = jnp.dot(normed_two_low, up_all[c], preferred_element_type=f32) + vec[8 + c]
        active, gelu_pullback = jax.vjp(gelu_tanh, up_linear)
        active_low = active.astype(bf16)
        branch = branch + contract_last(active_low, down_all[c])
        grad_active = jnp.dot(cotangent, down_all[c], preferred_element_type=f32)
        grad_up_linear = gelu_pullback(grad_active)[0]
        grad_up_low = grad_up_linear.astype(bf16)
        grad_down.append(contract_first(cotangent, active_low).astype(bf16))
        grad_up.append(contract_first(normed_two_low, grad_up_low).astype(bf16))
        grad_up_bias.append(jnp.sum(grad_up_linear, 0))
        grad_normed_two = grad_normed_two + contract_last(grad_up_low, up_all[c])
    layer_out = (residual + branch + vec[7]).astype(bf16)
    sum_down = scatter_blocks(jnp.stack(grad_down)).astype(f32)
    sum_up = scatter_blocks(jnp.stack(grad_up)).astype(f32)

    grad_residual = cotangent.astype(f32) + norm_back(
        grad_normed_two, scaled_two, inverse_two, vec[5]
    )
    grad_residual_low = grad_residual.astype(bf16)
    grad_mixed = jnp.dot(grad_residual_low, out_turned, preferred_element_type=f32).astype(bf16)
    grad_out = contract_first(grad_residual_low, mixed)
    dq, dk_own, dv_own, dk_oth, dv_oth = attend_back(
        later, labels, projected, others, grad_mixed, mixed, log_totals
    )
    back = lax.ppermute(jnp.concatenate([dk_oth, dv_oth], 1), "col", behind)
    grad_kv = jnp.concatenate([dk_own, dv_own], 1).astype(f32) + back.astype(f32)
    grad_projected = jnp.concatenate([dq, grad_kv.astype(bf16)], 1)
    grad_qkv = contract_first(normed_low, grad_projected)
    grad_normed_one = contract_last(grad_projected, qkv_flat)
    input_grad = grad_residual + norm_back(grad_normed_one, scaled_one, inverse_one, vec[0])

    grad_vector = jnp.concatenate(
        [
            jnp.stack(
                [
                    jnp.sum(grad_normed_one * scaled_one, 0),
                    jnp.sum(grad_normed_one, 0),
                    jnp.sum(dq.astype(f32), 0)[:width],
                    jnp.sum(grad_kv[:, padded:], 0)[:width],
                    jnp.sum(grad_residual, 0),
                    jnp.sum(grad_normed_two * scaled_two, 0),
                    jnp.sum(grad_normed_two, 0),
                    jnp.sum(cotangent.astype(f32), 0),
                ]
            ),
            jnp.stack(grad_up_bias),
        ],
        0,
    ).astype(bf16)
    vec_part = (
        grad_vector.reshape(cols, vec_shape[0], owners, vec_shape[1])
        .transpose(0, 2, 1, 3)
        .reshape(cols, owners, 1, vec_count)
    )
    vec_part = jnp.pad(vec_part, ((0, 0), (0, 0), (0, VEC_ROWS - 1), (0, 4 * piece - vec_count)))
    grad_attn = jnp.concatenate(
        [
            grad_qkv.astype(bf16).reshape(width, 3, padded),
            grad_out.astype(bf16).reshape(width, 1, padded),
        ],
        1,
    )[:, :, :width]
    grad_attn = (
        grad_attn.reshape(owners, rows_own, 4, cols, piece)
        .transpose(3, 0, 1, 2, 4)
        .reshape(cols, owners, rows_own, 4 * piece)
    )
    sum_attn = scatter_blocks(jnp.concatenate([grad_attn, vec_part], 2)).astype(f32)
    sum_qkv = sum_attn[:rows_own, : 3 * piece].reshape(rows_own, 3, piece)
    sum_out = sum_attn[:rows_own, 3 * piece :].T
    sum_vector = sum_attn[rows_own, :vec_count].reshape(vec_shape)

    qkv_m, qkv_v, qkv_w = adamw(
        qkv_weight, sum_qkv, qkv_first, qkv_second, 1.5 * D ** (-0.5), decay_rate
    )
    out_m, out_v, out_w = adamw(
        out_weight, sum_out, out_first, out_second, 1.5 * (D // 64) ** (-0.5), decay_rate
    )
    up_m, up_v, up_w = adamw(up_weight, sum_up, up_first, up_second, 1.5 * D ** (-0.5), decay_rate)
    down_m, down_v, down_w = adamw(
        down_weight, sum_down.T, down_first, down_second, 1.5 * FF ** (-0.5), decay_rate
    )
    vec_m, vec_v, vec_w = adamw(vectors, sum_vector, vectors_first, vectors_second, 0.5, 0.0)
    return (
        layer_out,
        input_grad,
        qkv_m,
        qkv_v,
        qkv_w,
        out_m,
        out_v,
        out_w,
        up_m,
        up_v,
        up_w,
        down_m,
        down_v,
        down_w,
        vec_m,
        vec_v,
        vec_w,
    )


def solution(mesh):
    tokens = P(("dp", "row", "col"), None)
    qkv = P(("dp", "row"), None, "col")
    tall = P("col", ("dp", "row"))
    up = P(("dp", "row"), "col")
    state = (qkv, tall, up, tall, tall)
    return jax.shard_map(
        local,
        mesh=mesh,
        in_specs=(tokens, tokens, P(("dp", "row"), None)) + state * 3,
        out_specs=(tokens, tokens)
        + (qkv,) * 3
        + (tall,) * 3
        + (up,) * 3
        + (tall,) * 3
        + (tall,) * 3,
        check_vma=False,
    )
```

```python
import functools

import jax
import jax.numpy as jnp
from jax import lax
from jax.experimental import pallas as pl
from jax.experimental.pallas import tpu as pltpu
from jax.sharding import PartitionSpec as P

D = 1088
HEAD_DIM = 64
FF = 4352
SEQ = 1024
STEP = 5

LANES = 128


beta_one = 0.9
beta_two = 0.999
epsilon = 1e-08
decay_rate = 0.1
masked_score = -1000000000.0

f32 = jnp.float32
bf16 = jnp.bfloat16


def contract(left, right, left_dim, right_dim):
    return lax.dot_general(
        left, right, (((left_dim,), (right_dim,)), ((), ())), preferred_element_type=f32
    )


def contract_first(left, right):
    return contract(left, right, 0, 0)


def contract_last(left, right):
    return contract(left, right, 1, 1)


def normalize(rows, gain, shift):
    row_mean = jnp.mean(rows, -1, keepdims=True)
    centred = rows - row_mean
    inverse = lax.rsqrt(jnp.mean(centred * centred, -1, keepdims=True) + 1e-05)
    scaled = centred * inverse
    return (scaled * gain + shift, scaled, inverse)


def norm_back(grad_out, scaled, inverse, gain):
    grad_scaled = grad_out * gain
    return inverse * (
        grad_scaled
        - jnp.mean(grad_scaled, -1, keepdims=True)
        - scaled * jnp.mean(grad_scaled * scaled, -1, keepdims=True)
    )


def gelu_tanh(values):
    return jax.nn.gelu(values, approximate=True)


def adamw(weight, gradient, moment_one, moment_two, step_rate, shrink):
    moment_one = beta_one * moment_one + (1.0 - beta_one) * gradient
    moment_two = beta_two * moment_two + (1.0 - beta_two) * gradient * gradient
    update = (
        moment_one
        / (1.0 - beta_one**STEP)
        / (jnp.sqrt(moment_two / (1.0 - beta_two**STEP)) + epsilon)
    )
    return (moment_one, moment_two, weight - step_rate * (update + shrink * weight))


def mask_tables(kseg_own, kseg_oth, qseg, bias_own, bias_oth):
    count = bias_own.shape[0]
    key_place = lax.broadcasted_iota(jnp.int32, (count, count), 0)
    query_place = lax.broadcasted_iota(jnp.int32, (count, count), 1)
    same = kseg_own[...] == qseg[...]
    bias_own[...] = jnp.where(same & (key_place <= query_place), 0.0, masked_score)
    bias_oth[...] = jnp.where(kseg_oth[...] == qseg[...], 0.0, masked_score)


def head_lanes(block, half):
    lane = lax.broadcasted_iota(jnp.int32, block.shape, 1)
    return jnp.where((lane // HEAD_DIM) == half, block, jnp.zeros_like(block))


def attention_forward(
    later, qseg, kseg_own, kseg_oth, q, k_own, v_own, k_oth, v_oth, out, lse, bias_own, bias_oth
):
    pair = pl.program_id(0)
    count = q.shape[0]
    step = count // 2

    @pl.when(pair == 0)
    def _():
        mask_tables(kseg_own, kseg_oth, qseg, bias_own, bias_oth)

    def body(with_other):
        queries = q[...] * jnp.asarray(HEAD_DIM**-0.5, bf16)
        values_own = v_own[...].astype(f32).T.astype(bf16)
        values_oth = v_oth[...].astype(f32).T.astype(bf16) if with_other else None
        for part in range(2):
            cols = slice(part * step, (part + 1) * step)
            seen = (part + 1) * step
            pieces = []
            for half in range(2):
                q_head = head_lanes(queries[cols], half)
                rows = slice(half * HEAD_DIM, (half + 1) * HEAD_DIM)
                s_own = contract_last(k_own[:seen], q_head) + bias_own[:seen, cols]
                top = jnp.max(s_own, 0, keepdims=True)
                if with_other:
                    s_oth = contract_last(k_oth[...], q_head) + bias_oth[:, cols]
                    top = jnp.maximum(top, jnp.max(s_oth, 0, keepdims=True))
                e_own = jnp.exp(s_own - top)
                total = jnp.sum(e_own, 0, keepdims=True)
                mixed = jnp.dot(
                    values_own[rows, :seen], e_own.astype(bf16), preferred_element_type=f32
                )
                if with_other:
                    e_oth = jnp.exp(s_oth - top)
                    total = total + jnp.sum(e_oth, 0, keepdims=True)
                    mixed = mixed + jnp.dot(
                        values_oth[rows], e_oth.astype(bf16), preferred_element_type=f32
                    )
                lse[0, half : half + 1, cols] = top + jnp.log(total)
                pieces.append(mixed / total)
            out[cols] = jnp.concatenate(pieces, 0).T.astype(bf16)

    @pl.when(later[0] == 1)
    def _():
        body(True)

    @pl.when(later[0] == 0)
    def _():
        body(False)


def attention_backward(
    later, qseg, kseg_own, kseg_oth, q, k_own, v_own, k_oth, v_oth, grad, out, lse,
    dq, dk_own, dv_own, dk_oth, dv_oth, bias_own, bias_oth,
):
    pair = pl.program_id(0)
    count = q.shape[0]
    step = count // 2

    @pl.when(pair == 0)
    def _():
        mask_tables(kseg_own, kseg_oth, qseg, bias_own, bias_oth)

    def body(with_other):
        scale = jnp.asarray(HEAD_DIM**-0.5, bf16)
        queries = q[...] * scale
        keys_own = k_own[...].astype(f32).T.astype(bf16)
        keys_oth = k_oth[...].astype(f32).T.astype(bf16) if with_other else None
        products = (grad[...].astype(f32) * out[...].astype(f32)).T
        dk_a = [jnp.zeros((step, LANES), f32) for _ in range(2)]
        dv_a = [jnp.zeros((step, LANES), f32) for _ in range(2)]
        dk_b = jnp.zeros((count, LANES), f32)
        dv_b = jnp.zeros((count, LANES), f32)
        for part in range(2):
            cols = slice(part * step, (part + 1) * step)
            pieces = []
            for half in range(2):
                q_head = head_lanes(queries[cols], half)
                g_head = head_lanes(grad[cols], half)
                rows = slice(half * HEAD_DIM, (half + 1) * HEAD_DIM)
                delta = jnp.sum(products[rows, cols], 0, keepdims=True)
                log_total = lse[0, half : half + 1, cols]

                def block(keys, values, bias):
                    probs = jnp.exp(contract_last(keys, q_head) + bias - log_total)
                    d_probs = contract_last(values, g_head)
                    d_scores = (probs * (d_probs - delta)).astype(bf16)
                    dk = jnp.dot(d_scores, q_head, preferred_element_type=f32)
                    dv = jnp.dot(probs.astype(bf16), g_head, preferred_element_type=f32)
                    return (d_scores, dk, dv)

                d_query = jnp.zeros((HEAD_DIM, step), f32)
                for chunk in range(part + 1):
                    span = slice(chunk * step, (chunk + 1) * step)
                    d_scores, dk, dv = block(k_own[span], v_own[span], bias_own[span, cols])
                    dk_a[chunk] = dk_a[chunk] + dk
                    dv_a[chunk] = dv_a[chunk] + dv
                    d_query = d_query + jnp.dot(
                        keys_own[rows, span], d_scores, preferred_element_type=f32
                    )
                if with_other:
                    d_scores, dk, dv = block(k_oth[...], v_oth[...], bias_oth[:, cols])
                    dk_b = dk_b + dk
                    dv_b = dv_b + dv
                    d_query = d_query + jnp.dot(
                        keys_oth[rows], d_scores, preferred_element_type=f32
                    )
                pieces.append(d_query)
            dq[cols] = (jnp.concatenate(pieces, 0).T * HEAD_DIM**-0.5).astype(bf16)
        for chunk in range(2):
            span = slice(chunk * step, (chunk + 1) * step)
            dk_own[span] = dk_a[chunk].astype(bf16)
            dv_own[span] = dv_a[chunk].astype(bf16)
        dk_oth[...] = dk_b.astype(bf16)
        dv_oth[...] = dv_b.astype(bf16)

    @pl.when(later[0] == 1)
    def _():
        body(True)

    @pl.when(later[0] == 0)
    def _():
        body(False)


def attention_specs(count, pairs):
    def whole(shape):
        return pl.BlockSpec(shape, lambda p, later: (0,) * len(shape))

    def lanes(start):
        return pl.BlockSpec((count, LANES), lambda p, later: (0, start + p))

    segments = [whole((1, count)), whole((count, 1)), whole((count, 1))]
    projected = [lanes(0), lanes(pairs), lanes(2 * pairs), lanes(0), lanes(pairs)]
    totals = pl.BlockSpec((1, 2, count), lambda p, later: (p, 0, 0))
    return segments, projected, lanes(0), totals


def attend(later, labels, projected, others):
    count = projected.shape[0]
    pairs = projected.shape[1] // (3 * LANES)
    segments, blocks, wide, totals = attention_specs(count, pairs)
    work = count * count * LANES * pairs * 2
    return pl.pallas_call(
        attention_forward,
        grid_spec=pltpu.PrefetchScalarGridSpec(
            num_scalar_prefetch=1,
            grid=(pairs,),
            in_specs=segments + blocks,
            out_specs=[wide, totals],
            scratch_shapes=[pltpu.VMEM((count, count), f32), pltpu.VMEM((count, count), f32)],
        ),
        out_shape=[
            jax.ShapeDtypeStruct((count, pairs * LANES), bf16),
            jax.ShapeDtypeStruct((pairs, 2, count), f32),
        ],
        compiler_params=pltpu.CompilerParams(vmem_limit_bytes=48 << 20),
        cost_estimate=pl.CostEstimate(
            flops=4 * work, bytes_accessed=6 * count * pairs * LANES * 2, transcendentals=0
        ),
        name="attention_forward",
    )(later, *labels, projected, projected, projected, others, others)


def attend_back(later, labels, projected, others, grad, mixed, log_totals):
    count = projected.shape[0]
    pairs = projected.shape[1] // (3 * LANES)
    segments, blocks, wide, totals = attention_specs(count, pairs)
    work = count * count * LANES * pairs * 2
    return pl.pallas_call(
        attention_backward,
        grid_spec=pltpu.PrefetchScalarGridSpec(
            num_scalar_prefetch=1,
            grid=(pairs,),
            in_specs=segments + blocks + [wide, wide, totals],
            out_specs=[wide] * 5,
            scratch_shapes=[pltpu.VMEM((count, count), f32), pltpu.VMEM((count, count), f32)],
        ),
        out_shape=[jax.ShapeDtypeStruct((count, pairs * LANES), bf16)] * 5,
        compiler_params=pltpu.CompilerParams(vmem_limit_bytes=48 << 20),
        cost_estimate=pl.CostEstimate(
            flops=10 * work, bytes_accessed=12 * count * pairs * LANES * 2, transcendentals=0
        ),
        name="attention_backward",
    )(later, *labels, projected, projected, projected, others, others, grad, mixed, log_totals)


def place_kernel(spans, piece, sources, biased, continued, places, x, *refs):
    weights, refs = refs[:sources], refs[sources:]
    bias, refs = (refs[0], refs[1:]) if biased else (None, refs)
    before, refs = (refs[0], refs[1:]) if continued else (None, refs)
    out, whole, product = refs
    step = pl.program_id(0)
    each = pl.num_programs(0) // sources

    @pl.when(step == 0)
    def _():
        whole[...] = before[...].astype(f32) if continued else jnp.zeros_like(whole)

    for k, weight in enumerate(weights):

        @pl.when(step // each == k)
        def _(weight=weight):
            product[...] = jnp.dot(x[...], weight[0], preferred_element_type=f32)

    for place in range(x.shape[1] // piece):

        @pl.when(places[step] == place)
        def _(place=place):
            for source, target in spans:
                start = target + place * piece
                block = product[:, source : source + piece]
                if biased:
                    block = block + bias[:, start : start + piece]
                whole[:, start : start + piece] = block

    @pl.when(step == pl.num_programs(0) - 1)
    def _():
        out[...] = whole[...].astype(bf16)


def multiply_and_place(places, x, weights, lanes, lane_block, spans, piece, out_lanes, bias, before):
    count, depth = x.shape
    each = weights[0].shape[0]
    sources = len(weights)

    def fixed(shape):
        return pl.BlockSpec(shape, lambda j, places: (0, 0))

    in_specs = [fixed((count, depth))]
    for k in range(sources):
        in_specs.append(
            pl.BlockSpec(
                (1, depth, lanes),
                lambda j, places, k=k: (jnp.clip(j - k * each, 0, each - 1), 0, lane_block),
            )
        )
    operands = [x, *weights]
    if bias is not None:
        in_specs.append(fixed(bias.shape))
        operands.append(bias)
    if before is not None:
        in_specs.append(fixed(before.shape))
        operands.append(before)
    return pl.pallas_call(
        functools.partial(
            place_kernel, spans, piece, sources, bias is not None, before is not None
        ),
        grid_spec=pltpu.PrefetchScalarGridSpec(
            num_scalar_prefetch=1,
            grid=(each * sources,),
            in_specs=in_specs,
            out_specs=fixed((count, out_lanes)),
            scratch_shapes=[pltpu.VMEM((count, out_lanes), f32), pltpu.VMEM((count, lanes), f32)],
        ),
        out_shape=jax.ShapeDtypeStruct((count, out_lanes), bf16),
        compiler_params=pltpu.CompilerParams(vmem_limit_bytes=48 << 20),
        cost_estimate=pl.CostEstimate(
            flops=2 * count * depth * lanes * each * sources,
            bytes_accessed=2 * (each * sources * depth * lanes + count * (depth + out_lanes)),
            transcendentals=0,
        ),
        name="multiply_and_place",
    )(places, *operands)


def split_both(parity, cols, write):
    for p in range(2):

        @pl.when(parity[0] == p)
        def _(p=p):
            for i in range(cols // 2):
                write(0, i, p + 2 * i)
                write(1, i, 1 - p + 2 * i)


def split_mixed_kernel(piece, cols, lead, parity, mixed, own, oth):
    count, lanes = own.shape[1:]
    values = mixed[...].astype(f32)
    before = jnp.zeros((count, lead), f32)
    after = jnp.zeros((count, lanes - lead - piece), f32)

    def write(which, i, c):
        block = values[:, c * piece : (c + 1) * piece]
        (own, oth)[which][i] = jnp.concatenate([before, block, after], 1).astype(bf16)

    split_both(parity, cols, write)


def split_grads_kernel(piece, cols, parity, dq, dk, dv, back, own, oth, sums):
    count, lanes = own.shape[1:]
    wide = dq.shape[1]
    grads = [
        dq[...].astype(f32),
        dk[...].astype(f32) + back[:, :wide].astype(f32),
        dv[...].astype(f32) + back[:, wide:].astype(f32),
    ]
    sums[0:1] = jnp.sum(grads[0], 0, keepdims=True)
    sums[1:2] = jnp.sum(grads[2], 0, keepdims=True)
    after = jnp.zeros((count, lanes - 3 * piece), f32)

    def write(which, i, c):
        blocks = [g[:, c * piece : (c + 1) * piece] for g in grads]
        (own, oth)[which][i] = jnp.concatenate([*blocks, after], 1).astype(bf16)

    split_both(parity, cols, write)


def whole_specs(shapes):
    return [pl.BlockSpec(s, lambda i, p, n=len(s): (0,) * n) for s in shapes]


def split_call(kernel, parity, operands, out_shapes, name):
    moved = sum(x.size * x.dtype.itemsize for x in operands) * 2
    return pl.pallas_call(
        kernel,
        grid_spec=pltpu.PrefetchScalarGridSpec(
            num_scalar_prefetch=1,
            grid=(1,),
            in_specs=whole_specs([x.shape for x in operands]),
            out_specs=whole_specs([s.shape for s in out_shapes]),
        ),
        out_shape=out_shapes,
        compiler_params=pltpu.CompilerParams(vmem_limit_bytes=48 << 20),
        cost_estimate=pl.CostEstimate(flops=moved, bytes_accessed=moved, transcendentals=0),
        name=name,
    )(parity, *operands)


def block_grads_kernel(lane_lead, joined, left_one, left_two, grads, mixed, vec_part, *refs):
    received, out, total = refs if joined else (None, *refs)
    lanes_one = grads.shape[2]
    total[:, :lanes_one] = jnp.dot(left_one[...], grads[0], preferred_element_type=f32)
    total[:, lanes_one:] = jnp.zeros_like(total[:, lanes_one:])
    total[:, lane_lead:] += jnp.dot(left_two[...], mixed[0], preferred_element_type=f32)
    total[:, -LANES:] += vec_part[0].astype(f32)
    whole = total[...]
    if joined:
        whole = whole + received[0].astype(f32)
    out[0] = whole.astype(bf16)


def block_grads(left_one, left_two, grads, mixed, vec_part, received, lane_lead):
    each, count, _ = grads.shape
    width = left_one.shape[0]
    lanes = lane_lead + mixed.shape[2]

    def fixed(shape):
        return pl.BlockSpec(shape, lambda i: (0, 0))

    def step(shape):
        return pl.BlockSpec((1, *shape[1:]), lambda i: (i, 0, 0))

    operands = [left_one, left_two, grads, mixed, vec_part]
    in_specs = [fixed(left_one.shape), fixed(left_two.shape)]
    in_specs += [step(x.shape) for x in operands[2:]]
    if received is not None:
        operands.append(received)
        in_specs.append(step(received.shape))
    return pl.pallas_call(
        functools.partial(block_grads_kernel, lane_lead, received is not None),
        grid=(each,),
        in_specs=in_specs,
        out_specs=step((each, width, lanes)),
        out_shape=jax.ShapeDtypeStruct((each, width, lanes), bf16),
        scratch_shapes=[pltpu.VMEM((width, lanes), f32)],
        compiler_params=pltpu.CompilerParams(vmem_limit_bytes=48 << 20),
        cost_estimate=pl.CostEstimate(
            flops=2 * each * count * width * (grads.shape[2] + mixed.shape[2]),
            bytes_accessed=2 * each * width * lanes * 2,
            transcendentals=0,
        ),
        name="block_grads",
    )(*operands)


AXES = ("col", "dp", "row")


def planes():
    owners = lax.axis_size("dp") * lax.axis_size("row")
    cols = lax.axis_size("col")
    return [
        [c * owners + k for c in range(p, cols, 2) for k in range(owners)] for p in range(2)
    ]


def partner(block):
    pairs = [(c, c ^ 1) for c in range(lax.axis_size("col"))]
    return lax.ppermute(block, "col", pairs)


def gather_plane(block):
    whole = lax.all_gather(block, AXES, axis=0, tiled=False, axis_index_groups=planes())
    return whole.reshape(lax.axis_size("col") // 2, -1, block.shape[-1])


def scatter_plane(blocks):
    flat = blocks.reshape(-1, blocks.shape[-1])
    return lax.psum_scatter(
        flat, AXES, scatter_dimension=0, tiled=True, axis_index_groups=planes()
    )


def local(
    hidden_in,
    cotangent,
    segments,
    qkv_weight,
    out_weight,
    up_weight,
    down_weight,
    vectors,
    qkv_first,
    out_first,
    up_first,
    down_first,
    vectors_first,
    qkv_second,
    out_second,
    up_second,
    down_second,
    vectors_second,
):
    column = lax.axis_index("col")
    cols = lax.axis_size("col")
    here, width = hidden_in.shape
    rows_own = qkv_weight.shape[0]
    owners = lax.axis_size("dp") * lax.axis_size("row")
    piece = qkv_weight.shape[2]
    halves = SEQ // here
    each = cols // 2
    odd = lax.rem(column, 2)
    even_here = odd == 0
    parity = odd.reshape(1).astype(jnp.int32)
    places_own = (odd + 2 * jnp.arange(each)).astype(jnp.int32)
    places_oth = (1 - odd + 2 * jnp.arange(each)).astype(jnp.int32)
    later = lax.rem(column, halves).reshape(1).astype(jnp.int32)
    padded = -(-width // LANES) * LANES
    spare = padded - width
    lanes_qkv = -(-3 * piece // LANES) * LANES
    lead_out = 3 * piece // LANES * LANES
    lanes_out = padded - lead_out

    def by_parity(own, oth):
        return jnp.where(even_here, own, oth), jnp.where(even_here, oth, own)

    vec_shape = vectors.shape
    vec_count = vec_shape[0] * vec_shape[1]
    vec_lines = -(-vec_count // spare)
    vec_fill = vec_lines * spare - vec_count
    vec_lanes = jnp.pad(vectors.reshape(vec_count).astype(bf16), (0, vec_fill))
    attn_block = jnp.concatenate(
        [
            qkv_weight.reshape(rows_own, 3 * piece).astype(bf16),
            out_weight.T.astype(bf16),
            jnp.pad(vec_lanes.reshape(vec_lines, spare), ((0, rows_own - vec_lines), (0, 0))),
        ],
        1,
    )
    attn_own = gather_plane(attn_block)
    vec_own = attn_own.reshape(each, owners, rows_own, padded)[:, :, :vec_lines, width:]
    vec_oth = partner(vec_own)
    attn_oth = partner(attn_own)
    up_own = gather_plane(up_weight.astype(bf16))
    up_oth = partner(up_own)
    down_own = gather_plane(down_weight.T.astype(bf16))
    down_oth = partner(down_own)

    def vec_rows(lines):
        lines = lines.reshape(each, owners, vec_lines * spare)[:, :, :vec_count]
        lines = lines.reshape(each, owners, *vec_shape).transpose(0, 2, 1, 3)
        return lines.reshape(each, vec_shape[0], width).astype(f32)

    vec = jnp.stack(by_parity(vec_rows(vec_own), vec_rows(vec_oth)), 1).reshape(-1, width)

    def widen(row):
        return jnp.pad(row, (0, spare))

    inputs = hidden_in.astype(f32)
    normed_one, scaled_one, inverse_one = normalize(inputs, vec[0], vec[1])
    normed_low = normed_one.astype(bf16)
    bias = jnp.concatenate([widen(vec[2]), jnp.zeros((padded,), f32), widen(vec[3])]).reshape(1, -1)
    spans = tuple((part * piece, part * padded) for part in range(3))
    projected = None
    for places, weights in ((places_own, attn_own), (places_oth, attn_oth)):
        projected = multiply_and_place(
            places, normed_low, [weights], lanes_qkv, 0, spans, piece, 3 * padded, bias, projected
        )
    ahead = [(c, c + 1) for c in range(cols - 1) if c % halves + 1 < halves]
    behind = [(b, a) for a, b in ahead]
    others = lax.ppermute(projected[:, padded:], "col", ahead)

    own_half = lax.dynamic_slice_in_dim(segments.reshape(-1), column * here, here, 0)
    first_half = lax.dynamic_slice_in_dim(
        segments.reshape(-1), (column - lax.rem(column, halves)) * here, here, 0
    )
    labels = (own_half.reshape(1, here), own_half.reshape(here, 1), first_half.reshape(here, 1))
    mixed, log_totals = attend(later, labels, projected, others)
    mixed_shape = jax.ShapeDtypeStruct((each, here, lanes_out), bf16)
    lead = 3 * piece - lead_out
    mixed_own, mixed_oth = split_call(
        functools.partial(split_mixed_kernel, piece, cols, lead),
        parity,
        [mixed],
        [mixed_shape] * 2,
        "split_mixed",
    )
    residual = inputs + vec[4]
    for blocks, weights in ((mixed_own, attn_own), (mixed_oth, attn_oth)):
        for i in range(each):
            residual = residual + contract_last(blocks[i], weights[i][:, lead_out:])
    normed_two, scaled_two, inverse_two = normalize(residual, vec[5], vec[6])
    normed_two_low = normed_two.astype(bf16)

    bias_even, bias_odd = vec[8::2], vec[9::2]
    bias_own, bias_oth = by_parity(bias_even, bias_odd)

    def up_part(ups, biases):
        return [
            jnp.dot(normed_two_low, ups[i], preferred_element_type=f32) + biases[i]
            for i in range(each)
        ]

    linear_own = up_part(up_own, bias_own)
    linear_oth = up_part(up_oth, bias_oth)
    (linear_own, linear_oth, down_own) = lax.optimization_barrier(
        (linear_own, linear_oth, down_own)
    )
    branch = jnp.zeros((here, width), f32)

    def forward_part(linears, downs, branch):
        lows, pullbacks = [], []
        for i in range(each):
            active, pullback = jax.vjp(gelu_tanh, linears[i])
            lows.append(active.astype(bf16))
            pullbacks.append(pullback)
            branch = branch + contract_last(lows[i], downs[i])
        return lows, pullbacks, branch

    lows_own, pull_own, branch = forward_part(linear_own, down_own, branch)
    lows_oth, pull_oth, branch = forward_part(linear_oth, down_oth, branch)
    layer_out = (residual + branch + vec[7]).astype(bf16)

    def paired_sum(left, rights_own, rights_oth):
        send = jnp.stack([contract_first(left, r).astype(bf16) for r in rights_oth])
        received = partner(send)
        total = jnp.stack(
            [
                (contract_first(left, r) + received[i].astype(f32)).astype(bf16)
                for i, r in enumerate(rights_own)
            ]
        )
        return scatter_plane(total).astype(f32)

    sum_down = paired_sum(cotangent, lows_own, lows_oth)

    grad_normed_two = jnp.zeros((here, width), f32)

    def backward_part(ups, downs, pullbacks, grad_normed_two):
        lows, sums = [], []
        for i in range(each):
            grad_active = jnp.dot(cotangent, downs[i], preferred_element_type=f32)
            grad_linear = pullbacks[i](grad_active)[0]
            lows.append(grad_linear.astype(bf16))
            sums.append(jnp.sum(grad_linear, 0))
            grad_normed_two = grad_normed_two + contract_last(lows[i], ups[i])
        return lows, sums, grad_normed_two

    dups_oth, dbias_oth, grad_normed_two = backward_part(
        up_oth, down_oth, pull_oth, grad_normed_two
    )
    dups_own, dbias_own, grad_normed_two = backward_part(
        up_own, down_own, pull_own, grad_normed_two
    )
    sum_up = paired_sum(normed_two_low, dups_own, dups_oth)

    grad_residual = cotangent.astype(f32) + norm_back(
        grad_normed_two, scaled_two, inverse_two, vec[5]
    )
    grad_residual_low = grad_residual.astype(bf16)
    grad_mixed = multiply_and_place(
        jnp.concatenate([places_own, places_oth]),
        grad_residual_low,
        [attn_own, attn_oth],
        lanes_out,
        lead_out // lanes_out,
        ((lead, 0),),
        piece,
        padded,
        None,
        None,
    )
    dq, dk_own, dv_own, dk_oth, dv_oth = attend_back(
        later, labels, projected, others, grad_mixed, mixed, log_totals
    )
    back = lax.ppermute(jnp.concatenate([dk_oth, dv_oth], 1), "col", behind)
    grads_shape = jax.ShapeDtypeStruct((each, here, lanes_qkv), bf16)
    grads_own, grads_oth, grad_sums = split_call(
        functools.partial(split_grads_kernel, piece, cols),
        parity,
        [dq, dk_own, dv_own, back],
        [grads_shape, grads_shape, jax.ShapeDtypeStruct((8, padded), f32)],
        "split_grads",
    )
    grad_normed_one = jnp.zeros((here, width), f32)
    for blocks, weights in ((grads_own, attn_own), (grads_oth, attn_oth)):
        for i in range(each):
            grad_normed_one = grad_normed_one + contract_last(blocks[i], weights[i][:, :lanes_qkv])
    input_grad = grad_residual + norm_back(grad_normed_one, scaled_one, inverse_one, vec[0])

    dbias_even, dbias_odd = by_parity(jnp.stack(dbias_own), jnp.stack(dbias_oth))
    grad_vector = jnp.concatenate(
        [
            jnp.stack(
                [
                    jnp.sum(grad_normed_one * scaled_one, 0),
                    jnp.sum(grad_normed_one, 0),
                    grad_sums[0, :width],
                    grad_sums[1, :width],
                    jnp.sum(grad_residual, 0),
                    jnp.sum(grad_normed_two * scaled_two, 0),
                    jnp.sum(grad_normed_two, 0),
                    jnp.sum(cotangent.astype(f32), 0),
                ]
            ),
            jnp.stack([dbias_even, dbias_odd], 1).reshape(cols, width),
        ],
        0,
    ).astype(bf16)
    vec_part = grad_vector.reshape(cols, vec_shape[0], owners, vec_shape[1]).transpose(0, 2, 1, 3)
    vec_part = jnp.pad(vec_part.reshape(cols, owners, vec_count), ((0, 0), (0, 0), (0, vec_fill)))
    vec_part = jnp.pad(
        vec_part.reshape(cols, owners, vec_lines, spare),
        ((0, 0), (0, 0), (0, rows_own - vec_lines), (LANES - spare, 0)),
    ).reshape(cols, width, LANES)
    vec_here, vec_there = by_parity(vec_part[0::2], vec_part[1::2])
    left_one, left_two = normed_low.T, grad_residual_low.T
    received = partner(
        block_grads(left_one, left_two, grads_oth, mixed_oth, vec_there, None, lead_out)
    )
    sum_attn = scatter_plane(
        block_grads(left_one, left_two, grads_own, mixed_own, vec_here, received, lead_out)
    ).astype(f32)
    sum_qkv = sum_attn[:, : 3 * piece].reshape(rows_own, 3, piece)
    sum_out = sum_attn[:, 3 * piece : width].T
    sum_vector = sum_attn[:vec_lines, width:].reshape(-1)[:vec_count].reshape(vec_shape)

    qkv_m, qkv_v, qkv_w = adamw(
        qkv_weight, sum_qkv, qkv_first, qkv_second, 1.5 * D ** (-0.5), decay_rate
    )
    out_m, out_v, out_w = adamw(
        out_weight, sum_out, out_first, out_second, 1.5 * (D // 64) ** (-0.5), decay_rate
    )
    up_m, up_v, up_w = adamw(up_weight, sum_up, up_first, up_second, 1.5 * D ** (-0.5), decay_rate)
    down_m, down_v, down_w = adamw(
        down_weight, sum_down.T, down_first, down_second, 1.5 * FF ** (-0.5), decay_rate
    )
    vec_m, vec_v, vec_w = adamw(vectors, sum_vector, vectors_first, vectors_second, 0.5, 0.0)
    return (
        layer_out,
        input_grad,
        qkv_m,
        qkv_v,
        qkv_w,
        out_m,
        out_v,
        out_w,
        up_m,
        up_v,
        up_w,
        down_m,
        down_v,
        down_w,
        vec_m,
        vec_v,
        vec_w,
    )


def solution(mesh):
    tokens = P(("dp", "row", "col"), None)
    qkv = P(("dp", "row"), None, "col")
    tall = P("col", ("dp", "row"))
    up = P(("dp", "row"), "col")
    state = (qkv, tall, up, tall, tall)
    return jax.shard_map(
        local,
        mesh=mesh,
        in_specs=(tokens, tokens, P(("dp", "row"), None)) + state * 3,
        out_specs=(tokens, tokens)
        + (qkv,) * 3
        + (tall,) * 3
        + (up,) * 3
        + (tall,) * 3
        + (tall,) * 3,
        check_vma=False,
    )
```

```python
import functools

import jax
import jax.numpy as jnp
from jax import lax
from jax.experimental import pallas as pl
from jax.experimental.pallas import tpu as pltpu
from jax.sharding import PartitionSpec as P

D = 1088
HEAD_DIM = 64
FF = 4352
SEQ = 1024
STEP = 5

LANES = 128


beta_one = 0.9
beta_two = 0.999
epsilon = 1e-08
decay_rate = 0.1
masked_score = -1000000000.0

f32 = jnp.float32
bf16 = jnp.bfloat16


def contract(left, right, left_dim, right_dim):
    return lax.dot_general(
        left, right, (((left_dim,), (right_dim,)), ((), ())), preferred_element_type=f32
    )


def contract_first(left, right):
    return contract(left, right, 0, 0)


def contract_last(left, right):
    return contract(left, right, 1, 1)


def normalize(rows, gain, shift):
    row_mean = jnp.mean(rows, -1, keepdims=True)
    centred = rows - row_mean
    inverse = lax.rsqrt(jnp.mean(centred * centred, -1, keepdims=True) + 1e-05)
    scaled = centred * inverse
    return (scaled * gain + shift, scaled, inverse)


def norm_back(grad_out, scaled, inverse, gain):
    grad_scaled = grad_out * gain
    return inverse * (
        grad_scaled
        - jnp.mean(grad_scaled, -1, keepdims=True)
        - scaled * jnp.mean(grad_scaled * scaled, -1, keepdims=True)
    )


def gelu_tanh(values):
    return jax.nn.gelu(values, approximate=True)


def adamw(weight, gradient, moment_one, moment_two, step_rate, shrink):
    moment_one = beta_one * moment_one + (1.0 - beta_one) * gradient
    moment_two = beta_two * moment_two + (1.0 - beta_two) * gradient * gradient
    update = (
        moment_one
        / (1.0 - beta_one**STEP)
        / (jnp.sqrt(moment_two / (1.0 - beta_two**STEP)) + epsilon)
    )
    return (moment_one, moment_two, weight - step_rate * (update + shrink * weight))


def mask_tables(kseg_own, kseg_oth, qseg, bias_own, bias_oth):
    count = bias_own.shape[0]
    key_place = lax.broadcasted_iota(jnp.int32, (count, count), 0)
    query_place = lax.broadcasted_iota(jnp.int32, (count, count), 1)
    same = kseg_own[...] == qseg[...]
    bias_own[...] = jnp.where(same & (key_place <= query_place), 0.0, masked_score)
    bias_oth[...] = jnp.where(kseg_oth[...] == qseg[...], 0.0, masked_score)


def head_lanes(block, half):
    lane = lax.broadcasted_iota(jnp.int32, block.shape, 1)
    return jnp.where((lane // HEAD_DIM) == half, block, jnp.zeros_like(block))


def attention_forward(
    later, qseg, kseg_own, kseg_oth, q, k_own, v_own, k_oth, v_oth, out, lse, bias_own, bias_oth
):
    pair = pl.program_id(0)
    count = q.shape[0]
    step = count // 2

    @pl.when(pair == 0)
    def _():
        mask_tables(kseg_own, kseg_oth, qseg, bias_own, bias_oth)

    def body(with_other):
        queries = q[...] * jnp.asarray(HEAD_DIM**-0.5, bf16)
        values_own = v_own[...].astype(f32).T.astype(bf16)
        values_oth = v_oth[...].astype(f32).T.astype(bf16) if with_other else None
        for part in range(2):
            cols = slice(part * step, (part + 1) * step)
            seen = (part + 1) * step
            pieces = []
            for half in range(2):
                q_head = head_lanes(queries[cols], half)
                rows = slice(half * HEAD_DIM, (half + 1) * HEAD_DIM)
                s_own = contract_last(k_own[:seen], q_head) + bias_own[:seen, cols]
                top = jnp.max(s_own, 0, keepdims=True)
                if with_other:
                    s_oth = contract_last(k_oth[...], q_head) + bias_oth[:, cols]
                    top = jnp.maximum(top, jnp.max(s_oth, 0, keepdims=True))
                e_own = jnp.exp(s_own - top)
                total = jnp.sum(e_own, 0, keepdims=True)
                mixed = jnp.dot(
                    values_own[rows, :seen], e_own.astype(bf16), preferred_element_type=f32
                )
                if with_other:
                    e_oth = jnp.exp(s_oth - top)
                    total = total + jnp.sum(e_oth, 0, keepdims=True)
                    mixed = mixed + jnp.dot(
                        values_oth[rows], e_oth.astype(bf16), preferred_element_type=f32
                    )
                lse[0, half : half + 1, cols] = top + jnp.log(total)
                pieces.append(mixed / total)
            out[cols] = jnp.concatenate(pieces, 0).T.astype(bf16)

    @pl.when(later[0] == 1)
    def _():
        body(True)

    @pl.when(later[0] == 0)
    def _():
        body(False)


def attention_backward(
    later, qseg, kseg_own, kseg_oth, q, k_own, v_own, k_oth, v_oth, grad, out, lse,
    dq, dk_own, dv_own, dk_oth, dv_oth, bias_own, bias_oth,
):
    pair = pl.program_id(0)
    count = q.shape[0]
    step = count // 2

    @pl.when(pair == 0)
    def _():
        mask_tables(kseg_own, kseg_oth, qseg, bias_own, bias_oth)

    def body(with_other):
        scale = jnp.asarray(HEAD_DIM**-0.5, bf16)
        queries = q[...] * scale
        keys_own = k_own[...].astype(f32).T.astype(bf16)
        keys_oth = k_oth[...].astype(f32).T.astype(bf16) if with_other else None
        products = (grad[...].astype(f32) * out[...].astype(f32)).T
        dk_a = [jnp.zeros((step, LANES), f32) for _ in range(2)]
        dv_a = [jnp.zeros((step, LANES), f32) for _ in range(2)]
        dk_b = jnp.zeros((count, LANES), f32)
        dv_b = jnp.zeros((count, LANES), f32)
        for part in range(2):
            cols = slice(part * step, (part + 1) * step)
            pieces = []
            for half in range(2):
                q_head = head_lanes(queries[cols], half)
                g_head = head_lanes(grad[cols], half)
                rows = slice(half * HEAD_DIM, (half + 1) * HEAD_DIM)
                delta = jnp.sum(products[rows, cols], 0, keepdims=True)
                log_total = lse[0, half : half + 1, cols]

                def block(keys, values, bias):
                    probs = jnp.exp(contract_last(keys, q_head) + bias - log_total)
                    d_probs = contract_last(values, g_head)
                    d_scores = (probs * (d_probs - delta)).astype(bf16)
                    dk = jnp.dot(d_scores, q_head, preferred_element_type=f32)
                    dv = jnp.dot(probs.astype(bf16), g_head, preferred_element_type=f32)
                    return (d_scores, dk, dv)

                d_query = jnp.zeros((HEAD_DIM, step), f32)
                for chunk in range(part + 1):
                    span = slice(chunk * step, (chunk + 1) * step)
                    d_scores, dk, dv = block(k_own[span], v_own[span], bias_own[span, cols])
                    dk_a[chunk] = dk_a[chunk] + dk
                    dv_a[chunk] = dv_a[chunk] + dv
                    d_query = d_query + jnp.dot(
                        keys_own[rows, span], d_scores, preferred_element_type=f32
                    )
                if with_other:
                    d_scores, dk, dv = block(k_oth[...], v_oth[...], bias_oth[:, cols])
                    dk_b = dk_b + dk
                    dv_b = dv_b + dv
                    d_query = d_query + jnp.dot(
                        keys_oth[rows], d_scores, preferred_element_type=f32
                    )
                pieces.append(d_query)
            dq[cols] = (jnp.concatenate(pieces, 0).T * HEAD_DIM**-0.5).astype(bf16)
        for chunk in range(2):
            span = slice(chunk * step, (chunk + 1) * step)
            dk_own[span] = dk_a[chunk].astype(bf16)
            dv_own[span] = dv_a[chunk].astype(bf16)
        dk_oth[...] = dk_b.astype(bf16)
        dv_oth[...] = dv_b.astype(bf16)

    @pl.when(later[0] == 1)
    def _():
        body(True)

    @pl.when(later[0] == 0)
    def _():
        body(False)


def attention_specs(count, pairs):
    def whole(shape):
        return pl.BlockSpec(shape, lambda p, later: (0,) * len(shape))

    def lanes(start):
        return pl.BlockSpec((count, LANES), lambda p, later: (0, start + p))

    segments = [whole((1, count)), whole((count, 1)), whole((count, 1))]
    projected = [lanes(0), lanes(pairs), lanes(2 * pairs), lanes(0), lanes(pairs)]
    totals = pl.BlockSpec((1, 2, count), lambda p, later: (p, 0, 0))
    return segments, projected, lanes(0), totals


def attend(later, labels, projected, others):
    count = projected.shape[0]
    pairs = projected.shape[1] // (3 * LANES)
    segments, blocks, wide, totals = attention_specs(count, pairs)
    work = count * count * LANES * pairs * 2
    return pl.pallas_call(
        attention_forward,
        grid_spec=pltpu.PrefetchScalarGridSpec(
            num_scalar_prefetch=1,
            grid=(pairs,),
            in_specs=segments + blocks,
            out_specs=[wide, totals],
            scratch_shapes=[pltpu.VMEM((count, count), f32), pltpu.VMEM((count, count), f32)],
        ),
        out_shape=[
            jax.ShapeDtypeStruct((count, pairs * LANES), bf16),
            jax.ShapeDtypeStruct((pairs, 2, count), f32),
        ],
        compiler_params=pltpu.CompilerParams(vmem_limit_bytes=48 << 20),
        cost_estimate=pl.CostEstimate(
            flops=4 * work, bytes_accessed=6 * count * pairs * LANES * 2, transcendentals=0
        ),
        name="attention_forward",
    )(later, *labels, projected, projected, projected, others, others)


def attend_back(later, labels, projected, others, grad, mixed, log_totals):
    count = projected.shape[0]
    pairs = projected.shape[1] // (3 * LANES)
    segments, blocks, wide, totals = attention_specs(count, pairs)
    work = count * count * LANES * pairs * 2
    return pl.pallas_call(
        attention_backward,
        grid_spec=pltpu.PrefetchScalarGridSpec(
            num_scalar_prefetch=1,
            grid=(pairs,),
            in_specs=segments + blocks + [wide, wide, totals],
            out_specs=[wide] * 5,
            scratch_shapes=[pltpu.VMEM((count, count), f32), pltpu.VMEM((count, count), f32)],
        ),
        out_shape=[jax.ShapeDtypeStruct((count, pairs * LANES), bf16)] * 5,
        compiler_params=pltpu.CompilerParams(vmem_limit_bytes=48 << 20),
        cost_estimate=pl.CostEstimate(
            flops=10 * work, bytes_accessed=12 * count * pairs * LANES * 2, transcendentals=0
        ),
        name="attention_backward",
    )(later, *labels, projected, projected, projected, others, others, grad, mixed, log_totals)


def place_kernel(spans, piece, sources, biased, continued, places, x, *refs):
    weights, refs = refs[:sources], refs[sources:]
    bias, refs = (refs[0], refs[1:]) if biased else (None, refs)
    before, refs = (refs[0], refs[1:]) if continued else (None, refs)
    out, whole, product = refs
    step = pl.program_id(0)
    each = pl.num_programs(0) // sources

    @pl.when(step == 0)
    def _():
        whole[...] = before[...].astype(f32) if continued else jnp.zeros_like(whole)

    for k, weight in enumerate(weights):

        @pl.when(step // each == k)
        def _(weight=weight):
            product[...] = jnp.dot(x[...], weight[0], preferred_element_type=f32)

    for place in range(x.shape[1] // piece):

        @pl.when(places[step] == place)
        def _(place=place):
            for source, target in spans:
                start = target + place * piece
                block = product[:, source : source + piece]
                if biased:
                    block = block + bias[:, start : start + piece]
                whole[:, start : start + piece] = block

    @pl.when(step == pl.num_programs(0) - 1)
    def _():
        out[...] = whole[...].astype(bf16)


def multiply_and_place(places, x, weights, lanes, lane_block, spans, piece, out_lanes, bias, before):
    count, depth = x.shape
    each = weights[0].shape[0]
    sources = len(weights)

    def fixed(shape):
        return pl.BlockSpec(shape, lambda j, places: (0, 0))

    in_specs = [fixed((count, depth))]
    for k in range(sources):
        in_specs.append(
            pl.BlockSpec(
                (1, depth, lanes),
                lambda j, places, k=k: (jnp.clip(j - k * each, 0, each - 1), 0, lane_block),
            )
        )
    operands = [x, *weights]
    if bias is not None:
        in_specs.append(fixed(bias.shape))
        operands.append(bias)
    if before is not None:
        in_specs.append(fixed(before.shape))
        operands.append(before)
    return pl.pallas_call(
        functools.partial(
            place_kernel, spans, piece, sources, bias is not None, before is not None
        ),
        grid_spec=pltpu.PrefetchScalarGridSpec(
            num_scalar_prefetch=1,
            grid=(each * sources,),
            in_specs=in_specs,
            out_specs=fixed((count, out_lanes)),
            scratch_shapes=[pltpu.VMEM((count, out_lanes), f32), pltpu.VMEM((count, lanes), f32)],
        ),
        out_shape=jax.ShapeDtypeStruct((count, out_lanes), bf16),
        compiler_params=pltpu.CompilerParams(vmem_limit_bytes=48 << 20),
        cost_estimate=pl.CostEstimate(
            flops=2 * count * depth * lanes * each * sources,
            bytes_accessed=2 * (each * sources * depth * lanes + count * (depth + out_lanes)),
            transcendentals=0,
        ),
        name="multiply_and_place",
    )(places, *operands)


def split_all(column, cols, write):
    for here in range(cols):

        @pl.when(column[0] == here)
        def _(here=here):
            for k in range(cols):
                write(k % 2, k // 2, here ^ k)


def split_mixed_kernel(piece, cols, lead, column, mixed, own, oth):
    count, lanes = own.shape[1:]
    values = mixed[...].astype(f32)
    before = jnp.zeros((count, lead), f32)
    after = jnp.zeros((count, lanes - lead - piece), f32)

    def write(which, i, c):
        block = values[:, c * piece : (c + 1) * piece]
        (own, oth)[which][i] = jnp.concatenate([before, block, after], 1).astype(bf16)

    split_all(column, cols, write)


def split_grads_kernel(piece, cols, column, dq, dk, dv, back, own, oth, sums):
    count, lanes = own.shape[1:]
    wide = dq.shape[1]
    grads = [
        dq[...].astype(f32),
        dk[...].astype(f32) + back[:, :wide].astype(f32),
        dv[...].astype(f32) + back[:, wide:].astype(f32),
    ]
    sums[0:1] = jnp.sum(grads[0], 0, keepdims=True)
    sums[1:2] = jnp.sum(grads[2], 0, keepdims=True)
    after = jnp.zeros((count, lanes - 3 * piece), f32)

    def write(which, i, c):
        blocks = [g[:, c * piece : (c + 1) * piece] for g in grads]
        (own, oth)[which][i] = jnp.concatenate([*blocks, after], 1).astype(bf16)

    split_all(column, cols, write)


def whole_specs(shapes):
    return [pl.BlockSpec(s, lambda i, p, n=len(s): (0,) * n) for s in shapes]


def split_call(kernel, column, operands, out_shapes, name):
    moved = sum(x.size * x.dtype.itemsize for x in operands) * 2
    return pl.pallas_call(
        kernel,
        grid_spec=pltpu.PrefetchScalarGridSpec(
            num_scalar_prefetch=1,
            grid=(1,),
            in_specs=whole_specs([x.shape for x in operands]),
            out_specs=whole_specs([s.shape for s in out_shapes]),
        ),
        out_shape=out_shapes,
        compiler_params=pltpu.CompilerParams(vmem_limit_bytes=48 << 20),
        cost_estimate=pl.CostEstimate(flops=moved, bytes_accessed=moved, transcendentals=0),
        name=name,
    )(column, *operands)


def block_grads_kernel(joined, left_one, left_two, grads, mixed, *refs):
    vec_part, received, out, total = refs if joined else (None, None, *refs)
    lanes_one = grads.shape[2]
    lane_lead = total.shape[1] - mixed.shape[2]
    total[:, :lanes_one] = jnp.dot(left_one[...], grads[0], preferred_element_type=f32)
    total[:, lanes_one:] = jnp.zeros_like(total[:, lanes_one:])
    total[:, lane_lead:] += jnp.dot(left_two[...], mixed[0], preferred_element_type=f32)
    if joined:
        total[:, -LANES:] += vec_part[0].astype(f32)
        out[0] = (total[...] + received[0].astype(f32)).astype(bf16)
    else:
        out[0] = total[...].astype(bf16)


def block_grads(left_one, left_two, grads, mixed, more):
    each, count, _ = grads.shape
    width = left_one.shape[0]
    lanes = -(-width // LANES) * LANES

    def fixed(shape):
        return pl.BlockSpec(shape, lambda i: (0, 0))

    def step(shape):
        return pl.BlockSpec((1, *shape[1:]), lambda i: (i, 0, 0))

    operands = [left_one, left_two, grads, mixed, *(more or ())]
    in_specs = [fixed(left_one.shape), fixed(left_two.shape)]
    in_specs += [step(x.shape) for x in operands[2:]]
    return pl.pallas_call(
        functools.partial(block_grads_kernel, more is not None),
        grid=(each,),
        in_specs=in_specs,
        out_specs=step((each, width, lanes)),
        out_shape=jax.ShapeDtypeStruct((each, width, lanes), bf16),
        scratch_shapes=[pltpu.VMEM((width, lanes), f32)],
        compiler_params=pltpu.CompilerParams(vmem_limit_bytes=48 << 20),
        cost_estimate=pl.CostEstimate(
            flops=2 * each * count * width * (grads.shape[2] + mixed.shape[2]),
            bytes_accessed=2 * each * width * lanes * 2,
            transcendentals=0,
        ),
        name="block_grads",
    )(*operands)


AXES = ("col", "dp", "row")


def planes():
    owners = lax.axis_size("dp") * lax.axis_size("row")
    cols = lax.axis_size("col")
    return [
        [c * owners + k for c in range(p, cols, 2) for k in range(owners)] for p in range(2)
    ]


def flip_col(block, bit):
    return lax.ppermute(block, "col", [(c, c ^ bit) for c in range(lax.axis_size("col"))])


def partner(block):
    return flip_col(block, 1)


def flip_dp(block):
    return lax.ppermute(block, "dp", [(0, 1), (1, 0)])


def shift_row(block, by):
    count = lax.axis_size("row")
    return lax.ppermute(block, "row", [(i, (i + by) % count) for i in range(count)])


def by_place(blocks):
    column = lax.axis_index("col")
    pairs = blocks.reshape(-1, 2, *blocks.shape[1:])
    pairs = jnp.where(column % 2 == 1, pairs[:, ::-1], pairs)
    return upper_bit(pairs).reshape(blocks.shape)


def upper_bit(blocks):
    return jnp.where(lax.axis_index("col") // 2 == 1, blocks[::-1], blocks)


def short_rows():
    return lax.axis_size("row") == 4 and lax.axis_size("dp") == 2 and lax.axis_size("col") == 4


def assemble_kernel(place, first, first_x, second, second_y, first_y, second_x, out, sems):
    dp, row = place[0], place[1]
    copies = []
    for m in range(2):
        for source, dx, dy, at in (
            (first.at[m], 0, 0, m),
            (first_x.at[m], 1, 0, m),
            (second.at[m], 0, 0, m + 2),
            (second_y.at[m], 0, 1, m + 2),
            (first_y.at[0, m], 0, 1, m),
            (first_y.at[1, m], 1, 1, m),
            (second_x.at[0, m], 1, 0, m + 2),
            (second_x.at[1, m], 1, 1, m + 2),
        ):
            target = out.at[dx, 1 - dp if dy else dp, lax.rem(row + 4 - at, 4)]
            copies.append(pltpu.make_async_copy(source, target, sems.at[len(copies)]))
    for copy in copies:
        copy.start()
    for copy in copies:
        copy.wait()


def assemble(pieces):
    block = pieces[0].shape[1:]
    place = jnp.stack([lax.axis_index("dp"), lax.axis_index("row")]).astype(jnp.int32)
    out = pl.pallas_call(
        assemble_kernel,
        grid_spec=pltpu.PrefetchScalarGridSpec(
            num_scalar_prefetch=1,
            grid=(1,),
            in_specs=[pl.BlockSpec(memory_space=pl.ANY)] * 6,
            out_specs=pl.BlockSpec(memory_space=pl.ANY),
            scratch_shapes=[pltpu.SemaphoreType.DMA((16,))],
        ),
        out_shape=jax.ShapeDtypeStruct((2, 2, 4, *block), bf16),
        cost_estimate=pl.CostEstimate(
            flops=0, bytes_accessed=64 * block[0] * block[1], transcendentals=0
        ),
        name="assemble",
    )(place, *pieces)
    return out.reshape(2, -1, block[1])


def spread_rows(block):
    return [block] + [shift_row(block, m) for m in range(1, 4)]


def spread_one(pieces):
    first, second = jnp.stack(pieces[:2]), jnp.stack(pieces[2:])
    return [first, flip_col(first, 2), second, flip_dp(second)]


def spread_two(pieces):
    first_y = flip_dp(jnp.stack(pieces[:2]))
    return [*pieces, first_y, flip_col(jnp.stack(pieces[2:]), 2)]


def gather_groups(block):
    whole = lax.all_gather(block, AXES, axis=0, tiled=False, axis_index_groups=planes())
    return upper_bit(whole.reshape(lax.axis_size("col") // 2, -1, block.shape[-1]))


def together(*arrays):
    return lax.optimization_barrier(arrays)


def added(one, other):
    return (one.astype(f32) + other.astype(f32)).astype(bf16)


def at_place(array, which, axis):
    return lax.dynamic_index_in_dim(array, which, axis, keepdims=False)


def scatter_one(blocks):
    if not short_rows():
        return blocks
    dp = lax.axis_index("dp")
    parts = blocks.reshape(2, 2, 4, -1, blocks.shape[-1])
    first, second = parts[:, :, :2], parts[:, :, 2:]
    first_y = flip_dp(at_place(first, 1 - dp, 1))
    second_x = flip_col(second[1], 2)
    return added(at_place(first, dp, 1), first_y), added(second[0], second_x)


def scatter_two(halves):
    if not short_rows():
        return halves
    dp = lax.axis_index("dp")
    first, second = halves
    first_x = flip_col(first[1], 2)
    second_y = flip_dp(at_place(second, 1 - dp, 0))
    return jnp.concatenate(
        [added(first[0], first_x), added(at_place(second, dp, 0), second_y)], 0
    )


def scatter_three(rows):
    if not short_rows():
        flat = upper_bit(rows).reshape(-1, rows.shape[-1])
        return lax.psum_scatter(
            flat, AXES, scatter_dimension=0, tiled=True, axis_index_groups=planes()
        ).astype(f32)
    row = lax.axis_index("row")
    total = at_place(rows, row, 0).astype(f32)
    for m in range(1, 4):
        total = total + shift_row(at_place(rows, (row + m) % 4, 0), m).astype(f32)
    return total


def local(
    hidden_in,
    cotangent,
    segments,
    qkv_weight,
    out_weight,
    up_weight,
    down_weight,
    vectors,
    qkv_first,
    out_first,
    up_first,
    down_first,
    vectors_first,
    qkv_second,
    out_second,
    up_second,
    down_second,
    vectors_second,
):
    column = lax.axis_index("col")
    cols = lax.axis_size("col")
    here, width = hidden_in.shape
    rows_own = qkv_weight.shape[0]
    owners = lax.axis_size("dp") * lax.axis_size("row")
    piece = qkv_weight.shape[2]
    halves = SEQ // here
    each = cols // 2
    column_word = column.reshape(1).astype(jnp.int32)
    places_own = (column ^ (2 * jnp.arange(each))).astype(jnp.int32)
    places_oth = (column ^ (2 * jnp.arange(each) + 1)).astype(jnp.int32)
    later = lax.rem(column, halves).reshape(1).astype(jnp.int32)
    padded = -(-width // LANES) * LANES
    spare = padded - width
    lanes_qkv = -(-3 * piece // LANES) * LANES
    lead_out = 3 * piece // LANES * LANES
    lanes_out = padded - lead_out

    vec_shape = vectors.shape
    vec_count = vec_shape[0] * vec_shape[1]
    vec_lines = -(-vec_count // spare)
    vec_fill = vec_lines * spare - vec_count
    vec_lanes = jnp.pad(vectors.reshape(vec_count).astype(bf16), (0, vec_fill))
    attn_block = jnp.concatenate(
        [
            qkv_weight.reshape(rows_own, 3 * piece).astype(bf16),
            out_weight.T.astype(bf16),
            jnp.pad(vec_lanes.reshape(vec_lines, spare), ((0, rows_own - vec_lines), (0, 0))),
        ],
        1,
    )
    up_block, down_block = up_weight.astype(bf16), down_weight.T.astype(bf16)
    staged = short_rows()
    if staged:
        attn_one = spread_one(spread_rows(attn_block))
        up_block, attn_one = together(up_block, attn_one)
        up_rows = spread_rows(up_block)
        down_block, up_rows = together(down_block, up_rows)
        down_rows = spread_rows(down_block)
        attn_own = assemble(spread_two(attn_one))
        up_one, down_one = spread_one(up_rows), spread_one(down_rows)
    else:
        attn_own, up_own, down_own = [
            gather_groups(b) for b in (attn_block, up_block, down_block)
        ]
    vec_own = attn_own.reshape(each, owners, rows_own, padded)[:, :, :vec_lines, width:]
    vec_oth = partner(vec_own)
    attn_oth = partner(attn_own)

    def vec_rows(lines):
        lines = lines.reshape(each, owners, vec_lines * spare)[:, :, :vec_count]
        lines = lines.reshape(each, owners, *vec_shape).transpose(0, 2, 1, 3)
        return lines.reshape(each, vec_shape[0], width).astype(f32)

    vec = jnp.stack([vec_rows(vec_own), vec_rows(vec_oth)], 1).reshape(cols, -1, width)
    vec = by_place(vec).reshape(-1, width)

    def widen(row):
        return jnp.pad(row, (0, spare))

    inputs = hidden_in.astype(f32)
    normed_one, scaled_one, inverse_one = normalize(inputs, vec[0], vec[1])
    normed_low = normed_one.astype(bf16)
    if staged:
        normed_low, up_one = together(normed_low, up_one)
        up_two = spread_two(up_one)
    bias = jnp.concatenate([widen(vec[2]), jnp.zeros((padded,), f32), widen(vec[3])]).reshape(1, -1)
    spans = tuple((part * piece, part * padded) for part in range(3))
    projected = None
    for places, weights in ((places_own, attn_own), (places_oth, attn_oth)):
        projected = multiply_and_place(
            places, normed_low, [weights], lanes_qkv, 0, spans, piece, 3 * padded, bias, projected
        )
    if staged:
        projected, down_one = together(projected, down_one)
        down_two = spread_two(down_one)
    ahead = [(c, c + 1) for c in range(cols - 1) if c % halves + 1 < halves]
    behind = [(b, a) for a, b in ahead]
    others = lax.ppermute(projected[:, padded:], "col", ahead)

    own_half = lax.dynamic_slice_in_dim(segments.reshape(-1), column * here, here, 0)
    first_half = lax.dynamic_slice_in_dim(
        segments.reshape(-1), (column - lax.rem(column, halves)) * here, here, 0
    )
    labels = (own_half.reshape(1, here), own_half.reshape(here, 1), first_half.reshape(here, 1))
    mixed, log_totals = attend(later, labels, projected, others)
    if staged:
        mixed, up_two = together(mixed, up_two)
        up_own = assemble(up_two)
    up_oth = partner(up_own)
    mixed_shape = jax.ShapeDtypeStruct((each, here, lanes_out), bf16)
    lead = 3 * piece - lead_out
    mixed_own, mixed_oth = split_call(
        functools.partial(split_mixed_kernel, piece, cols, lead),
        column_word,
        [mixed],
        [mixed_shape] * 2,
        "split_mixed",
    )
    residual = inputs + vec[4]
    for blocks, weights in ((mixed_own, attn_own), (mixed_oth, attn_oth)):
        for i in range(each):
            residual = residual + contract_last(blocks[i], weights[i][:, lead_out:])
    normed_two, scaled_two, inverse_two = normalize(residual, vec[5], vec[6])
    normed_two_low = normed_two.astype(bf16)

    bias_up = by_place(vec[8:])
    bias_own, bias_oth = bias_up[0::2], bias_up[1::2]

    def up_part(ups, biases):
        return [
            jnp.dot(normed_two_low, ups[i], preferred_element_type=f32) + biases[i]
            for i in range(each)
        ]

    linear_own = up_part(up_own, bias_own)
    if staged:
        linear_own, down_two = together(linear_own, down_two)
        down_own = assemble(down_two)
    down_oth = partner(down_own)
    linear_oth = up_part(up_oth, bias_oth)

    branch = jnp.zeros((here, width), f32)

    def forward_part(linears, downs, branch):
        lows, pullbacks = [], []
        for i in range(each):
            active, pullback = jax.vjp(gelu_tanh, linears[i])
            lows.append(active.astype(bf16))
            pullbacks.append(pullback)
            branch = branch + contract_last(lows[i], downs[i])
        return lows, pullbacks, branch

    lows_own, pull_own, branch = forward_part(linear_own, down_own, branch)
    lows_oth, pull_oth, branch = forward_part(linear_oth, down_oth, branch)
    layer_out = (residual + branch + vec[7]).astype(bf16)

    def partner_grads(left, rights):
        return jnp.stack([contract_first(left, r).astype(bf16) for r in rights])

    def plane_grads(left, rights, received):
        return jnp.stack(
            [
                (contract_first(left, r) + received[i].astype(f32)).astype(bf16)
                for i, r in enumerate(rights)
            ]
        )

    sent_down = partner_grads(cotangent, lows_oth)
    down_oth, sent_down = together(down_oth, sent_down)
    received_down = partner(sent_down)

    grad_normed_two = jnp.zeros((here, width), f32)

    def backward_part(ups, downs, pullbacks, grad_normed_two):
        lows, sums = [], []
        for i in range(each):
            grad_active = jnp.dot(cotangent, downs[i], preferred_element_type=f32)
            grad_linear = pullbacks[i](grad_active)[0]
            lows.append(grad_linear.astype(bf16))
            sums.append(jnp.sum(grad_linear, 0))
            grad_normed_two = grad_normed_two + contract_last(lows[i], ups[i])
        return lows, sums, grad_normed_two

    dups_oth, dbias_oth, grad_normed_two = backward_part(
        up_oth, down_oth, pull_oth, grad_normed_two
    )
    lows_own, dups_oth = together(lows_own, dups_oth)
    total_down = plane_grads(cotangent, lows_own, received_down)
    sent_up = partner_grads(normed_two_low, dups_oth)
    down_own, total_down, sent_up = together(down_own, total_down, sent_up)
    received_up = partner(sent_up)
    one_down = scatter_one(total_down)
    dups_own, dbias_own, grad_normed_two = backward_part(
        up_own, down_own, pull_own, grad_normed_two
    )

    grad_residual = cotangent.astype(f32) + norm_back(
        grad_normed_two, scaled_two, inverse_two, vec[5]
    )
    grad_residual_low = grad_residual.astype(bf16)
    grad_mixed = multiply_and_place(
        jnp.concatenate([places_own, places_oth]),
        grad_residual_low,
        [attn_own, attn_oth],
        lanes_out,
        lead_out // lanes_out,
        ((lead, 0),),
        piece,
        padded,
        None,
        None,
    )
    total_up = plane_grads(normed_two_low, dups_own, received_up)
    grad_mixed, total_up, one_down = together(grad_mixed, total_up, one_down)
    dq, dk_own, dv_own, dk_oth, dv_oth = attend_back(
        later, labels, projected, others, grad_mixed, mixed, log_totals
    )
    back = lax.ppermute(jnp.concatenate([dk_oth, dv_oth], 1), "col", behind)
    two_down = scatter_two(one_down)
    one_up = scatter_one(total_up)
    dq, dk_own, dv_own, two_down, one_up = together(dq, dk_own, dv_own, two_down, one_up)
    grads_shape = jax.ShapeDtypeStruct((each, here, lanes_qkv), bf16)
    grads_own, grads_oth, grad_sums = split_call(
        functools.partial(split_grads_kernel, piece, cols),
        column_word,
        [dq, dk_own, dv_own, back],
        [grads_shape, grads_shape, jax.ShapeDtypeStruct((8, padded), f32)],
        "split_grads",
    )
    two_up = scatter_two(one_up)
    left_one, left_two = normed_low.T, grad_residual_low.T
    received = partner(block_grads(left_one, left_two, grads_oth, mixed_oth, None))
    grad_normed_one = jnp.zeros((here, width), f32)
    for blocks, weights in ((grads_own, attn_own), (grads_oth, attn_oth)):
        for i in range(each):
            grad_normed_one = grad_normed_one + contract_last(blocks[i], weights[i][:, :lanes_qkv])
    input_grad = grad_residual + norm_back(grad_normed_one, scaled_one, inverse_one, vec[0])

    dbias = jnp.stack([jnp.stack(dbias_own), jnp.stack(dbias_oth)], 1).reshape(cols, width)
    grad_vector = jnp.concatenate(
        [
            jnp.stack(
                [
                    jnp.sum(grad_normed_one * scaled_one, 0),
                    jnp.sum(grad_normed_one, 0),
                    grad_sums[0, :width],
                    grad_sums[1, :width],
                    jnp.sum(grad_residual, 0),
                    jnp.sum(grad_normed_two * scaled_two, 0),
                    jnp.sum(grad_normed_two, 0),
                    jnp.sum(cotangent.astype(f32), 0),
                ]
            ),
            by_place(dbias),
        ],
        0,
    ).astype(bf16)
    vec_part = grad_vector.reshape(cols, vec_shape[0], owners, vec_shape[1]).transpose(0, 2, 1, 3)
    vec_part = jnp.pad(vec_part.reshape(cols, owners, vec_count), ((0, 0), (0, 0), (0, vec_fill)))
    vec_part = by_place(vec_part.reshape(cols, owners, vec_lines, spare))
    vec_here = (vec_part[0::2].astype(f32) + partner(vec_part[1::2]).astype(f32)).astype(bf16)
    vec_here = jnp.pad(
        vec_here, ((0, 0), (0, 0), (0, rows_own - vec_lines), (LANES - spare, 0))
    ).reshape(each, width, LANES)
    total_attn = block_grads(
        left_one, left_two, grads_own, mixed_own, (vec_here, received)
    )
    sum_down, sum_up = scatter_three(two_down), scatter_three(two_up)
    sum_attn = scatter_three(scatter_two(scatter_one(total_attn)))
    sum_qkv = sum_attn[:, : 3 * piece].reshape(rows_own, 3, piece)
    sum_out = sum_attn[:, 3 * piece : width].T
    sum_vector = sum_attn[:vec_lines, width:].reshape(-1)[:vec_count].reshape(vec_shape)

    qkv_m, qkv_v, qkv_w = adamw(
        qkv_weight, sum_qkv, qkv_first, qkv_second, 1.5 * D ** (-0.5), decay_rate
    )
    out_m, out_v, out_w = adamw(
        out_weight, sum_out, out_first, out_second, 1.5 * (D // 64) ** (-0.5), decay_rate
    )
    up_m, up_v, up_w = adamw(up_weight, sum_up, up_first, up_second, 1.5 * D ** (-0.5), decay_rate)
    down_m, down_v, down_w = adamw(
        down_weight, sum_down.T, down_first, down_second, 1.5 * FF ** (-0.5), decay_rate
    )
    vec_m, vec_v, vec_w = adamw(vectors, sum_vector, vectors_first, vectors_second, 0.5, 0.0)
    return (
        layer_out,
        input_grad,
        qkv_m,
        qkv_v,
        qkv_w,
        out_m,
        out_v,
        out_w,
        up_m,
        up_v,
        up_w,
        down_m,
        down_v,
        down_w,
        vec_m,
        vec_v,
        vec_w,
    )


def solution(mesh):
    tokens = P(("dp", "row", "col"), None)
    qkv = P(("dp", "row"), None, "col")
    tall = P("col", ("dp", "row"))
    up = P(("dp", "row"), "col")
    state = (qkv, tall, up, tall, tall)
    return jax.shard_map(
        local,
        mesh=mesh,
        in_specs=(tokens, tokens, P(("dp", "row"), None)) + state * 3,
        out_specs=(tokens, tokens)
        + (qkv,) * 3
        + (tall,) * 3
        + (up,) * 3
        + (tall,) * 3
        + (tall,) * 3,
        check_vma=False,
    )
```

```python
import functools

import jax
import jax.numpy as jnp
from jax import lax
from jax.experimental import pallas as pl
from jax.experimental.pallas import tpu as pltpu
from jax.sharding import PartitionSpec as P

D = 1088
HEAD_DIM = 64
FF = 4352
SEQ = 1024
STEP = 5

LANES = 128


beta_one = 0.9
beta_two = 0.999
epsilon = 1e-08
decay_rate = 0.1
masked_score = -1000000000.0

f32 = jnp.float32
bf16 = jnp.bfloat16


def contract(left, right, left_dim, right_dim):
    return lax.dot_general(
        left, right, (((left_dim,), (right_dim,)), ((), ())), preferred_element_type=f32
    )


def contract_first(left, right):
    return contract(left, right, 0, 0)


def contract_last(left, right):
    return contract(left, right, 1, 1)


def normalize(rows, gain, shift):
    row_mean = jnp.mean(rows, -1, keepdims=True)
    centred = rows - row_mean
    inverse = lax.rsqrt(jnp.mean(centred * centred, -1, keepdims=True) + 1e-05)
    scaled = centred * inverse
    return (scaled * gain + shift, scaled, inverse)


def norm_back(grad_out, scaled, inverse, gain):
    grad_scaled = grad_out * gain
    return inverse * (
        grad_scaled
        - jnp.mean(grad_scaled, -1, keepdims=True)
        - scaled * jnp.mean(grad_scaled * scaled, -1, keepdims=True)
    )


def gelu_tanh(values):
    return jax.nn.gelu(values, approximate=True)


def adamw(weight, gradient, moment_one, moment_two, step_rate, shrink):
    moment_one = beta_one * moment_one + (1.0 - beta_one) * gradient
    moment_two = beta_two * moment_two + (1.0 - beta_two) * gradient * gradient
    update = (
        moment_one
        / (1.0 - beta_one**STEP)
        / (jnp.sqrt(moment_two / (1.0 - beta_two**STEP)) + epsilon)
    )
    return (moment_one, moment_two, weight - step_rate * (update + shrink * weight))


def mask_tables(kseg_own, kseg_oth, qseg, bias_own, bias_oth):
    count = bias_own.shape[0]
    key_place = lax.broadcasted_iota(jnp.int32, (count, count), 0)
    query_place = lax.broadcasted_iota(jnp.int32, (count, count), 1)
    same = kseg_own[...] == qseg[...]
    bias_own[...] = jnp.where(same & (key_place <= query_place), 0.0, masked_score)
    bias_oth[...] = jnp.where(kseg_oth[...] == qseg[...], 0.0, masked_score)


def head_lanes(block, half):
    lane = lax.broadcasted_iota(jnp.int32, block.shape, 1)
    return jnp.where((lane // HEAD_DIM) == half, block, jnp.zeros_like(block))


def attention_forward(
    later, qseg, kseg_own, kseg_oth, q, k_own, v_own, k_oth, v_oth, out, lse, bias_own, bias_oth
):
    pair = pl.program_id(0)
    count = q.shape[0]
    step = count // 2

    @pl.when(pair == 0)
    def _():
        mask_tables(kseg_own, kseg_oth, qseg, bias_own, bias_oth)

    def body(with_other):
        queries = q[...] * jnp.asarray(HEAD_DIM**-0.5, bf16)
        values_own = v_own[...].astype(f32).T.astype(bf16)
        values_oth = v_oth[...].astype(f32).T.astype(bf16) if with_other else None
        for part in range(2):
            cols = slice(part * step, (part + 1) * step)
            seen = (part + 1) * step
            pieces = []
            for half in range(2):
                q_head = head_lanes(queries[cols], half)
                rows = slice(half * HEAD_DIM, (half + 1) * HEAD_DIM)
                s_own = contract_last(k_own[:seen], q_head) + bias_own[:seen, cols]
                top = jnp.max(s_own, 0, keepdims=True)
                if with_other:
                    s_oth = contract_last(k_oth[...], q_head) + bias_oth[:, cols]
                    top = jnp.maximum(top, jnp.max(s_oth, 0, keepdims=True))
                e_own = jnp.exp(s_own - top)
                total = jnp.sum(e_own, 0, keepdims=True)
                mixed = jnp.dot(
                    values_own[rows, :seen], e_own.astype(bf16), preferred_element_type=f32
                )
                if with_other:
                    e_oth = jnp.exp(s_oth - top)
                    total = total + jnp.sum(e_oth, 0, keepdims=True)
                    mixed = mixed + jnp.dot(
                        values_oth[rows], e_oth.astype(bf16), preferred_element_type=f32
                    )
                lse[0, half : half + 1, cols] = top + jnp.log(total)
                pieces.append(mixed / total)
            out[cols] = jnp.concatenate(pieces, 0).T.astype(bf16)

    @pl.when(later[0] == 1)
    def _():
        body(True)

    @pl.when(later[0] == 0)
    def _():
        body(False)


def attention_backward(
    later, qseg, kseg_own, kseg_oth, q, k_own, v_own, k_oth, v_oth, grad, out, lse,
    dq, dk_own, dv_own, dk_oth, dv_oth, bias_own, bias_oth,
):
    pair = pl.program_id(0)
    count = q.shape[0]
    step = count // 2

    @pl.when(pair == 0)
    def _():
        mask_tables(kseg_own, kseg_oth, qseg, bias_own, bias_oth)

    def body(with_other):
        scale = jnp.asarray(HEAD_DIM**-0.5, bf16)
        queries = q[...] * scale
        keys_own = k_own[...].astype(f32).T.astype(bf16)
        keys_oth = k_oth[...].astype(f32).T.astype(bf16) if with_other else None
        products = (grad[...].astype(f32) * out[...].astype(f32)).T
        dk_a = [jnp.zeros((step, LANES), f32) for _ in range(2)]
        dv_a = [jnp.zeros((step, LANES), f32) for _ in range(2)]
        dk_b = jnp.zeros((count, LANES), f32)
        dv_b = jnp.zeros((count, LANES), f32)
        for part in range(2):
            cols = slice(part * step, (part + 1) * step)
            pieces = []
            for half in range(2):
                q_head = head_lanes(queries[cols], half)
                g_head = head_lanes(grad[cols], half)
                rows = slice(half * HEAD_DIM, (half + 1) * HEAD_DIM)
                delta = jnp.sum(products[rows, cols], 0, keepdims=True)
                log_total = lse[0, half : half + 1, cols]

                def block(keys, values, bias):
                    probs = jnp.exp(contract_last(keys, q_head) + bias - log_total)
                    d_probs = contract_last(values, g_head)
                    d_scores = (probs * (d_probs - delta)).astype(bf16)
                    dk = jnp.dot(d_scores, q_head, preferred_element_type=f32)
                    dv = jnp.dot(probs.astype(bf16), g_head, preferred_element_type=f32)
                    return (d_scores, dk, dv)

                d_query = jnp.zeros((HEAD_DIM, step), f32)
                for chunk in range(part + 1):
                    span = slice(chunk * step, (chunk + 1) * step)
                    d_scores, dk, dv = block(k_own[span], v_own[span], bias_own[span, cols])
                    dk_a[chunk] = dk_a[chunk] + dk
                    dv_a[chunk] = dv_a[chunk] + dv
                    d_query = d_query + jnp.dot(
                        keys_own[rows, span], d_scores, preferred_element_type=f32
                    )
                if with_other:
                    d_scores, dk, dv = block(k_oth[...], v_oth[...], bias_oth[:, cols])
                    dk_b = dk_b + dk
                    dv_b = dv_b + dv
                    d_query = d_query + jnp.dot(
                        keys_oth[rows], d_scores, preferred_element_type=f32
                    )
                pieces.append(d_query)
            dq[cols] = (jnp.concatenate(pieces, 0).T * HEAD_DIM**-0.5).astype(bf16)
        for chunk in range(2):
            span = slice(chunk * step, (chunk + 1) * step)
            dk_own[span] = dk_a[chunk].astype(bf16)
            dv_own[span] = dv_a[chunk].astype(bf16)
        dk_oth[...] = dk_b.astype(bf16)
        dv_oth[...] = dv_b.astype(bf16)

    @pl.when(later[0] == 1)
    def _():
        body(True)

    @pl.when(later[0] == 0)
    def _():
        body(False)


def attention_specs(count, pairs):
    def whole(shape):
        return pl.BlockSpec(shape, lambda p, later: (0,) * len(shape))

    def lanes(start):
        return pl.BlockSpec((count, LANES), lambda p, later: (0, start + p))

    segments = [whole((1, count)), whole((count, 1)), whole((count, 1))]
    projected = [lanes(0), lanes(pairs), lanes(2 * pairs), lanes(0), lanes(pairs)]
    totals = pl.BlockSpec((1, 2, count), lambda p, later: (p, 0, 0))
    return segments, projected, lanes(0), totals


def attend(later, labels, projected, others):
    count = projected.shape[0]
    pairs = projected.shape[1] // (3 * LANES)
    segments, blocks, wide, totals = attention_specs(count, pairs)
    work = count * count * LANES * pairs * 2
    return pl.pallas_call(
        attention_forward,
        grid_spec=pltpu.PrefetchScalarGridSpec(
            num_scalar_prefetch=1,
            grid=(pairs,),
            in_specs=segments + blocks,
            out_specs=[wide, totals],
            scratch_shapes=[pltpu.VMEM((count, count), f32), pltpu.VMEM((count, count), f32)],
        ),
        out_shape=[
            jax.ShapeDtypeStruct((count, pairs * LANES), bf16),
            jax.ShapeDtypeStruct((pairs, 2, count), f32),
        ],
        compiler_params=pltpu.CompilerParams(vmem_limit_bytes=48 << 20),
        cost_estimate=pl.CostEstimate(
            flops=4 * work, bytes_accessed=6 * count * pairs * LANES * 2, transcendentals=0
        ),
        name="attention_forward",
    )(later, *labels, projected, projected, projected, others, others)


def attend_back(later, labels, projected, others, grad, mixed, log_totals):
    count = projected.shape[0]
    pairs = projected.shape[1] // (3 * LANES)
    segments, blocks, wide, totals = attention_specs(count, pairs)
    work = count * count * LANES * pairs * 2
    return pl.pallas_call(
        attention_backward,
        grid_spec=pltpu.PrefetchScalarGridSpec(
            num_scalar_prefetch=1,
            grid=(pairs,),
            in_specs=segments + blocks + [wide, wide, totals],
            out_specs=[wide] * 5,
            scratch_shapes=[pltpu.VMEM((count, count), f32), pltpu.VMEM((count, count), f32)],
        ),
        out_shape=[jax.ShapeDtypeStruct((count, pairs * LANES), bf16)] * 5,
        compiler_params=pltpu.CompilerParams(vmem_limit_bytes=48 << 20),
        cost_estimate=pl.CostEstimate(
            flops=10 * work, bytes_accessed=12 * count * pairs * LANES * 2, transcendentals=0
        ),
        name="attention_backward",
    )(later, *labels, projected, projected, projected, others, others, grad, mixed, log_totals)


def place_kernel(spans, piece, sources, biased, continued, places, x, *refs):
    weights, refs = refs[:sources], refs[sources:]
    bias, refs = (refs[0], refs[1:]) if biased else (None, refs)
    before, refs = (refs[0], refs[1:]) if continued else (None, refs)
    out, whole, product = refs
    step = pl.program_id(0)
    each = pl.num_programs(0) // sources

    @pl.when(step == 0)
    def _():
        whole[...] = before[...].astype(f32) if continued else jnp.zeros_like(whole)

    for k, weight in enumerate(weights):

        @pl.when(step // each == k)
        def _(weight=weight):
            product[...] = jnp.dot(x[...], weight[0], preferred_element_type=f32)

    for place in range(x.shape[1] // piece):

        @pl.when(places[step] == place)
        def _(place=place):
            for source, target in spans:
                start = target + place * piece
                block = product[:, source : source + piece]
                if biased:
                    block = block + bias[:, start : start + piece]
                whole[:, start : start + piece] = block

    @pl.when(step == pl.num_programs(0) - 1)
    def _():
        out[...] = whole[...].astype(bf16)


def multiply_and_place(places, x, weights, lanes, lane_block, spans, piece, out_lanes, bias, before):
    count, depth = x.shape
    each = weights[0].shape[0]
    sources = len(weights)

    def fixed(shape):
        return pl.BlockSpec(shape, lambda j, places: (0, 0))

    in_specs = [fixed((count, depth))]
    for k in range(sources):
        in_specs.append(
            pl.BlockSpec(
                (1, depth, lanes),
                lambda j, places, k=k: (jnp.clip(j - k * each, 0, each - 1), 0, lane_block),
            )
        )
    operands = [x, *weights]
    if bias is not None:
        in_specs.append(fixed(bias.shape))
        operands.append(bias)
    if before is not None:
        in_specs.append(fixed(before.shape))
        operands.append(before)
    return pl.pallas_call(
        functools.partial(
            place_kernel, spans, piece, sources, bias is not None, before is not None
        ),
        grid_spec=pltpu.PrefetchScalarGridSpec(
            num_scalar_prefetch=1,
            grid=(each * sources,),
            in_specs=in_specs,
            out_specs=fixed((count, out_lanes)),
            scratch_shapes=[pltpu.VMEM((count, out_lanes), f32), pltpu.VMEM((count, lanes), f32)],
        ),
        out_shape=jax.ShapeDtypeStruct((count, out_lanes), bf16),
        compiler_params=pltpu.CompilerParams(vmem_limit_bytes=48 << 20),
        cost_estimate=pl.CostEstimate(
            flops=2 * count * depth * lanes * each * sources,
            bytes_accessed=2 * (each * sources * depth * lanes + count * (depth + out_lanes)),
            transcendentals=0,
        ),
        name="multiply_and_place",
    )(places, *operands)


def split_all(column, cols, write):
    for here in range(cols):

        @pl.when(column[0] == here)
        def _(here=here):
            for k in range(cols):
                write(k % 2, k // 2, here ^ k)


def split_mixed_kernel(piece, cols, lead, column, mixed, own, oth):
    count, lanes = own.shape[1:]
    values = mixed[...].astype(f32)
    before = jnp.zeros((count, lead), f32)
    after = jnp.zeros((count, lanes - lead - piece), f32)

    def write(which, i, c):
        block = values[:, c * piece : (c + 1) * piece]
        (own, oth)[which][i] = jnp.concatenate([before, block, after], 1).astype(bf16)

    split_all(column, cols, write)


def split_grads_kernel(piece, cols, column, dq, dk, dv, back, own, oth, sums):
    count, lanes = own.shape[1:]
    wide = dq.shape[1]
    grads = [
        dq[...].astype(f32),
        dk[...].astype(f32) + back[:, :wide].astype(f32),
        dv[...].astype(f32) + back[:, wide:].astype(f32),
    ]
    sums[0:1] = jnp.sum(grads[0], 0, keepdims=True)
    sums[1:2] = jnp.sum(grads[2], 0, keepdims=True)
    after = jnp.zeros((count, lanes - 3 * piece), f32)

    def write(which, i, c):
        blocks = [g[:, c * piece : (c + 1) * piece] for g in grads]
        (own, oth)[which][i] = jnp.concatenate([*blocks, after], 1).astype(bf16)

    split_all(column, cols, write)


def whole_specs(shapes):
    return [pl.BlockSpec(s, lambda i, p, n=len(s): (0,) * n) for s in shapes]


def split_call(kernel, column, operands, out_shapes, name):
    moved = sum(x.size * x.dtype.itemsize for x in operands) * 2
    return pl.pallas_call(
        kernel,
        grid_spec=pltpu.PrefetchScalarGridSpec(
            num_scalar_prefetch=1,
            grid=(1,),
            in_specs=whole_specs([x.shape for x in operands]),
            out_specs=whole_specs([s.shape for s in out_shapes]),
        ),
        out_shape=out_shapes,
        compiler_params=pltpu.CompilerParams(vmem_limit_bytes=48 << 20),
        cost_estimate=pl.CostEstimate(flops=moved, bytes_accessed=moved, transcendentals=0),
        name=name,
    )(column, *operands)


def block_grads_kernel(counts, has_vec, has_received, split, place, *refs):
    refs = list(refs)
    step = pl.program_id(0)
    lefts = [refs.pop(0) for _ in counts]
    rights = [[refs.pop(0) for _ in range(count)] for count in counts]
    vec_part = refs.pop(0) if has_vec else None
    received = refs.pop(0) if has_received else None
    total = refs.pop()

    def product(left, right):
        right = right[0] if len(right.shape) == 3 else right[...]
        return jnp.dot(left[...], right, preferred_element_type=f32)

    if counts[0] > 1:
        for i, right in enumerate(rights[0]):

            @pl.when(step == i)
            def _(right=right):
                total[...] = product(lefts[0], right)

    else:
        lanes_one = rights[0][0].shape[-1]
        total[:, :lanes_one] = product(lefts[0], rights[0][0])
        total[:, lanes_one:] = jnp.zeros_like(total[:, lanes_one:])
    for left, right in zip(lefts[1:], rights[1:]):
        total[:, -right[0].shape[-1] :] += product(left, right[0])
    if has_vec:
        total[:, -LANES:] += vec_part[0].astype(f32)
    if has_received:
        total[...] += received[0].astype(f32)
    if not split:
        refs[0][0] = total[...].astype(bf16)
        return
    first_keep, first_send, second_keep, second_send = refs
    half = total.shape[0] // 2
    quarter = half // 2

    def rows(start):
        return total[pl.ds(pl.multiple_of(start, 8), quarter)].astype(bf16)

    first_keep[0] = rows(place[0] * half)
    first_send[0] = rows((1 - place[0]) * half)
    for i, second in enumerate((second_keep, second_send)):

        @pl.when(step == i)
        def _(second=second):
            for dp in range(2):
                second[dp] = total[dp * half + quarter : (dp + 1) * half].astype(bf16)


def block_grads(pairs, vec_part, received, split):
    lefts, rights = zip(*pairs)
    rights = [r if isinstance(r, list) else [r] for r in rights]
    width, count = lefts[0].shape
    each = 2
    lanes = rights[0][0].shape[-1] if len(pairs) == 1 else -(-width // LANES) * LANES
    place = lax.axis_index("dp").reshape(1).astype(jnp.int32)

    def fixed(shape):
        return pl.BlockSpec(shape, lambda i, place: (0,) * len(shape))

    def step(shape):
        return pl.BlockSpec((1, *shape[1:]), lambda i, place: (i, 0, 0))

    flat = [r for right in rights for r in right]
    more = [x for x in (vec_part, received) if x is not None]
    in_specs = [fixed(x.shape) for x in lefts]
    in_specs += [step(x.shape) if x.ndim == 3 else fixed(x.shape) for x in flat]
    in_specs += [step(x.shape) for x in more]
    if split:
        part = (each, width // 4, lanes)
        out_specs = [step(part), step(part), fixed(part), fixed(part)]
        out_shape = [jax.ShapeDtypeStruct(part, bf16)] * 4
    else:
        out_specs = step((each, width, lanes))
        out_shape = jax.ShapeDtypeStruct((each, width, lanes), bf16)
    return pl.pallas_call(
        functools.partial(
            block_grads_kernel,
            [len(r) for r in rights],
            vec_part is not None,
            received is not None,
            split,
        ),
        grid_spec=pltpu.PrefetchScalarGridSpec(
            num_scalar_prefetch=1,
            grid=(each,),
            in_specs=in_specs,
            out_specs=out_specs,
            scratch_shapes=[pltpu.VMEM((width, lanes), f32)],
        ),
        out_shape=out_shape,
        compiler_params=pltpu.CompilerParams(vmem_limit_bytes=56 << 20),
        cost_estimate=pl.CostEstimate(
            flops=2 * each * count * width * lanes,
            bytes_accessed=2 * each * width * lanes * 2,
            transcendentals=0,
        ),
        name="block_grads",
    )(place, *lefts, *flat, *more)


AXES = ("col", "dp", "row")


def planes():
    owners = lax.axis_size("dp") * lax.axis_size("row")
    cols = lax.axis_size("col")
    return [
        [c * owners + k for c in range(p, cols, 2) for k in range(owners)] for p in range(2)
    ]


def flip_col(block, bit):
    return lax.ppermute(block, "col", [(c, c ^ bit) for c in range(lax.axis_size("col"))])


def partner(block):
    return flip_col(block, 1)


def flip_dp(block):
    return lax.ppermute(block, "dp", [(0, 1), (1, 0)])


def shift_row(block, by):
    count = lax.axis_size("row")
    return lax.ppermute(block, "row", [(i, (i + by) % count) for i in range(count)])


def by_place(blocks):
    column = lax.axis_index("col")
    pairs = blocks.reshape(-1, 2, *blocks.shape[1:])
    pairs = jnp.where(column % 2 == 1, pairs[:, ::-1], pairs)
    return upper_bit(pairs).reshape(blocks.shape)


def upper_bit(blocks):
    return jnp.where(lax.axis_index("col") // 2 == 1, blocks[::-1], blocks)


def short_rows():
    return lax.axis_size("row") == 4 and lax.axis_size("dp") == 2 and lax.axis_size("col") == 4


def assemble_kernel(ranges, targets, *refs):
    sources, out = refs[:-1], refs[-1]
    step = pl.program_id(0)
    for (start, end), source in zip(ranges, sources):

        @pl.when((step >= start) & (step < end))
        def _(source=source):
            out[...] = source[...]


def assemble(pieces):
    rows, lanes = pieces[0].shape[-2:]
    pieces = [p.reshape(-1, rows, lanes) for p in pieces]
    starts = [sum(p.shape[0] for p in pieces[:k]) for k in range(len(pieces))]
    ends = [start + p.shape[0] for start, p in zip(starts, pieces)]
    over_x = jnp.array([0, 0, 1, 1, 0, 0, 0, 0, 0, 0, 1, 1, 1, 1, 1, 1], jnp.int32)
    over_y = jnp.array([0, 0, 0, 0, 0, 0, 1, 1, 1, 1, 1, 1, 0, 0, 1, 1], jnp.int32)
    behind = jnp.array([0, 1, 0, 1, 2, 3, 2, 3, 0, 1, 0, 1, 2, 3, 2, 3], jnp.int32)
    dp, row = lax.axis_index("dp"), lax.axis_index("row")
    targets = (over_x * 8 + (dp ^ over_y) * 4 + (row + 4 - behind) % 4).astype(jnp.int32)

    def from_piece(start, end):
        return pl.BlockSpec(
            (1, rows, lanes), lambda i, targets: (jnp.clip(i - start, 0, end - start - 1), 0, 0)
        )

    out = pl.pallas_call(
        functools.partial(assemble_kernel, tuple(zip(starts, ends))),
        grid_spec=pltpu.PrefetchScalarGridSpec(
            num_scalar_prefetch=1,
            grid=(ends[-1],),
            in_specs=[from_piece(start, end) for start, end in zip(starts, ends)],
            out_specs=pl.BlockSpec((1, rows, lanes), lambda i, targets: (targets[i], 0, 0)),
        ),
        out_shape=jax.ShapeDtypeStruct((ends[-1], rows, lanes), bf16),
        compiler_params=pltpu.CompilerParams(vmem_limit_bytes=32 << 20),
        cost_estimate=pl.CostEstimate(
            flops=0, bytes_accessed=64 * rows * lanes, transcendentals=0
        ),
        name="assemble",
    )(targets, *pieces)
    return out.reshape(2, -1, lanes)


def spread_rows(block):
    return [block] + [shift_row(block, m) for m in range(1, 4)]


def spread_one(pieces):
    first, second = jnp.stack(pieces[:2]), jnp.stack(pieces[2:])
    return [first, flip_col(first, 2), second, flip_dp(second)]


def spread_two(pieces):
    first_y = flip_dp(jnp.stack(pieces[:2]))
    return [*pieces, first_y, flip_col(jnp.stack(pieces[2:]), 2)]


def gather_groups(block):
    whole = lax.all_gather(block, AXES, axis=0, tiled=False, axis_index_groups=planes())
    return upper_bit(whole.reshape(lax.axis_size("col") // 2, -1, block.shape[-1]))


def together(*arrays):
    return lax.optimization_barrier(arrays)


def added(one, other):
    return (one.astype(f32) + other.astype(f32)).astype(bf16)


def at_place(array, which, axis):
    return lax.dynamic_index_in_dim(array, which, axis, keepdims=False)


def scatter_one(blocks):
    if not short_rows():
        return blocks
    first_keep, first_send, second_keep, second_send = blocks
    first_y, second_x = flip_dp(first_send), flip_col(second_send, 2)
    return added(first_keep, first_y), added(second_keep, second_x)


def scatter_two(halves):
    if not short_rows():
        return halves
    dp = lax.axis_index("dp")
    first, second = halves
    first_x = flip_col(first[1], 2)
    second_y = flip_dp(at_place(second, 1 - dp, 0))
    both = jnp.concatenate(
        [added(first[0], first_x), added(at_place(second, dp, 0), second_y)], 0
    )
    return both.reshape(4, -1, both.shape[-1])


def scatter_three(rows):
    if not short_rows():
        flat = upper_bit(rows).reshape(-1, rows.shape[-1])
        return lax.psum_scatter(
            flat, AXES, scatter_dimension=0, tiled=True, axis_index_groups=planes()
        ).astype(f32)
    row = lax.axis_index("row")
    total = at_place(rows, row, 0).astype(f32)
    for m in range(1, 4):
        total = total + shift_row(at_place(rows, (row + m) % 4, 0), m).astype(f32)
    return total


def local(
    hidden_in,
    cotangent,
    segments,
    qkv_weight,
    out_weight,
    up_weight,
    down_weight,
    vectors,
    qkv_first,
    out_first,
    up_first,
    down_first,
    vectors_first,
    qkv_second,
    out_second,
    up_second,
    down_second,
    vectors_second,
):
    column = lax.axis_index("col")
    cols = lax.axis_size("col")
    here, width = hidden_in.shape
    rows_own = qkv_weight.shape[0]
    owners = lax.axis_size("dp") * lax.axis_size("row")
    piece = qkv_weight.shape[2]
    halves = SEQ // here
    each = cols // 2
    column_word = column.reshape(1).astype(jnp.int32)
    places_own = (column ^ (2 * jnp.arange(each))).astype(jnp.int32)
    places_oth = (column ^ (2 * jnp.arange(each) + 1)).astype(jnp.int32)
    later = lax.rem(column, halves).reshape(1).astype(jnp.int32)
    padded = -(-width // LANES) * LANES
    spare = padded - width
    lanes_qkv = -(-3 * piece // LANES) * LANES
    lead_out = 3 * piece // LANES * LANES
    lanes_out = padded - lead_out

    vec_shape = vectors.shape
    vec_count = vec_shape[0] * vec_shape[1]
    vec_lines = -(-vec_count // spare)
    vec_fill = vec_lines * spare - vec_count
    vec_lanes = jnp.pad(vectors.reshape(vec_count).astype(bf16), (0, vec_fill))
    attn_block = jnp.concatenate(
        [
            qkv_weight.reshape(rows_own, 3 * piece).astype(bf16),
            out_weight.T.astype(bf16),
            jnp.pad(vec_lanes.reshape(vec_lines, spare), ((0, rows_own - vec_lines), (0, 0))),
        ],
        1,
    )
    up_block, down_block = up_weight.astype(bf16), down_weight.T.astype(bf16)
    staged = short_rows()
    if staged:
        attn_one = spread_one(spread_rows(attn_block))
        up_block, attn_one = together(up_block, attn_one)
        up_rows = spread_rows(up_block)
        down_block, up_rows = together(down_block, up_rows)
        down_rows = spread_rows(down_block)
        attn_own = assemble(spread_two(attn_one))
        up_one, down_one = spread_one(up_rows), spread_one(down_rows)
    else:
        attn_own, up_own, down_own = [
            gather_groups(b) for b in (attn_block, up_block, down_block)
        ]
    vec_own = attn_own.reshape(each, owners, rows_own, padded)[:, :, :vec_lines, width:]
    vec_oth = partner(vec_own)
    attn_oth = partner(attn_own)

    def vec_rows(lines):
        lines = lines.reshape(each, owners, vec_lines * spare)[:, :, :vec_count]
        lines = lines.reshape(each, owners, *vec_shape).transpose(0, 2, 1, 3)
        return lines.reshape(each, vec_shape[0], width).astype(f32)

    vec = jnp.stack([vec_rows(vec_own), vec_rows(vec_oth)], 1).reshape(cols, -1, width)
    vec = by_place(vec).reshape(-1, width)

    def widen(row):
        return jnp.pad(row, (0, spare))

    inputs = hidden_in.astype(f32)
    normed_one, scaled_one, inverse_one = normalize(inputs, vec[0], vec[1])
    normed_low = normed_one.astype(bf16)
    if staged:
        normed_low, up_one = together(normed_low, up_one)
        up_two = spread_two(up_one)
    bias = jnp.concatenate([widen(vec[2]), jnp.zeros((padded,), f32), widen(vec[3])]).reshape(1, -1)
    spans = tuple((part * piece, part * padded) for part in range(3))
    projected = None
    for places, weights in ((places_own, attn_own), (places_oth, attn_oth)):
        projected = multiply_and_place(
            places, normed_low, [weights], lanes_qkv, 0, spans, piece, 3 * padded, bias, projected
        )
    if staged:
        projected, down_one = together(projected, down_one)
        down_two = spread_two(down_one)
    ahead = [(c, c + 1) for c in range(cols - 1) if c % halves + 1 < halves]
    behind = [(b, a) for a, b in ahead]
    others = lax.ppermute(projected[:, padded:], "col", ahead)

    own_half = lax.dynamic_slice_in_dim(segments.reshape(-1), column * here, here, 0)
    first_half = lax.dynamic_slice_in_dim(
        segments.reshape(-1), (column - lax.rem(column, halves)) * here, here, 0
    )
    labels = (own_half.reshape(1, here), own_half.reshape(here, 1), first_half.reshape(here, 1))
    mixed, log_totals = attend(later, labels, projected, others)
    if staged:
        mixed, up_two = together(mixed, up_two)
        up_own = assemble(up_two)
    up_oth = partner(up_own)
    mixed_shape = jax.ShapeDtypeStruct((each, here, lanes_out), bf16)
    lead = 3 * piece - lead_out
    mixed_own, mixed_oth = split_call(
        functools.partial(split_mixed_kernel, piece, cols, lead),
        column_word,
        [mixed],
        [mixed_shape] * 2,
        "split_mixed",
    )
    residual = inputs + vec[4]
    for blocks, weights in ((mixed_own, attn_own), (mixed_oth, attn_oth)):
        for i in range(each):
            residual = residual + contract_last(blocks[i], weights[i][:, lead_out:])
    normed_two, scaled_two, inverse_two = normalize(residual, vec[5], vec[6])
    normed_two_low = normed_two.astype(bf16)

    bias_up = by_place(vec[8:])
    bias_own, bias_oth = bias_up[0::2], bias_up[1::2]

    def up_part(ups, biases):
        return [
            jnp.dot(normed_two_low, ups[i], preferred_element_type=f32) + biases[i]
            for i in range(each)
        ]

    linear_own = up_part(up_own, bias_own)
    if staged:
        linear_own, down_two = together(linear_own, down_two)
        down_own = assemble(down_two)
    down_oth = partner(down_own)
    linear_oth = up_part(up_oth, bias_oth)

    branch = jnp.zeros((here, width), f32)

    def forward_part(linears, downs, branch):
        lows, pullbacks = [], []
        for i in range(each):
            active, pullback = jax.vjp(gelu_tanh, linears[i])
            lows.append(active.astype(bf16))
            pullbacks.append(pullback)
            branch = branch + contract_last(lows[i], downs[i])
        return lows, pullbacks, branch

    lows_own, pull_own, branch = forward_part(linear_own, down_own, branch)
    lows_oth, pull_oth, branch = forward_part(linear_oth, down_oth, branch)
    layer_out = (residual + branch + vec[7]).astype(bf16)

    left_down, left_up = cotangent.T, normed_two_low.T
    sent_down = block_grads([(left_down, lows_oth)], None, None, False)
    down_oth, sent_down = together(down_oth, sent_down)
    received_down = partner(sent_down)

    grad_normed_two = jnp.zeros((here, width), f32)

    def backward_part(ups, downs, pullbacks, grad_normed_two):
        lows, sums = [], []
        for i in range(each):
            grad_active = jnp.dot(cotangent, downs[i], preferred_element_type=f32)
            grad_linear = pullbacks[i](grad_active)[0]
            lows.append(grad_linear.astype(bf16))
            sums.append(jnp.sum(grad_linear, 0))
            grad_normed_two = grad_normed_two + contract_last(lows[i], ups[i])
        return lows, sums, grad_normed_two

    dups_oth, dbias_oth, grad_normed_two = backward_part(
        up_oth, down_oth, pull_oth, grad_normed_two
    )
    lows_own, dups_oth = together(lows_own, dups_oth)
    total_down = block_grads([(left_down, lows_own)], None, received_down, staged)
    sent_up = block_grads([(left_up, dups_oth)], None, None, False)
    down_own, total_down, sent_up = together(down_own, total_down, sent_up)
    received_up = partner(sent_up)
    one_down = scatter_one(total_down)
    dups_own, dbias_own, grad_normed_two = backward_part(
        up_own, down_own, pull_own, grad_normed_two
    )

    grad_residual = cotangent.astype(f32) + norm_back(
        grad_normed_two, scaled_two, inverse_two, vec[5]
    )
    grad_residual_low = grad_residual.astype(bf16)
    grad_mixed = multiply_and_place(
        jnp.concatenate([places_own, places_oth]),
        grad_residual_low,
        [attn_own, attn_oth],
        lanes_out,
        lead_out // lanes_out,
        ((lead, 0),),
        piece,
        padded,
        None,
        None,
    )
    total_up = block_grads([(left_up, dups_own)], None, received_up, staged)
    grad_mixed, total_up, one_down = together(grad_mixed, total_up, one_down)
    dq, dk_own, dv_own, dk_oth, dv_oth = attend_back(
        later, labels, projected, others, grad_mixed, mixed, log_totals
    )
    back = lax.ppermute(jnp.concatenate([dk_oth, dv_oth], 1), "col", behind)
    two_down = scatter_two(one_down)
    one_up = scatter_one(total_up)
    dq, dk_own, dv_own, two_down, one_up = together(dq, dk_own, dv_own, two_down, one_up)
    grads_shape = jax.ShapeDtypeStruct((each, here, lanes_qkv), bf16)
    grads_own, grads_oth, grad_sums = split_call(
        functools.partial(split_grads_kernel, piece, cols),
        column_word,
        [dq, dk_own, dv_own, back],
        [grads_shape, grads_shape, jax.ShapeDtypeStruct((8, padded), f32)],
        "split_grads",
    )
    two_up = scatter_two(one_up)
    left_one, left_two = normed_low.T, grad_residual_low.T
    pairs_oth = [(left_one, grads_oth), (left_two, mixed_oth)]
    pairs_own = [(left_one, grads_own), (left_two, mixed_own)]
    received = partner(block_grads(pairs_oth, None, None, False))
    grad_normed_one = jnp.zeros((here, width), f32)
    for blocks, weights in ((grads_own, attn_own), (grads_oth, attn_oth)):
        for i in range(each):
            grad_normed_one = grad_normed_one + contract_last(blocks[i], weights[i][:, :lanes_qkv])
    input_grad = grad_residual + norm_back(grad_normed_one, scaled_one, inverse_one, vec[0])

    dbias = jnp.stack([jnp.stack(dbias_own), jnp.stack(dbias_oth)], 1).reshape(cols, width)
    grad_vector = jnp.concatenate(
        [
            jnp.stack(
                [
                    jnp.sum(grad_normed_one * scaled_one, 0),
                    jnp.sum(grad_normed_one, 0),
                    grad_sums[0, :width],
                    grad_sums[1, :width],
                    jnp.sum(grad_residual, 0),
                    jnp.sum(grad_normed_two * scaled_two, 0),
                    jnp.sum(grad_normed_two, 0),
                    jnp.sum(cotangent.astype(f32), 0),
                ]
            ),
            by_place(dbias),
        ],
        0,
    ).astype(bf16)
    vec_part = grad_vector.reshape(cols, vec_shape[0], owners, vec_shape[1]).transpose(0, 2, 1, 3)
    vec_part = jnp.pad(vec_part.reshape(cols, owners, vec_count), ((0, 0), (0, 0), (0, vec_fill)))
    vec_part = by_place(vec_part.reshape(cols, owners, vec_lines, spare))
    vec_here = (vec_part[0::2].astype(f32) + partner(vec_part[1::2]).astype(f32)).astype(bf16)
    vec_here = jnp.pad(
        vec_here, ((0, 0), (0, 0), (0, rows_own - vec_lines), (LANES - spare, 0))
    ).reshape(each, width, LANES)
    total_attn = block_grads(pairs_own, vec_here, received, staged)
    sum_down, sum_up = scatter_three(two_down), scatter_three(two_up)
    sum_attn = scatter_three(scatter_two(scatter_one(total_attn)))
    sum_qkv = sum_attn[:, : 3 * piece].reshape(rows_own, 3, piece)
    sum_out = sum_attn[:, 3 * piece : width].T
    sum_vector = sum_attn[:vec_lines, width:].reshape(-1)[:vec_count].reshape(vec_shape)

    qkv_m, qkv_v, qkv_w = adamw(
        qkv_weight, sum_qkv, qkv_first, qkv_second, 1.5 * D ** (-0.5), decay_rate
    )
    out_m, out_v, out_w = adamw(
        out_weight, sum_out, out_first, out_second, 1.5 * (D // 64) ** (-0.5), decay_rate
    )
    up_m, up_v, up_w = adamw(up_weight, sum_up, up_first, up_second, 1.5 * D ** (-0.5), decay_rate)
    down_m, down_v, down_w = adamw(
        down_weight, sum_down.T, down_first, down_second, 1.5 * FF ** (-0.5), decay_rate
    )
    vec_m, vec_v, vec_w = adamw(vectors, sum_vector, vectors_first, vectors_second, 0.5, 0.0)
    return (
        layer_out,
        input_grad,
        qkv_m,
        qkv_v,
        qkv_w,
        out_m,
        out_v,
        out_w,
        up_m,
        up_v,
        up_w,
        down_m,
        down_v,
        down_w,
        vec_m,
        vec_v,
        vec_w,
    )


def solution(mesh):
    tokens = P(("dp", "row", "col"), None)
    qkv = P(("dp", "row"), None, "col")
    tall = P("col", ("dp", "row"))
    up = P(("dp", "row"), "col")
    state = (qkv, tall, up, tall, tall)
    return jax.shard_map(
        local,
        mesh=mesh,
        in_specs=(tokens, tokens, P(("dp", "row"), None)) + state * 3,
        out_specs=(tokens, tokens)
        + (qkv,) * 3
        + (tall,) * 3
        + (up,) * 3
        + (tall,) * 3
        + (tall,) * 3,
        check_vma=False,
    )
```

```python
import functools

import jax
import jax.numpy as jnp
from jax import lax
from jax.experimental import pallas as pl
from jax.experimental.pallas import tpu as pltpu
from jax.sharding import PartitionSpec as P

D = 1088
HEAD_DIM = 64
FF = 4352
SEQ = 1024
STEP = 5

LANES = 128


beta_one = 0.9
beta_two = 0.999
epsilon = 1e-08
decay_rate = 0.1
masked_score = -1000000000.0

f32 = jnp.float32
bf16 = jnp.bfloat16


def contract(left, right, left_dim, right_dim):
    return lax.dot_general(
        left, right, (((left_dim,), (right_dim,)), ((), ())), preferred_element_type=f32
    )


def contract_first(left, right):
    return contract(left, right, 0, 0)


def contract_last(left, right):
    return contract(left, right, 1, 1)


def normalize(rows, gain, shift):
    row_mean = jnp.mean(rows, -1, keepdims=True)
    centred = rows - row_mean
    inverse = lax.rsqrt(jnp.mean(centred * centred, -1, keepdims=True) + 1e-05)
    scaled = centred * inverse
    return (scaled * gain + shift, scaled, inverse)


def norm_back(grad_out, scaled, inverse, gain):
    grad_scaled = grad_out * gain
    return inverse * (
        grad_scaled
        - jnp.mean(grad_scaled, -1, keepdims=True)
        - scaled * jnp.mean(grad_scaled * scaled, -1, keepdims=True)
    )


def gelu_tanh(values):
    return jax.nn.gelu(values, approximate=True)


def adamw(weight, gradient, moment_one, moment_two, step_rate, shrink):
    moment_one = beta_one * moment_one + (1.0 - beta_one) * gradient
    moment_two = beta_two * moment_two + (1.0 - beta_two) * gradient * gradient
    update = (
        moment_one
        / (1.0 - beta_one**STEP)
        / (jnp.sqrt(moment_two / (1.0 - beta_two**STEP)) + epsilon)
    )
    return (moment_one, moment_two, weight - step_rate * (update + shrink * weight))


def mask_tables(kseg_own, kseg_oth, qseg, bias_own, bias_oth):
    count = bias_own.shape[0]
    key_place = lax.broadcasted_iota(jnp.int32, (count, count), 0)
    query_place = lax.broadcasted_iota(jnp.int32, (count, count), 1)
    same = kseg_own[...] == qseg[...]
    bias_own[...] = jnp.where(same & (key_place <= query_place), 0.0, masked_score)
    bias_oth[...] = jnp.where(kseg_oth[...] == qseg[...], 0.0, masked_score)


def head_lanes(block, half):
    lane = lax.broadcasted_iota(jnp.int32, block.shape, 1)
    return jnp.where((lane // HEAD_DIM) == half, block, jnp.zeros_like(block))


def attention_forward(
    later, qseg, kseg_own, kseg_oth, q, k_own, v_own, k_oth, v_oth, out, lse, bias_own, bias_oth
):
    pair = pl.program_id(0)
    count = q.shape[0]
    step = count // 2

    @pl.when(pair == 0)
    def _():
        mask_tables(kseg_own, kseg_oth, qseg, bias_own, bias_oth)

    def body(with_other):
        queries = q[...] * jnp.asarray(HEAD_DIM**-0.5, bf16)
        values_own = v_own[...].astype(f32).T.astype(bf16)
        values_oth = v_oth[...].astype(f32).T.astype(bf16) if with_other else None
        for part in range(2):
            cols = slice(part * step, (part + 1) * step)
            seen = (part + 1) * step
            pieces = []
            for half in range(2):
                q_head = head_lanes(queries[cols], half)
                rows = slice(half * HEAD_DIM, (half + 1) * HEAD_DIM)
                s_own = contract_last(k_own[:seen], q_head) + bias_own[:seen, cols]
                top = jnp.max(s_own, 0, keepdims=True)
                if with_other:
                    s_oth = contract_last(k_oth[...], q_head) + bias_oth[:, cols]
                    top = jnp.maximum(top, jnp.max(s_oth, 0, keepdims=True))
                e_own = jnp.exp(s_own - top)
                total = jnp.sum(e_own, 0, keepdims=True)
                mixed = jnp.dot(
                    values_own[rows, :seen], e_own.astype(bf16), preferred_element_type=f32
                )
                if with_other:
                    e_oth = jnp.exp(s_oth - top)
                    total = total + jnp.sum(e_oth, 0, keepdims=True)
                    mixed = mixed + jnp.dot(
                        values_oth[rows], e_oth.astype(bf16), preferred_element_type=f32
                    )
                lse[0, half : half + 1, cols] = top + jnp.log(total)
                pieces.append(mixed / total)
            out[cols] = jnp.concatenate(pieces, 0).T.astype(bf16)

    @pl.when(later[0] == 1)
    def _():
        body(True)

    @pl.when(later[0] == 0)
    def _():
        body(False)


def attention_backward(
    later, qseg, kseg_own, kseg_oth, q, k_own, v_own, k_oth, v_oth, grad, out, lse,
    dq, dk_own, dv_own, dk_oth, dv_oth, bias_own, bias_oth,
):
    pair = pl.program_id(0)
    count = q.shape[0]
    step = count // 2

    @pl.when(pair == 0)
    def _():
        mask_tables(kseg_own, kseg_oth, qseg, bias_own, bias_oth)

    def body(with_other):
        scale = jnp.asarray(HEAD_DIM**-0.5, bf16)
        queries = q[...] * scale
        keys_own = k_own[...].astype(f32).T.astype(bf16)
        keys_oth = k_oth[...].astype(f32).T.astype(bf16) if with_other else None
        products = (grad[...].astype(f32) * out[...].astype(f32)).T
        dk_a = [jnp.zeros((step, LANES), f32) for _ in range(2)]
        dv_a = [jnp.zeros((step, LANES), f32) for _ in range(2)]
        dk_b = jnp.zeros((count, LANES), f32)
        dv_b = jnp.zeros((count, LANES), f32)
        for part in range(2):
            cols = slice(part * step, (part + 1) * step)
            pieces = []
            for half in range(2):
                q_head = head_lanes(queries[cols], half)
                g_head = head_lanes(grad[cols], half)
                rows = slice(half * HEAD_DIM, (half + 1) * HEAD_DIM)
                delta = jnp.sum(products[rows, cols], 0, keepdims=True)
                log_total = lse[0, half : half + 1, cols]

                def block(keys, values, bias):
                    probs = jnp.exp(contract_last(keys, q_head) + bias - log_total)
                    d_probs = contract_last(values, g_head)
                    d_scores = (probs * (d_probs - delta)).astype(bf16)
                    dk = jnp.dot(d_scores, q_head, preferred_element_type=f32)
                    dv = jnp.dot(probs.astype(bf16), g_head, preferred_element_type=f32)
                    return (d_scores, dk, dv)

                d_query = jnp.zeros((HEAD_DIM, step), f32)
                for chunk in range(part + 1):
                    span = slice(chunk * step, (chunk + 1) * step)
                    d_scores, dk, dv = block(k_own[span], v_own[span], bias_own[span, cols])
                    dk_a[chunk] = dk_a[chunk] + dk
                    dv_a[chunk] = dv_a[chunk] + dv
                    d_query = d_query + jnp.dot(
                        keys_own[rows, span], d_scores, preferred_element_type=f32
                    )
                if with_other:
                    d_scores, dk, dv = block(k_oth[...], v_oth[...], bias_oth[:, cols])
                    dk_b = dk_b + dk
                    dv_b = dv_b + dv
                    d_query = d_query + jnp.dot(
                        keys_oth[rows], d_scores, preferred_element_type=f32
                    )
                pieces.append(d_query)
            dq[cols] = (jnp.concatenate(pieces, 0).T * HEAD_DIM**-0.5).astype(bf16)
        for chunk in range(2):
            span = slice(chunk * step, (chunk + 1) * step)
            dk_own[span] = dk_a[chunk].astype(bf16)
            dv_own[span] = dv_a[chunk].astype(bf16)
        dk_oth[...] = dk_b.astype(bf16)
        dv_oth[...] = dv_b.astype(bf16)

    @pl.when(later[0] == 1)
    def _():
        body(True)

    @pl.when(later[0] == 0)
    def _():
        body(False)


def attention_specs(count, pairs):
    def whole(shape):
        return pl.BlockSpec(shape, lambda p, later: (0,) * len(shape))

    def lanes(start):
        return pl.BlockSpec((count, LANES), lambda p, later: (0, start + p))

    segments = [whole((1, count)), whole((count, 1)), whole((count, 1))]
    projected = [lanes(0), lanes(pairs), lanes(2 * pairs), lanes(0), lanes(pairs)]
    totals = pl.BlockSpec((1, 2, count), lambda p, later: (p, 0, 0))
    return segments, projected, lanes(0), totals


def attend(later, labels, projected, others):
    count = projected.shape[0]
    pairs = projected.shape[1] // (3 * LANES)
    segments, blocks, wide, totals = attention_specs(count, pairs)
    work = count * count * LANES * pairs * 2
    return pl.pallas_call(
        attention_forward,
        grid_spec=pltpu.PrefetchScalarGridSpec(
            num_scalar_prefetch=1,
            grid=(pairs,),
            in_specs=segments + blocks,
            out_specs=[wide, totals],
            scratch_shapes=[pltpu.VMEM((count, count), f32), pltpu.VMEM((count, count), f32)],
        ),
        out_shape=[
            jax.ShapeDtypeStruct((count, pairs * LANES), bf16),
            jax.ShapeDtypeStruct((pairs, 2, count), f32),
        ],
        compiler_params=pltpu.CompilerParams(vmem_limit_bytes=48 << 20),
        name="attention_forward",
    )(later, *labels, projected, projected, projected, others, others)


def attend_back(later, labels, projected, others, grad, mixed, log_totals):
    count = projected.shape[0]
    pairs = projected.shape[1] // (3 * LANES)
    segments, blocks, wide, totals = attention_specs(count, pairs)
    work = count * count * LANES * pairs * 2
    return pl.pallas_call(
        attention_backward,
        grid_spec=pltpu.PrefetchScalarGridSpec(
            num_scalar_prefetch=1,
            grid=(pairs,),
            in_specs=segments + blocks + [wide, wide, totals],
            out_specs=[wide] * 5,
            scratch_shapes=[pltpu.VMEM((count, count), f32), pltpu.VMEM((count, count), f32)],
        ),
        out_shape=[jax.ShapeDtypeStruct((count, pairs * LANES), bf16)] * 5,
        compiler_params=pltpu.CompilerParams(vmem_limit_bytes=48 << 20),
        name="attention_backward",
    )(later, *labels, projected, projected, projected, others, others, grad, mixed, log_totals)


def place_kernel(spans, piece, sources, biased, continued, places, x, *refs):
    weights, refs = refs[:sources], refs[sources:]
    bias, refs = (refs[0], refs[1:]) if biased else (None, refs)
    before, refs = (refs[0], refs[1:]) if continued else (None, refs)
    out, whole, product = refs
    step = pl.program_id(0)
    each = pl.num_programs(0) // sources

    @pl.when(step == 0)
    def _():
        whole[...] = before[...].astype(f32) if continued else jnp.zeros_like(whole)

    for k, weight in enumerate(weights):

        @pl.when(step // each == k)
        def _(weight=weight):
            product[...] = jnp.dot(x[...], weight[0], preferred_element_type=f32)

    for place in range(x.shape[1] // piece):

        @pl.when(places[step] == place)
        def _(place=place):
            for source, target in spans:
                start = target + place * piece
                block = product[:, source : source + piece]
                if biased:
                    block = block + bias[:, start : start + piece]
                whole[:, start : start + piece] = block

    @pl.when(step == pl.num_programs(0) - 1)
    def _():
        out[...] = whole[...].astype(bf16)


def multiply_and_place(places, x, weights, lanes, lane_block, spans, piece, out_lanes, bias, before):
    count, depth = x.shape
    each = weights[0].shape[0]
    sources = len(weights)

    def fixed(shape):
        return pl.BlockSpec(shape, lambda j, places: (0, 0))

    in_specs = [fixed((count, depth))]
    for k in range(sources):
        in_specs.append(
            pl.BlockSpec(
                (1, depth, lanes),
                lambda j, places, k=k: (jnp.clip(j - k * each, 0, each - 1), 0, lane_block),
            )
        )
    operands = [x, *weights]
    if bias is not None:
        in_specs.append(fixed(bias.shape))
        operands.append(bias)
    if before is not None:
        in_specs.append(fixed(before.shape))
        operands.append(before)
    return pl.pallas_call(
        functools.partial(
            place_kernel, spans, piece, sources, bias is not None, before is not None
        ),
        grid_spec=pltpu.PrefetchScalarGridSpec(
            num_scalar_prefetch=1,
            grid=(each * sources,),
            in_specs=in_specs,
            out_specs=fixed((count, out_lanes)),
            scratch_shapes=[pltpu.VMEM((count, out_lanes), f32), pltpu.VMEM((count, lanes), f32)],
        ),
        out_shape=jax.ShapeDtypeStruct((count, out_lanes), bf16),
        compiler_params=pltpu.CompilerParams(vmem_limit_bytes=48 << 20),
        name="multiply_and_place",
    )(places, *operands)


def split_all(column, cols, write):
    for here in range(cols):

        @pl.when(column[0] == here)
        def _(here=here):
            for k in range(cols):
                write(k % 2, k // 2, here ^ k)


def split_mixed_kernel(piece, cols, lead, column, mixed, own, oth):
    count, lanes = own.shape[1:]
    values = mixed[...].astype(f32)
    before = jnp.zeros((count, lead), f32)
    after = jnp.zeros((count, lanes - lead - piece), f32)

    def write(which, i, c):
        block = values[:, c * piece : (c + 1) * piece]
        (own, oth)[which][i] = jnp.concatenate([before, block, after], 1).astype(bf16)

    split_all(column, cols, write)


def split_grads_kernel(piece, cols, column, dq, dk, dv, back, own, oth, sums):
    count, lanes = own.shape[1:]
    wide = dq.shape[1]
    grads = [
        dq[...].astype(f32),
        dk[...].astype(f32) + back[:, :wide].astype(f32),
        dv[...].astype(f32) + back[:, wide:].astype(f32),
    ]
    sums[0:1] = jnp.sum(grads[0], 0, keepdims=True)
    sums[1:2] = jnp.sum(grads[2], 0, keepdims=True)
    after = jnp.zeros((count, lanes - 3 * piece), f32)

    def write(which, i, c):
        blocks = [g[:, c * piece : (c + 1) * piece] for g in grads]
        (own, oth)[which][i] = jnp.concatenate([*blocks, after], 1).astype(bf16)

    split_all(column, cols, write)


def whole_specs(shapes):
    return [pl.BlockSpec(s, lambda i, p, n=len(s): (0,) * n) for s in shapes]


def split_call(kernel, column, operands, out_shapes, name):
    moved = sum(x.size * x.dtype.itemsize for x in operands) * 2
    return pl.pallas_call(
        kernel,
        grid_spec=pltpu.PrefetchScalarGridSpec(
            num_scalar_prefetch=1,
            grid=(1,),
            in_specs=whole_specs([x.shape for x in operands]),
            out_specs=whole_specs([s.shape for s in out_shapes]),
        ),
        out_shape=out_shapes,
        compiler_params=pltpu.CompilerParams(vmem_limit_bytes=48 << 20),
        name=name,
    )(column, *operands)


def block_grads_kernel(counts, has_vec, has_received, split, place, *refs):
    refs = list(refs)
    step = pl.program_id(0)
    lefts = [refs.pop(0) for _ in counts]
    rights = [[refs.pop(0) for _ in range(count)] for count in counts]
    vec_part = refs.pop(0) if has_vec else None
    received = refs.pop(0) if has_received else None
    width = lefts[0].shape[0]
    quarter = width // 4

    def value(start, which):
        rows = pl.ds(start, quarter)
        if counts[0] > 1:
            whole = contract_last(lefts[0][rows], rights[0][which][...])
        else:
            one, two = [
                jnp.dot(left[rows], right[0][0], preferred_element_type=f32)
                for left, right in zip(lefts, rights)
            ]
            lead = one.shape[1] - LANES
            whole = jnp.concatenate(
                [one[:, :lead], one[:, lead:] + two[:, :LANES], two[:, LANES:]], 1
            )
        if has_vec:
            more = whole[:, -LANES:] + vec_part[0, rows].astype(f32)
            whole = jnp.concatenate([whole[:, :-LANES], more], 1)
        if has_received:
            whole = whole + received[0, rows].astype(f32)
        return whole.astype(bf16)

    for i in range(2):

        @pl.when(step == i)
        def _(i=i):
            if not split:
                for k in range(4):
                    refs[0][0, k * quarter : (k + 1) * quarter] = value(k * quarter, i)
                return
            first_keep, first_send, second_keep, second_send = refs
            half = width // 2
            first_keep[0] = value(pl.multiple_of(place[0] * half, 16), i)
            first_send[0] = value(pl.multiple_of((1 - place[0]) * half, 16), i)
            second = (second_keep, second_send)[i]
            for dp in range(2):
                second[dp] = value(dp * half + quarter, i)


def block_grads(pairs, vec_part, received, split):
    lefts, rights = zip(*pairs)
    rights = [r if isinstance(r, list) else [r] for r in rights]
    width, count = lefts[0].shape
    each = 2
    lanes = width if len(pairs) == 1 else -(-width // LANES) * LANES
    place = lax.axis_index("dp").reshape(1).astype(jnp.int32)

    def fixed(shape):
        return pl.BlockSpec(shape, lambda i, place: (0,) * len(shape))

    def step(shape):
        return pl.BlockSpec((1, *shape[1:]), lambda i, place: (i, 0, 0))

    flat = [r for right in rights for r in right]
    more = [x for x in (vec_part, received) if x is not None]
    in_specs = [fixed(x.shape) for x in lefts]
    in_specs += [step(x.shape) if x.ndim == 3 else fixed(x.shape) for x in flat]
    in_specs += [step(x.shape) for x in more]
    if split:
        part = (each, width // 4, lanes)
        out_specs = [step(part), step(part), fixed(part), fixed(part)]
        out_shape = [jax.ShapeDtypeStruct(part, bf16)] * 4
    else:
        out_specs = step((each, width, lanes))
        out_shape = jax.ShapeDtypeStruct((each, width, lanes), bf16)
    return pl.pallas_call(
        functools.partial(
            block_grads_kernel,
            [len(r) for r in rights],
            vec_part is not None,
            received is not None,
            split,
        ),
        grid_spec=pltpu.PrefetchScalarGridSpec(
            num_scalar_prefetch=1,
            grid=(each,),
            in_specs=in_specs,
            out_specs=out_specs,
        ),
        out_shape=out_shape,
        compiler_params=pltpu.CompilerParams(vmem_limit_bytes=48 << 20),
        name="block_grads",
    )(place, *lefts, *flat, *more)


AXES = ("col", "dp", "row")


def planes():
    owners = lax.axis_size("dp") * lax.axis_size("row")
    cols = lax.axis_size("col")
    return [
        [c * owners + k for c in range(p, cols, 2) for k in range(owners)] for p in range(2)
    ]


def flip_col(block, bit):
    return lax.ppermute(block, "col", [(c, c ^ bit) for c in range(lax.axis_size("col"))])


def partner(block):
    return flip_col(block, 1)


def flip_dp(block):
    return lax.ppermute(block, "dp", [(0, 1), (1, 0)])


def shift_row(block, by):
    count = lax.axis_size("row")
    return lax.ppermute(block, "row", [(i, (i + by) % count) for i in range(count)])


def by_place(blocks):
    column = lax.axis_index("col")
    pairs = blocks.reshape(-1, 2, *blocks.shape[1:])
    pairs = jnp.where(column % 2 == 1, pairs[:, ::-1], pairs)
    return upper_bit(pairs).reshape(blocks.shape)


def upper_bit(blocks):
    return jnp.where(lax.axis_index("col") // 2 == 1, blocks[::-1], blocks)


def short_rows():
    return lax.axis_size("row") == 4 and lax.axis_size("dp") == 2 and lax.axis_size("col") == 4


def assemble_kernel(place, *refs):
    sources, (out, held, sems_in, sems_out) = refs[:-4], refs[-4:]
    dp, row = place[0], place[1]
    order = (
        [(0, 0, 0), (0, 0, 1), (1, 0, 0), (1, 0, 1), (0, 0, 2), (0, 0, 3), (0, 1, 2), (0, 1, 3)]
        + [(0, 1, 0), (0, 1, 1), (1, 1, 0), (1, 1, 1)]
        + [(1, 0, 2), (1, 0, 3), (1, 1, 2), (1, 1, 3)]
    )
    blocks = [source.at[i] for source in sources for i in range(source.shape[0])]
    copies_in, copies_out = [], []
    for k, (block, (over_x, over_y, behind)) in enumerate(zip(blocks, order)):
        target = over_x * 8 + (1 - dp if over_y else dp) * 4 + lax.rem(row + 4 - behind, 4)
        copies_in.append(pltpu.make_async_copy(block, held.at[k], sems_in.at[k]))
        copies_out.append(pltpu.make_async_copy(held.at[k], out.at[target], sems_out.at[k]))
    for copy in copies_in:
        copy.start()
    for copy_in, copy_out in zip(copies_in, copies_out):
        copy_in.wait()
        copy_out.start()
    for copy in copies_out:
        copy.wait()


def assemble(pieces):
    rows, lanes = pieces[0].shape[-2:]
    pieces = [p.reshape(-1, rows, lanes) for p in pieces]
    place = jnp.stack([lax.axis_index("dp"), lax.axis_index("row")]).astype(jnp.int32)
    anywhere = pl.BlockSpec(memory_space=pl.ANY)
    out = pl.pallas_call(
        assemble_kernel,
        grid_spec=pltpu.PrefetchScalarGridSpec(
            num_scalar_prefetch=1,
            grid=(1,),
            in_specs=[anywhere] * len(pieces),
            out_specs=anywhere,
            scratch_shapes=[
                pltpu.VMEM((16, rows, lanes), bf16),
                pltpu.SemaphoreType.DMA((16,)),
                pltpu.SemaphoreType.DMA((16,)),
            ],
        ),
        out_shape=jax.ShapeDtypeStruct((16, rows, lanes), bf16),
        compiler_params=pltpu.CompilerParams(vmem_limit_bytes=48 << 20),
        name="assemble",
    )(place, *pieces)
    return out.reshape(2, -1, lanes)


def spread_rows(block):
    return [block] + [shift_row(block, m) for m in range(1, 4)]


def spread_one(pieces):
    first, second = jnp.stack(pieces[:2]), jnp.stack(pieces[2:])
    return [first, flip_col(first, 2), second, flip_dp(second)]


def spread_two(pieces):
    first_y = flip_dp(jnp.stack(pieces[:2]))
    return [*pieces, first_y, flip_col(jnp.stack(pieces[2:]), 2)]


def gather_groups(block):
    whole = lax.all_gather(block, AXES, axis=0, tiled=False, axis_index_groups=planes())
    return upper_bit(whole.reshape(lax.axis_size("col") // 2, -1, block.shape[-1]))


def together(*arrays):
    return lax.optimization_barrier(arrays)


def added(one, other):
    return (one.astype(f32) + other.astype(f32)).astype(bf16)


def at_place(array, which, axis):
    return lax.dynamic_index_in_dim(array, which, axis, keepdims=False)


def scatter_one(blocks):
    if not short_rows():
        return blocks
    first_keep, first_send, second_keep, second_send = blocks
    first_y, second_x = flip_dp(first_send), flip_col(second_send, 2)
    return added(first_keep, first_y), added(second_keep, second_x)


def scatter_two(halves):
    if not short_rows():
        return halves
    dp = lax.axis_index("dp")
    first, second = halves
    first_x = flip_col(first[1], 2)
    second_y = flip_dp(at_place(second, 1 - dp, 0))
    both = jnp.concatenate(
        [added(first[0], first_x), added(at_place(second, dp, 0), second_y)], 0
    )
    return both.reshape(4, -1, both.shape[-1])


def scatter_three(rows):
    if not short_rows():
        flat = upper_bit(rows).reshape(-1, rows.shape[-1])
        return lax.psum_scatter(
            flat, AXES, scatter_dimension=0, tiled=True, axis_index_groups=planes()
        ).astype(f32)
    row = lax.axis_index("row")
    total = at_place(rows, row, 0).astype(f32)
    for m in range(1, 4):
        total = total + shift_row(at_place(rows, (row + m) % 4, 0), m).astype(f32)
    return total


def local(
    hidden_in,
    cotangent,
    segments,
    qkv_weight,
    out_weight,
    up_weight,
    down_weight,
    vectors,
    qkv_first,
    out_first,
    up_first,
    down_first,
    vectors_first,
    qkv_second,
    out_second,
    up_second,
    down_second,
    vectors_second,
):
    column = lax.axis_index("col")
    cols = lax.axis_size("col")
    here, width = hidden_in.shape
    rows_own = qkv_weight.shape[0]
    owners = lax.axis_size("dp") * lax.axis_size("row")
    piece = qkv_weight.shape[2]
    halves = SEQ // here
    each = cols // 2
    column_word = column.reshape(1).astype(jnp.int32)
    places_own = (column ^ (2 * jnp.arange(each))).astype(jnp.int32)
    places_oth = (column ^ (2 * jnp.arange(each) + 1)).astype(jnp.int32)
    later = lax.rem(column, halves).reshape(1).astype(jnp.int32)
    padded = -(-width // LANES) * LANES
    spare = padded - width
    lanes_qkv = -(-3 * piece // LANES) * LANES
    lead_out = 3 * piece // LANES * LANES
    lanes_out = padded - lead_out

    vec_shape = vectors.shape
    vec_count = vec_shape[0] * vec_shape[1]
    vec_lines = -(-vec_count // spare)
    vec_fill = vec_lines * spare - vec_count
    vec_lanes = jnp.pad(vectors.reshape(vec_count).astype(bf16), (0, vec_fill))
    attn_block = jnp.concatenate(
        [
            qkv_weight.reshape(rows_own, 3 * piece).astype(bf16),
            out_weight.T.astype(bf16),
            jnp.pad(vec_lanes.reshape(vec_lines, spare), ((0, rows_own - vec_lines), (0, 0))),
        ],
        1,
    )
    up_block, down_block = up_weight.astype(bf16), down_weight.T.astype(bf16)
    staged = short_rows()
    if staged:
        attn_rows = spread_rows(attn_block)
        up_block, attn_rows = together(up_block, attn_rows)
        attn_one = spread_one(attn_rows)
        up_rows = spread_rows(up_block)
        down_block, up_rows = together(down_block, up_rows)
        down_rows = spread_rows(down_block)
        attn_own = assemble(spread_two(attn_one))
        up_one = spread_one(up_rows)
    else:
        attn_own, up_own, down_own = [
            gather_groups(b) for b in (attn_block, up_block, down_block)
        ]
    vec_own = attn_own.reshape(each, owners, rows_own, padded)[:, :, :vec_lines, width:]
    vec_oth = partner(vec_own)
    attn_oth = partner(attn_own)

    def vec_rows(lines):
        lines = lines.reshape(each, owners, vec_lines * spare)[:, :, :vec_count]
        lines = lines.reshape(each, owners, *vec_shape).transpose(0, 2, 1, 3)
        return lines.reshape(each, vec_shape[0], width).astype(f32)

    vec = jnp.stack([vec_rows(vec_own), vec_rows(vec_oth)], 1).reshape(cols, -1, width)
    vec = by_place(vec).reshape(-1, width)

    def widen(row):
        return jnp.pad(row, (0, spare))

    inputs = hidden_in.astype(f32)
    normed_one, scaled_one, inverse_one = normalize(inputs, vec[0], vec[1])
    normed_low = normed_one.astype(bf16)
    if staged:
        normed_low, up_one = together(normed_low, up_one)
        up_two = spread_two(up_one)
    bias = jnp.concatenate([widen(vec[2]), jnp.zeros((padded,), f32), widen(vec[3])]).reshape(1, -1)
    spans = tuple((part * piece, part * padded) for part in range(3))
    projected = None
    for places, weights in ((places_own, attn_own), (places_oth, attn_oth)):
        if staged and projected is not None:
            projected, down_rows = together(projected, down_rows)
        projected = multiply_and_place(
            places, normed_low, [weights], lanes_qkv, 0, spans, piece, 3 * padded, bias, projected
        )
    if staged:
        projected, down_one = together(projected, spread_one(down_rows))
        down_two = spread_two(down_one)
    ahead = [(c, c + 1) for c in range(cols - 1) if c % halves + 1 < halves]
    behind = [(b, a) for a, b in ahead]
    others = lax.ppermute(projected[:, padded:], "col", ahead)

    own_half = lax.dynamic_slice_in_dim(segments.reshape(-1), column * here, here, 0)
    first_half = lax.dynamic_slice_in_dim(
        segments.reshape(-1), (column - lax.rem(column, halves)) * here, here, 0
    )
    labels = (own_half.reshape(1, here), own_half.reshape(here, 1), first_half.reshape(here, 1))
    mixed, log_totals = attend(later, labels, projected, others)
    if staged:
        mixed, up_two = together(mixed, up_two)
        up_own = assemble(up_two)
    up_oth = partner(up_own)
    mixed_shape = jax.ShapeDtypeStruct((each, here, lanes_out), bf16)
    lead = 3 * piece - lead_out
    mixed_own, mixed_oth = split_call(
        functools.partial(split_mixed_kernel, piece, cols, lead),
        column_word,
        [mixed],
        [mixed_shape] * 2,
        "split_mixed",
    )
    residual = inputs + vec[4]
    for blocks, weights in ((mixed_own, attn_own), (mixed_oth, attn_oth)):
        for i in range(each):
            residual = residual + contract_last(blocks[i], weights[i][:, lead_out:])
    normed_two, scaled_two, inverse_two = normalize(residual, vec[5], vec[6])
    normed_two_low = normed_two.astype(bf16)

    bias_up = by_place(vec[8:])
    bias_own, bias_oth = bias_up[0::2], bias_up[1::2]

    def up_part(ups, biases):
        return [
            jnp.dot(normed_two_low, ups[i], preferred_element_type=f32) + biases[i]
            for i in range(each)
        ]

    linear_own = up_part(up_own, bias_own)
    if staged:
        linear_own, down_two = together(linear_own, down_two)
        down_own = assemble(down_two)
    down_oth = partner(down_own)
    linear_oth = up_part(up_oth, bias_oth)

    branch = jnp.zeros((here, width), f32)

    def forward_part(linears, downs, branch):
        lows, pullbacks = [], []
        for i in range(each):
            active, pullback = jax.vjp(gelu_tanh, linears[i])
            lows.append(active.astype(bf16))
            pullbacks.append(pullback)
            branch = branch + contract_last(lows[i], downs[i])
        return lows, pullbacks, branch

    left_down, left_up = cotangent.T, normed_two_low.T

    def turned(rights):
        return [r.T for r in rights]

    lows_oth, pull_oth, branch = forward_part(linear_oth, down_oth, branch)
    sent_down = block_grads([(left_down, turned(lows_oth))], None, None, False)
    linear_own, sent_down = together(linear_own, sent_down)
    received_down = partner(sent_down)
    lows_own, pull_own, branch = forward_part(linear_own, down_own, branch)
    total_down = block_grads([(left_down, turned(lows_own))], None, received_down, staged)
    layer_out = (residual + branch + vec[7]).astype(bf16)
    down_oth, total_down = together(down_oth, total_down)
    grad_normed_two = jnp.zeros((here, width), f32)

    def backward_part(ups, downs, pullbacks, grad_normed_two):
        lows, sums = [], []
        for i in range(each):
            grad_active = jnp.dot(cotangent, downs[i], preferred_element_type=f32)
            grad_linear = pullbacks[i](grad_active)[0]
            lows.append(grad_linear.astype(bf16))
            sums.append(jnp.sum(grad_linear, 0))
            grad_normed_two = grad_normed_two + contract_last(lows[i], ups[i])
        return lows, sums, grad_normed_two

    dups_oth, dbias_oth, grad_normed_two = backward_part(
        up_oth, down_oth, pull_oth, grad_normed_two
    )
    one_down = scatter_one(total_down)
    sent_up = block_grads([(left_up, turned(dups_oth))], None, None, False)
    down_own, one_down, sent_up = together(down_own, one_down, sent_up)
    received_up = partner(sent_up)
    two_down = scatter_two(one_down)
    dups_own, dbias_own, grad_normed_two = backward_part(
        up_own, down_own, pull_own, grad_normed_two
    )

    grad_residual = cotangent.astype(f32) + norm_back(
        grad_normed_two, scaled_two, inverse_two, vec[5]
    )
    grad_residual_low = grad_residual.astype(bf16)
    grad_mixed = multiply_and_place(
        jnp.concatenate([places_own, places_oth]),
        grad_residual_low,
        [attn_own, attn_oth],
        lanes_out,
        lead_out // lanes_out,
        ((lead, 0),),
        piece,
        padded,
        None,
        None,
    )
    total_up = block_grads([(left_up, turned(dups_own))], None, received_up, staged)
    grad_mixed, total_up, two_down = together(grad_mixed, total_up, two_down)
    dq, dk_own, dv_own, dk_oth, dv_oth = attend_back(
        later, labels, projected, others, grad_mixed, mixed, log_totals
    )
    back = lax.ppermute(jnp.concatenate([dk_oth, dv_oth], 1), "col", behind)
    one_up = scatter_one(total_up)
    dq, dk_own, dv_own, one_up = together(dq, dk_own, dv_own, one_up)
    grads_shape = jax.ShapeDtypeStruct((each, here, lanes_qkv), bf16)
    grads_own, grads_oth, grad_sums = split_call(
        functools.partial(split_grads_kernel, piece, cols),
        column_word,
        [dq, dk_own, dv_own, back],
        [grads_shape, grads_shape, jax.ShapeDtypeStruct((8, padded), f32)],
        "split_grads",
    )
    two_up = scatter_two(one_up)
    left_one, left_two = normed_low.T, grad_residual_low.T
    pairs_oth = [(left_one, grads_oth), (left_two, mixed_oth)]
    pairs_own = [(left_one, grads_own), (left_two, mixed_own)]
    received = partner(block_grads(pairs_oth, None, None, False))
    grad_normed_one = jnp.zeros((here, width), f32)
    for blocks, weights in ((grads_own, attn_own), (grads_oth, attn_oth)):
        for i in range(each):
            grad_normed_one = grad_normed_one + contract_last(blocks[i], weights[i][:, :lanes_qkv])
    input_grad = grad_residual + norm_back(grad_normed_one, scaled_one, inverse_one, vec[0])

    dbias = jnp.stack([jnp.stack(dbias_own), jnp.stack(dbias_oth)], 1).reshape(cols, width)
    grad_vector = jnp.concatenate(
        [
            jnp.stack(
                [
                    jnp.sum(grad_normed_one * scaled_one, 0),
                    jnp.sum(grad_normed_one, 0),
                    grad_sums[0, :width],
                    grad_sums[1, :width],
                    jnp.sum(grad_residual, 0),
                    jnp.sum(grad_normed_two * scaled_two, 0),
                    jnp.sum(grad_normed_two, 0),
                    jnp.sum(cotangent.astype(f32), 0),
                ]
            ),
            by_place(dbias),
        ],
        0,
    ).astype(bf16)
    vec_part = grad_vector.reshape(cols, vec_shape[0], owners, vec_shape[1]).transpose(0, 2, 1, 3)
    vec_part = jnp.pad(vec_part.reshape(cols, owners, vec_count), ((0, 0), (0, 0), (0, vec_fill)))
    vec_part = by_place(vec_part.reshape(cols, owners, vec_lines, spare))
    vec_here = (vec_part[0::2].astype(f32) + partner(vec_part[1::2]).astype(f32)).astype(bf16)
    vec_here = jnp.pad(
        vec_here, ((0, 0), (0, 0), (0, rows_own - vec_lines), (LANES - spare, 0))
    ).reshape(each, width, LANES)
    total_attn = block_grads(pairs_own, vec_here, received, staged)
    sum_down, sum_up = scatter_three(two_down), scatter_three(two_up)
    sum_attn = scatter_three(scatter_two(scatter_one(total_attn)))
    sum_qkv = sum_attn[:, : 3 * piece].reshape(rows_own, 3, piece)
    sum_out = sum_attn[:, 3 * piece : width].T
    sum_vector = sum_attn[:vec_lines, width:].reshape(-1)[:vec_count].reshape(vec_shape)

    qkv_m, qkv_v, qkv_w = adamw(
        qkv_weight, sum_qkv, qkv_first, qkv_second, 1.5 * D ** (-0.5), decay_rate
    )
    out_m, out_v, out_w = adamw(
        out_weight, sum_out, out_first, out_second, 1.5 * (D // 64) ** (-0.5), decay_rate
    )
    up_m, up_v, up_w = adamw(up_weight, sum_up, up_first, up_second, 1.5 * D ** (-0.5), decay_rate)
    down_m, down_v, down_w = adamw(
        down_weight, sum_down.T, down_first, down_second, 1.5 * FF ** (-0.5), decay_rate
    )
    vec_m, vec_v, vec_w = adamw(vectors, sum_vector, vectors_first, vectors_second, 0.5, 0.0)
    return (
        layer_out,
        input_grad,
        qkv_m,
        qkv_v,
        qkv_w,
        out_m,
        out_v,
        out_w,
        up_m,
        up_v,
        up_w,
        down_m,
        down_v,
        down_w,
        vec_m,
        vec_v,
        vec_w,
    )


def solution(mesh):
    tokens = P(("dp", "row", "col"), None)
    qkv = P(("dp", "row"), None, "col")
    tall = P("col", ("dp", "row"))
    up = P(("dp", "row"), "col")
    state = (qkv, tall, up, tall, tall)
    return jax.shard_map(
        local,
        mesh=mesh,
        in_specs=(tokens, tokens, P(("dp", "row"), None)) + state * 3,
        out_specs=(tokens, tokens)
        + (qkv,) * 3
        + (tall,) * 3
        + (up,) * 3
        + (tall,) * 3
        + (tall,) * 3,
        check_vma=False,
    )
```

```python
import functools

import jax
import jax.numpy as jnp
from jax import lax
from jax.experimental import pallas as pl
from jax.experimental.pallas import tpu as pltpu
from jax.sharding import PartitionSpec as P

D = 1088
HEAD_DIM = 64
FF = 4352
SEQ = 1024
STEP = 5

LANES = 128


beta_one = 0.9
beta_two = 0.999
epsilon = 1e-08
decay_rate = 0.1
masked_score = -1000000000.0

f32 = jnp.float32
bf16 = jnp.bfloat16


def contract(left, right, left_dim, right_dim):
    return lax.dot_general(
        left, right, (((left_dim,), (right_dim,)), ((), ())), preferred_element_type=f32
    )


def contract_first(left, right):
    return contract(left, right, 0, 0)


def contract_last(left, right):
    return contract(left, right, 1, 1)


def normalize(rows, gain, shift):
    row_mean = jnp.mean(rows, -1, keepdims=True)
    centred = rows - row_mean
    inverse = lax.rsqrt(jnp.mean(centred * centred, -1, keepdims=True) + 1e-05)
    scaled = centred * inverse
    return (scaled * gain + shift, scaled, inverse)


def norm_back(grad_out, scaled, inverse, gain):
    grad_scaled = grad_out * gain
    return inverse * (
        grad_scaled
        - jnp.mean(grad_scaled, -1, keepdims=True)
        - scaled * jnp.mean(grad_scaled * scaled, -1, keepdims=True)
    )


def gelu_tanh(values):
    return jax.nn.gelu(values, approximate=True)


def adamw(weight, gradient, moment_one, moment_two, step_rate, shrink):
    moment_one = beta_one * moment_one + (1.0 - beta_one) * gradient
    moment_two = beta_two * moment_two + (1.0 - beta_two) * gradient * gradient
    update = (
        moment_one
        / (1.0 - beta_one**STEP)
        / (jnp.sqrt(moment_two / (1.0 - beta_two**STEP)) + epsilon)
    )
    return (moment_one, moment_two, weight - step_rate * (update + shrink * weight))


def mask_tables(kseg_own, kseg_oth, qseg, bias_own, bias_oth):
    count = bias_own.shape[0]
    key_place = lax.broadcasted_iota(jnp.int32, (count, count), 0)
    query_place = lax.broadcasted_iota(jnp.int32, (count, count), 1)
    same = kseg_own[...] == qseg[...]
    bias_own[...] = jnp.where(same & (key_place <= query_place), 0.0, masked_score)
    bias_oth[...] = jnp.where(kseg_oth[...] == qseg[...], 0.0, masked_score)


def head_lanes(block, half):
    lane = lax.broadcasted_iota(jnp.int32, block.shape, 1)
    return jnp.where((lane // HEAD_DIM) == half, block, jnp.zeros_like(block))


def attention_forward(
    later, qseg, kseg_own, kseg_oth, q, k_own, v_own, k_oth, v_oth, out, lse, bias_own, bias_oth
):
    pair = pl.program_id(0)
    count = q.shape[0]
    step = count // 2

    @pl.when(pair == 0)
    def _():
        mask_tables(kseg_own, kseg_oth, qseg, bias_own, bias_oth)

    def body(with_other):
        queries = q[...] * jnp.asarray(HEAD_DIM**-0.5, bf16)
        values_own = v_own[...].astype(f32).T.astype(bf16)
        values_oth = v_oth[...].astype(f32).T.astype(bf16) if with_other else None
        for part in range(2):
            cols = slice(part * step, (part + 1) * step)
            seen = (part + 1) * step
            pieces = []
            for half in range(2):
                q_head = head_lanes(queries[cols], half)
                rows = slice(half * HEAD_DIM, (half + 1) * HEAD_DIM)
                s_own = contract_last(k_own[:seen], q_head) + bias_own[:seen, cols]
                top = jnp.max(s_own, 0, keepdims=True)
                if with_other:
                    s_oth = contract_last(k_oth[...], q_head) + bias_oth[:, cols]
                    top = jnp.maximum(top, jnp.max(s_oth, 0, keepdims=True))
                e_own = jnp.exp(s_own - top)
                total = jnp.sum(e_own, 0, keepdims=True)
                mixed = jnp.dot(
                    values_own[rows, :seen], e_own.astype(bf16), preferred_element_type=f32
                )
                if with_other:
                    e_oth = jnp.exp(s_oth - top)
                    total = total + jnp.sum(e_oth, 0, keepdims=True)
                    mixed = mixed + jnp.dot(
                        values_oth[rows], e_oth.astype(bf16), preferred_element_type=f32
                    )
                lse[0, half : half + 1, cols] = top + jnp.log(total)
                pieces.append(mixed / total)
            out[cols] = jnp.concatenate(pieces, 0).T.astype(bf16)

    @pl.when(later[0] == 1)
    def _():
        body(True)

    @pl.when(later[0] == 0)
    def _():
        body(False)


def attention_backward(
    later, qseg, kseg_own, kseg_oth, q, k_own, v_own, k_oth, v_oth, grad, out, lse,
    dq, dk_own, dv_own, dk_oth, dv_oth, bias_own, bias_oth,
):
    pair = pl.program_id(0)
    count = q.shape[0]
    step = count // 2

    @pl.when(pair == 0)
    def _():
        mask_tables(kseg_own, kseg_oth, qseg, bias_own, bias_oth)

    def body(with_other):
        scale = jnp.asarray(HEAD_DIM**-0.5, bf16)
        queries = q[...] * scale
        keys_own = k_own[...].astype(f32).T.astype(bf16)
        keys_oth = k_oth[...].astype(f32).T.astype(bf16) if with_other else None
        products = (grad[...].astype(f32) * out[...].astype(f32)).T
        dk_a = [jnp.zeros((step, LANES), f32) for _ in range(2)]
        dv_a = [jnp.zeros((step, LANES), f32) for _ in range(2)]
        dk_b = jnp.zeros((count, LANES), f32)
        dv_b = jnp.zeros((count, LANES), f32)
        for part in range(2):
            cols = slice(part * step, (part + 1) * step)
            pieces = []
            for half in range(2):
                q_head = head_lanes(queries[cols], half)
                g_head = head_lanes(grad[cols], half)
                rows = slice(half * HEAD_DIM, (half + 1) * HEAD_DIM)
                delta = jnp.sum(products[rows, cols], 0, keepdims=True)
                log_total = lse[0, half : half + 1, cols]

                def block(keys, values, bias):
                    probs = jnp.exp(contract_last(keys, q_head) + bias - log_total)
                    d_probs = contract_last(values, g_head)
                    d_scores = (probs * (d_probs - delta)).astype(bf16)
                    dk = jnp.dot(d_scores, q_head, preferred_element_type=f32)
                    dv = jnp.dot(probs.astype(bf16), g_head, preferred_element_type=f32)
                    return (d_scores, dk, dv)

                d_query = jnp.zeros((HEAD_DIM, step), f32)
                for chunk in range(part + 1):
                    span = slice(chunk * step, (chunk + 1) * step)
                    d_scores, dk, dv = block(k_own[span], v_own[span], bias_own[span, cols])
                    dk_a[chunk] = dk_a[chunk] + dk
                    dv_a[chunk] = dv_a[chunk] + dv
                    d_query = d_query + jnp.dot(
                        keys_own[rows, span], d_scores, preferred_element_type=f32
                    )
                if with_other:
                    d_scores, dk, dv = block(k_oth[...], v_oth[...], bias_oth[:, cols])
                    dk_b = dk_b + dk
                    dv_b = dv_b + dv
                    d_query = d_query + jnp.dot(
                        keys_oth[rows], d_scores, preferred_element_type=f32
                    )
                pieces.append(d_query)
            dq[cols] = (jnp.concatenate(pieces, 0).T * HEAD_DIM**-0.5).astype(bf16)
        for chunk in range(2):
            span = slice(chunk * step, (chunk + 1) * step)
            dk_own[span] = dk_a[chunk].astype(bf16)
            dv_own[span] = dv_a[chunk].astype(bf16)
        dk_oth[...] = dk_b.astype(bf16)
        dv_oth[...] = dv_b.astype(bf16)

    @pl.when(later[0] == 1)
    def _():
        body(True)

    @pl.when(later[0] == 0)
    def _():
        body(False)


def attention_specs(count, pairs):
    def whole(shape):
        return pl.BlockSpec(shape, lambda p, later: (0,) * len(shape))

    def lanes(start):
        return pl.BlockSpec((count, LANES), lambda p, later: (0, start + p))

    segments = [whole((1, count)), whole((count, 1)), whole((count, 1))]
    projected = [lanes(0), lanes(pairs), lanes(2 * pairs), lanes(0), lanes(pairs)]
    totals = pl.BlockSpec((1, 2, count), lambda p, later: (p, 0, 0))
    return segments, projected, lanes(0), totals


def attend(later, labels, projected, others):
    count = projected.shape[0]
    pairs = projected.shape[1] // (3 * LANES)
    segments, blocks, wide, totals = attention_specs(count, pairs)
    work = count * count * LANES * pairs * 2
    return pl.pallas_call(
        attention_forward,
        grid_spec=pltpu.PrefetchScalarGridSpec(
            num_scalar_prefetch=1,
            grid=(pairs,),
            in_specs=segments + blocks,
            out_specs=[wide, totals],
            scratch_shapes=[pltpu.VMEM((count, count), f32), pltpu.VMEM((count, count), f32)],
        ),
        out_shape=[
            jax.ShapeDtypeStruct((count, pairs * LANES), bf16),
            jax.ShapeDtypeStruct((pairs, 2, count), f32),
        ],
        compiler_params=pltpu.CompilerParams(vmem_limit_bytes=48 << 20),
        name="attention_forward",
    )(later, *labels, projected, projected, projected, others, others)


def attend_back(later, labels, projected, others, grad, mixed, log_totals):
    count = projected.shape[0]
    pairs = projected.shape[1] // (3 * LANES)
    segments, blocks, wide, totals = attention_specs(count, pairs)
    work = count * count * LANES * pairs * 2
    return pl.pallas_call(
        attention_backward,
        grid_spec=pltpu.PrefetchScalarGridSpec(
            num_scalar_prefetch=1,
            grid=(pairs,),
            in_specs=segments + blocks + [wide, wide, totals],
            out_specs=[wide] * 5,
            scratch_shapes=[pltpu.VMEM((count, count), f32), pltpu.VMEM((count, count), f32)],
        ),
        out_shape=[jax.ShapeDtypeStruct((count, pairs * LANES), bf16)] * 5,
        compiler_params=pltpu.CompilerParams(vmem_limit_bytes=48 << 20),
        name="attention_backward",
    )(later, *labels, projected, projected, projected, others, others, grad, mixed, log_totals)


def place_kernel(spans, piece, sources, biased, continued, places, x, *refs):
    weights, refs = refs[:sources], refs[sources:]
    bias, refs = (refs[0], refs[1:]) if biased else (None, refs)
    before, refs = (refs[0], refs[1:]) if continued else (None, refs)
    out, whole, product = refs
    step = pl.program_id(0)
    each = pl.num_programs(0) // sources

    @pl.when(step == 0)
    def _():
        whole[...] = before[...].astype(f32) if continued else jnp.zeros_like(whole)

    for k, weight in enumerate(weights):

        @pl.when(step // each == k)
        def _(weight=weight):
            product[...] = jnp.dot(x[...], weight[0], preferred_element_type=f32)

    for place in range(x.shape[1] // piece):

        @pl.when(places[step] == place)
        def _(place=place):
            for source, target in spans:
                start = target + place * piece
                block = product[:, source : source + piece]
                if biased:
                    block = block + bias[:, start : start + piece]
                whole[:, start : start + piece] = block

    @pl.when(step == pl.num_programs(0) - 1)
    def _():
        out[...] = whole[...].astype(bf16)


def multiply_and_place(places, x, weights, lanes, lane_block, spans, piece, out_lanes, bias, before):
    count, depth = x.shape
    each = weights[0].shape[0]
    sources = len(weights)

    def fixed(shape):
        return pl.BlockSpec(shape, lambda j, places: (0, 0))

    in_specs = [fixed((count, depth))]
    for k in range(sources):
        in_specs.append(
            pl.BlockSpec(
                (1, depth, lanes),
                lambda j, places, k=k: (jnp.clip(j - k * each, 0, each - 1), 0, lane_block),
            )
        )
    operands = [x, *weights]
    if bias is not None:
        in_specs.append(fixed(bias.shape))
        operands.append(bias)
    if before is not None:
        in_specs.append(fixed(before.shape))
        operands.append(before)
    return pl.pallas_call(
        functools.partial(
            place_kernel, spans, piece, sources, bias is not None, before is not None
        ),
        grid_spec=pltpu.PrefetchScalarGridSpec(
            num_scalar_prefetch=1,
            grid=(each * sources,),
            in_specs=in_specs,
            out_specs=fixed((count, out_lanes)),
            scratch_shapes=[pltpu.VMEM((count, out_lanes), f32), pltpu.VMEM((count, lanes), f32)],
        ),
        out_shape=jax.ShapeDtypeStruct((count, out_lanes), bf16),
        compiler_params=pltpu.CompilerParams(vmem_limit_bytes=48 << 20),
        name="multiply_and_place",
    )(places, *operands)


def split_all(column, cols, write):
    for here in range(cols):

        @pl.when(column[0] == here)
        def _(here=here):
            for k in range(cols):
                write(k % 2, k // 2, here ^ k)


def split_mixed_kernel(piece, cols, lead, column, mixed, own, oth):
    count, lanes = own.shape[1:]
    values = mixed[...].astype(f32)
    before = jnp.zeros((count, lead), f32)
    after = jnp.zeros((count, lanes - lead - piece), f32)

    def write(which, i, c):
        block = values[:, c * piece : (c + 1) * piece]
        (own, oth)[which][i] = jnp.concatenate([before, block, after], 1).astype(bf16)

    split_all(column, cols, write)


def split_grads_kernel(piece, cols, column, dq, dk, dv, back, own, oth, sums):
    count, lanes = own.shape[1:]
    wide = dq.shape[1]
    grads = [
        dq[...].astype(f32),
        dk[...].astype(f32) + back[:, :wide].astype(f32),
        dv[...].astype(f32) + back[:, wide:].astype(f32),
    ]
    sums[0:1] = jnp.sum(grads[0], 0, keepdims=True)
    sums[1:2] = jnp.sum(grads[2], 0, keepdims=True)
    after = jnp.zeros((count, lanes - 3 * piece), f32)

    def write(which, i, c):
        blocks = [g[:, c * piece : (c + 1) * piece] for g in grads]
        (own, oth)[which][i] = jnp.concatenate([*blocks, after], 1).astype(bf16)

    split_all(column, cols, write)


def whole_specs(shapes):
    return [pl.BlockSpec(s, lambda i, p, n=len(s): (0,) * n) for s in shapes]


def split_call(kernel, column, operands, out_shapes, name):
    moved = sum(x.size * x.dtype.itemsize for x in operands) * 2
    return pl.pallas_call(
        kernel,
        grid_spec=pltpu.PrefetchScalarGridSpec(
            num_scalar_prefetch=1,
            grid=(1,),
            in_specs=whole_specs([x.shape for x in operands]),
            out_specs=whole_specs([s.shape for s in out_shapes]),
        ),
        out_shape=out_shapes,
        compiler_params=pltpu.CompilerParams(vmem_limit_bytes=48 << 20),
        name=name,
    )(column, *operands)


def block_grads_kernel(counts, has_vec, has_received, split, place, *refs):
    refs = list(refs)
    step = pl.program_id(0)
    lefts = [refs.pop(0) for _ in counts]
    rights = [[refs.pop(0) for _ in range(count)] for count in counts]
    vec_part = refs.pop(0) if has_vec else None
    received = refs.pop(0) if has_received else None
    width = lefts[0].shape[0]
    quarter = width // 4

    def value(start):
        rows = pl.ds(start, quarter)
        if len(counts) == 1:
            whole = jnp.dot(lefts[0][rows], rights[0][0][0], preferred_element_type=f32)
        else:
            one, two = [
                jnp.dot(left[rows], right[0][0], preferred_element_type=f32)
                for left, right in zip(lefts, rights)
            ]
            lead = one.shape[1] - LANES
            whole = jnp.concatenate(
                [one[:, :lead], one[:, lead:] + two[:, :LANES], two[:, LANES:]], 1
            )
        if has_vec:
            more = whole[:, -LANES:] + vec_part[0, rows].astype(f32)
            whole = jnp.concatenate([whole[:, :-LANES], more], 1)
        if has_received:
            whole = whole + received[0, rows].astype(f32)
        return whole.astype(bf16)

    for i in range(2):

        @pl.when(step == i)
        def _(i=i):
            if not split:
                for k in range(4):
                    refs[0][0, k * quarter : (k + 1) * quarter] = value(k * quarter)
                return
            first_keep, first_send, second_keep, second_send = refs
            half = width // 2
            first_keep[0] = value(pl.multiple_of(place[0] * half, 16))
            first_send[0] = value(pl.multiple_of((1 - place[0]) * half, 16))
            second = (second_keep, second_send)[i]
            for dp in range(2):
                second[dp] = value(dp * half + quarter)


def block_grads(pairs, vec_part, received, split):
    lefts, rights = zip(*pairs)
    rights = [r if isinstance(r, list) else [r] for r in rights]
    width, count = lefts[0].shape
    each = 2
    lanes = width if len(pairs) == 1 else -(-width // LANES) * LANES
    place = lax.axis_index("dp").reshape(1).astype(jnp.int32)

    def fixed(shape):
        return pl.BlockSpec(shape, lambda i, place: (0,) * len(shape))

    def step(shape):
        return pl.BlockSpec((1, *shape[1:]), lambda i, place: (i, 0, 0))

    flat = [r for right in rights for r in right]
    more = [x for x in (vec_part, received) if x is not None]
    in_specs = [fixed(x.shape) for x in lefts]
    in_specs += [step(x.shape) if x.ndim == 3 else fixed(x.shape) for x in flat]
    in_specs += [step(x.shape) for x in more]
    if split:
        part = (each, width // 4, lanes)
        out_specs = [step(part), step(part), fixed(part), fixed(part)]
        out_shape = [jax.ShapeDtypeStruct(part, bf16)] * 4
    else:
        out_specs = step((each, width, lanes))
        out_shape = jax.ShapeDtypeStruct((each, width, lanes), bf16)
    return pl.pallas_call(
        functools.partial(
            block_grads_kernel,
            [len(r) for r in rights],
            vec_part is not None,
            received is not None,
            split,
        ),
        grid_spec=pltpu.PrefetchScalarGridSpec(
            num_scalar_prefetch=1,
            grid=(each,),
            in_specs=in_specs,
            out_specs=out_specs,
        ),
        out_shape=out_shape,
        compiler_params=pltpu.CompilerParams(vmem_limit_bytes=48 << 20),
        name="block_grads",
    )(place, *lefts, *flat, *more)


def gelu_parts(values):
    scale = (2.0 / jnp.pi) ** 0.5
    square = values * values
    return jnp.tanh(scale * values * (1.0 + 0.044715 * square)), scale * (
        1.0 + (3.0 * 0.044715) * square
    )


def feed_forward_kernel(continued, x, up, bias, down, *refs):
    before, refs = (refs[0], refs[1:]) if continued else (None, refs)
    linear, active, branch = refs
    count = x.shape[0]

    @pl.when(pl.program_id(0) == 0)
    def _():
        branch[...] = before[...] if continued else jnp.zeros_like(branch)

    for k in range(2):
        rows = slice(k * count // 2, (k + 1) * count // 2)
        values = jnp.dot(x[rows], up[0], preferred_element_type=f32) + bias[0]
        linear[0, rows] = values
        low = (0.5 * values * (1.0 + gelu_parts(values)[0])).astype(bf16)
        active[0, rows] = low
        branch[rows] += contract_last(low, down[0])


def feed_backward_kernel(continued, grad, up, down, linear, *refs):
    before, refs = (refs[0], refs[1:]) if continued else (None, refs)
    lows, sums, grad_in = refs
    count = grad.shape[0]

    @pl.when(pl.program_id(0) == 0)
    def _():
        grad_in[...] = before[...] if continued else jnp.zeros_like(grad_in)

    sums[...] = jnp.zeros_like(sums)
    for k in range(2):
        rows = slice(k * count // 2, (k + 1) * count // 2)
        values = linear[0, rows]
        tanh, slope = gelu_parts(values)
        derivative = 0.5 * (1.0 + tanh) + 0.5 * values * (1.0 - tanh * tanh) * slope
        grads = jnp.dot(grad[rows], down[0], preferred_element_type=f32) * derivative
        sums[0] += jnp.sum(grads, 0, keepdims=True)
        low = grads.astype(bf16)
        lows[0, rows] = low
        grad_in[rows] += contract_last(low, up[0])


def feed_call(kernel, fixed, stepped, before, out_stepped, out_fixed, name):
    each = stepped[0].shape[0]

    def whole(x):
        return pl.BlockSpec(x.shape, lambda i: (0,) * len(x.shape))

    def step(x):
        return pl.BlockSpec((1, *x.shape[1:]), lambda i: (i, 0, 0))

    operands = [fixed, *stepped]
    in_specs = [whole(fixed)] + [step(x) for x in stepped]
    if before is not None:
        operands.append(before)
        in_specs.append(whole(before))
    return pl.pallas_call(
        functools.partial(kernel, before is not None),
        grid=(each,),
        in_specs=in_specs,
        out_specs=[step(x) for x in out_stepped] + [whole(out_fixed)],
        out_shape=[*out_stepped, out_fixed],
        compiler_params=pltpu.CompilerParams(vmem_limit_bytes=56 << 20),
        name=name,
    )(*operands)


AXES = ("col", "dp", "row")


def planes():
    owners = lax.axis_size("dp") * lax.axis_size("row")
    cols = lax.axis_size("col")
    return [
        [c * owners + k for c in range(p, cols, 2) for k in range(owners)] for p in range(2)
    ]


def flip_col(block, bit):
    return lax.ppermute(block, "col", [(c, c ^ bit) for c in range(lax.axis_size("col"))])


def partner(block):
    return flip_col(block, 1)


def flip_dp(block):
    return lax.ppermute(block, "dp", [(0, 1), (1, 0)])


def shift_row(block, by):
    count = lax.axis_size("row")
    return lax.ppermute(block, "row", [(i, (i + by) % count) for i in range(count)])


def by_place(blocks):
    column = lax.axis_index("col")
    pairs = blocks.reshape(-1, 2, *blocks.shape[1:])
    pairs = jnp.where(column % 2 == 1, pairs[:, ::-1], pairs)
    return upper_bit(pairs).reshape(blocks.shape)


def upper_bit(blocks):
    return jnp.where(lax.axis_index("col") // 2 == 1, blocks[::-1], blocks)


def short_rows():
    return lax.axis_size("row") == 4 and lax.axis_size("dp") == 2 and lax.axis_size("col") == 4


def assemble_kernel(place, *refs):
    sources, (out, held, sems_in, sems_out) = refs[:-4], refs[-4:]
    dp, row = place[0], place[1]
    order = (
        [(0, 0, 0), (0, 0, 1), (1, 0, 0), (1, 0, 1), (0, 0, 2), (0, 0, 3), (0, 1, 2), (0, 1, 3)]
        + [(0, 1, 0), (0, 1, 1), (1, 1, 0), (1, 1, 1)]
        + [(1, 0, 2), (1, 0, 3), (1, 1, 2), (1, 1, 3)]
    )
    blocks = [source.at[i] for source in sources for i in range(source.shape[0])]
    copies_in, copies_out = [], []
    for k, (block, (over_x, over_y, behind)) in enumerate(zip(blocks, order)):
        target = over_x * 8 + (1 - dp if over_y else dp) * 4 + lax.rem(row + 4 - behind, 4)
        copies_in.append(pltpu.make_async_copy(block, held.at[k], sems_in.at[k]))
        copies_out.append(pltpu.make_async_copy(held.at[k], out.at[target], sems_out.at[k]))
    for copy in copies_in:
        copy.start()
    for copy_in, copy_out in zip(copies_in, copies_out):
        copy_in.wait()
        copy_out.start()
    for copy in copies_out:
        copy.wait()


def assemble(pieces):
    rows, lanes = pieces[0].shape[-2:]
    pieces = [p.reshape(-1, rows, lanes) for p in pieces]
    place = jnp.stack([lax.axis_index("dp"), lax.axis_index("row")]).astype(jnp.int32)
    anywhere = pl.BlockSpec(memory_space=pl.ANY)
    out = pl.pallas_call(
        assemble_kernel,
        grid_spec=pltpu.PrefetchScalarGridSpec(
            num_scalar_prefetch=1,
            grid=(1,),
            in_specs=[anywhere] * len(pieces),
            out_specs=anywhere,
            scratch_shapes=[
                pltpu.VMEM((16, rows, lanes), bf16),
                pltpu.SemaphoreType.DMA((16,)),
                pltpu.SemaphoreType.DMA((16,)),
            ],
        ),
        out_shape=jax.ShapeDtypeStruct((16, rows, lanes), bf16),
        compiler_params=pltpu.CompilerParams(vmem_limit_bytes=48 << 20),
        name="assemble",
    )(place, *pieces)
    return out.reshape(2, -1, lanes)


def spread_rows(block):
    return [block] + [shift_row(block, m) for m in range(1, 4)]


def spread_one(pieces):
    first, second = jnp.stack(pieces[:2]), jnp.stack(pieces[2:])
    return [first, flip_col(first, 2), second, flip_dp(second)]


def spread_two(pieces):
    first_y = flip_dp(jnp.stack(pieces[:2]))
    return [*pieces, first_y, flip_col(jnp.stack(pieces[2:]), 2)]


def gather_groups(block):
    whole = lax.all_gather(block, AXES, axis=0, tiled=False, axis_index_groups=planes())
    return upper_bit(whole.reshape(lax.axis_size("col") // 2, -1, block.shape[-1]))


def together(*arrays):
    return lax.optimization_barrier(arrays)


def added(one, other):
    return (one.astype(f32) + other.astype(f32)).astype(bf16)


def at_place(array, which, axis):
    return lax.dynamic_index_in_dim(array, which, axis, keepdims=False)


def scatter_one(blocks):
    if not short_rows():
        return blocks
    first_keep, first_send, second_keep, second_send = blocks
    first_y, second_x = flip_dp(first_send), flip_col(second_send, 2)
    return added(first_keep, first_y), added(second_keep, second_x)


def scatter_two(halves):
    if not short_rows():
        return halves
    dp = lax.axis_index("dp")
    first, second = halves
    first_x = flip_col(first[1], 2)
    second_y = flip_dp(at_place(second, 1 - dp, 0))
    both = jnp.concatenate(
        [added(first[0], first_x), added(at_place(second, dp, 0), second_y)], 0
    )
    return both.reshape(4, -1, both.shape[-1])


def scatter_three(rows):
    if not short_rows():
        flat = upper_bit(rows).reshape(-1, rows.shape[-1])
        return lax.psum_scatter(
            flat, AXES, scatter_dimension=0, tiled=True, axis_index_groups=planes()
        ).astype(f32)
    row = lax.axis_index("row")
    total = at_place(rows, row, 0).astype(f32)
    for m in range(1, 4):
        total = total + shift_row(at_place(rows, (row + m) % 4, 0), m).astype(f32)
    return total


def local(
    hidden_in,
    cotangent,
    segments,
    qkv_weight,
    out_weight,
    up_weight,
    down_weight,
    vectors,
    qkv_first,
    out_first,
    up_first,
    down_first,
    vectors_first,
    qkv_second,
    out_second,
    up_second,
    down_second,
    vectors_second,
):
    column = lax.axis_index("col")
    cols = lax.axis_size("col")
    here, width = hidden_in.shape
    rows_own = qkv_weight.shape[0]
    owners = lax.axis_size("dp") * lax.axis_size("row")
    piece = qkv_weight.shape[2]
    halves = SEQ // here
    each = cols // 2
    column_word = column.reshape(1).astype(jnp.int32)
    places_own = (column ^ (2 * jnp.arange(each))).astype(jnp.int32)
    places_oth = (column ^ (2 * jnp.arange(each) + 1)).astype(jnp.int32)
    later = lax.rem(column, halves).reshape(1).astype(jnp.int32)
    padded = -(-width // LANES) * LANES
    spare = padded - width
    lanes_qkv = -(-3 * piece // LANES) * LANES
    lead_out = 3 * piece // LANES * LANES
    lanes_out = padded - lead_out

    vec_shape = vectors.shape
    vec_count = vec_shape[0] * vec_shape[1]
    vec_lines = -(-vec_count // spare)
    vec_fill = vec_lines * spare - vec_count
    vec_lanes = jnp.pad(vectors.reshape(vec_count).astype(bf16), (0, vec_fill))
    attn_block = jnp.concatenate(
        [
            qkv_weight.reshape(rows_own, 3 * piece).astype(bf16),
            out_weight.T.astype(bf16),
            jnp.pad(vec_lanes.reshape(vec_lines, spare), ((0, rows_own - vec_lines), (0, 0))),
        ],
        1,
    )
    up_block, down_block = up_weight.astype(bf16), down_weight.T.astype(bf16)
    staged = short_rows()
    if staged:
        attn_rows = spread_rows(attn_block)
        up_block, attn_rows = together(up_block, attn_rows)
        attn_one = spread_one(attn_rows)
        up_rows = spread_rows(up_block)
        down_block, up_rows = together(down_block, up_rows)
        down_rows = spread_rows(down_block)
        attn_own = assemble(spread_two(attn_one))
        up_one = spread_one(up_rows)
    else:
        attn_own, up_own, down_own = [
            gather_groups(b) for b in (attn_block, up_block, down_block)
        ]
    vec_own = attn_own.reshape(each, owners, rows_own, padded)[:, :, :vec_lines, width:]
    vec_oth = partner(vec_own)
    attn_oth = partner(attn_own)

    def vec_rows(lines):
        lines = lines.reshape(each, owners, vec_lines * spare)[:, :, :vec_count]
        lines = lines.reshape(each, owners, *vec_shape).transpose(0, 2, 1, 3)
        return lines.reshape(each, vec_shape[0], width).astype(f32)

    vec = jnp.stack([vec_rows(vec_own), vec_rows(vec_oth)], 1).reshape(cols, -1, width)
    vec = by_place(vec).reshape(-1, width)

    def widen(row):
        return jnp.pad(row, (0, spare))

    inputs = hidden_in.astype(f32)
    normed_one, scaled_one, inverse_one = normalize(inputs, vec[0], vec[1])
    normed_low = normed_one.astype(bf16)
    if staged:
        normed_low, up_one = together(normed_low, up_one)
        up_two = spread_two(up_one)
    bias = jnp.concatenate([widen(vec[2]), jnp.zeros((padded,), f32), widen(vec[3])]).reshape(1, -1)
    spans = tuple((part * piece, part * padded) for part in range(3))
    projected = None
    for places, weights in ((places_own, attn_own), (places_oth, attn_oth)):
        if staged and projected is not None:
            projected, down_rows = together(projected, down_rows)
        projected = multiply_and_place(
            places, normed_low, [weights], lanes_qkv, 0, spans, piece, 3 * padded, bias, projected
        )
    if staged:
        projected, down_one = together(projected, spread_one(down_rows))
        down_two = spread_two(down_one)
    ahead = [(c, c + 1) for c in range(cols - 1) if c % halves + 1 < halves]
    behind = [(b, a) for a, b in ahead]
    others = lax.ppermute(projected[:, padded:], "col", ahead)

    own_half = lax.dynamic_slice_in_dim(segments.reshape(-1), column * here, here, 0)
    first_half = lax.dynamic_slice_in_dim(
        segments.reshape(-1), (column - lax.rem(column, halves)) * here, here, 0
    )
    labels = (own_half.reshape(1, here), own_half.reshape(here, 1), first_half.reshape(here, 1))
    mixed, log_totals = attend(later, labels, projected, others)
    if staged:
        mixed, up_two = together(mixed, up_two)
        up_own = assemble(up_two)
    up_oth = partner(up_own)
    mixed_shape = jax.ShapeDtypeStruct((each, here, lanes_out), bf16)
    lead = 3 * piece - lead_out
    mixed_own, mixed_oth = split_call(
        functools.partial(split_mixed_kernel, piece, cols, lead),
        column_word,
        [mixed],
        [mixed_shape] * 2,
        "split_mixed",
    )
    residual = inputs + vec[4]
    for blocks, weights in ((mixed_own, attn_own), (mixed_oth, attn_oth)):
        for i in range(each):
            residual = residual + contract_last(blocks[i], weights[i][:, lead_out:])
    normed_two, scaled_two, inverse_two = normalize(residual, vec[5], vec[6])
    normed_two_low = normed_two.astype(bf16)

    bias_up = by_place(vec[8:])
    bias_own, bias_oth = bias_up[0::2], bias_up[1::2]

    if staged:
        normed_two_low, down_two = together(normed_two_low, down_two)
        down_own = assemble(down_two)
    down_oth = partner(down_own)
    unit = up_own.shape[2]
    wide_shape = jax.ShapeDtypeStruct((each, here, unit), f32)
    low_shape = jax.ShapeDtypeStruct((each, here, unit), bf16)
    sums_shape = jax.ShapeDtypeStruct((each, 1, unit), f32)
    sum_shape = jax.ShapeDtypeStruct((here, width), f32)

    def forward_part(ups, biases, downs, before):
        return feed_call(
            feed_forward_kernel,
            normed_two_low,
            [ups, biases.reshape(each, 1, unit), downs],
            before,
            [wide_shape, low_shape],
            sum_shape,
            "feed_forward",
        )

    def backward_part(ups, downs, linears, before):
        return feed_call(
            feed_backward_kernel,
            cotangent,
            [ups, downs, linears],
            before,
            [low_shape, sums_shape],
            sum_shape,
            "feed_backward",
        )

    left_down, left_up = cotangent.T, normed_two_low.T
    linear_own, lows_own, branch = forward_part(up_own, bias_own, down_own, None)
    linear_oth, lows_oth, branch = forward_part(up_oth, bias_oth, down_oth, branch)
    layer_out = (residual + branch + vec[7]).astype(bf16)
    sent_down = block_grads([(left_down, lows_oth)], None, None, False)
    linear_oth, sent_down = together(linear_oth, sent_down)
    received_down = partner(sent_down)
    dups_oth, dbias_oth, grad_normed_two = backward_part(up_oth, down_oth, linear_oth, None)
    sent_up = block_grads([(left_up, dups_oth)], None, None, False)
    lows_own, sent_up = together(lows_own, sent_up)
    received_up = partner(sent_up)
    total_down = block_grads([(left_down, lows_own)], None, received_down, staged)
    linear_own, total_down = together(linear_own, total_down)
    dups_own, dbias_own, grad_normed_two = backward_part(
        up_own, down_own, linear_own, grad_normed_two
    )
    one_down = scatter_one(total_down)

    grad_residual = cotangent.astype(f32) + norm_back(
        grad_normed_two, scaled_two, inverse_two, vec[5]
    )
    total_up = block_grads([(left_up, dups_own)], None, received_up, staged)
    grad_residual_low = grad_residual.astype(bf16)
    grad_residual_low, total_up, one_down = together(grad_residual_low, total_up, one_down)
    two_down = scatter_two(one_down)
    grad_mixed = multiply_and_place(
        jnp.concatenate([places_own, places_oth]),
        grad_residual_low,
        [attn_own, attn_oth],
        lanes_out,
        lead_out // lanes_out,
        ((lead, 0),),
        piece,
        padded,
        None,
        None,
    )
    dq, dk_own, dv_own, dk_oth, dv_oth = attend_back(
        later, labels, projected, others, grad_mixed, mixed, log_totals
    )
    one_up = scatter_one(total_up)
    dq, dk_own, dv_own, dk_oth, dv_oth, one_up, two_down = together(
        dq, dk_own, dv_own, dk_oth, dv_oth, one_up, two_down
    )
    back = lax.ppermute(jnp.concatenate([dk_oth, dv_oth], 1), "col", behind)
    grads_shape = jax.ShapeDtypeStruct((each, here, lanes_qkv), bf16)
    grads_own, grads_oth, grad_sums = split_call(
        functools.partial(split_grads_kernel, piece, cols),
        column_word,
        [dq, dk_own, dv_own, back],
        [grads_shape, grads_shape, jax.ShapeDtypeStruct((8, padded), f32)],
        "split_grads",
    )
    two_up = scatter_two(one_up)
    left_one, left_two = normed_low.T, grad_residual_low.T
    pairs_oth = [(left_one, grads_oth), (left_two, mixed_oth)]
    pairs_own = [(left_one, grads_own), (left_two, mixed_own)]
    received = partner(block_grads(pairs_oth, None, None, False))
    grad_normed_one = jnp.zeros((here, width), f32)
    for blocks, weights in ((grads_own, attn_own), (grads_oth, attn_oth)):
        for i in range(each):
            grad_normed_one = grad_normed_one + contract_last(blocks[i], weights[i][:, :lanes_qkv])
    input_grad = grad_residual + norm_back(grad_normed_one, scaled_one, inverse_one, vec[0])

    dbias = jnp.stack([dbias_own, dbias_oth], 1).reshape(cols, width)
    grad_vector = jnp.concatenate(
        [
            jnp.stack(
                [
                    jnp.sum(grad_normed_one * scaled_one, 0),
                    jnp.sum(grad_normed_one, 0),
                    grad_sums[0, :width],
                    grad_sums[1, :width],
                    jnp.sum(grad_residual, 0),
                    jnp.sum(grad_normed_two * scaled_two, 0),
                    jnp.sum(grad_normed_two, 0),
                    jnp.sum(cotangent.astype(f32), 0),
                ]
            ),
            by_place(dbias),
        ],
        0,
    ).astype(bf16)
    vec_part = grad_vector.reshape(cols, vec_shape[0], owners, vec_shape[1]).transpose(0, 2, 1, 3)
    vec_part = jnp.pad(vec_part.reshape(cols, owners, vec_count), ((0, 0), (0, 0), (0, vec_fill)))
    vec_part = by_place(vec_part.reshape(cols, owners, vec_lines, spare))
    vec_here = (vec_part[0::2].astype(f32) + partner(vec_part[1::2]).astype(f32)).astype(bf16)
    vec_here = jnp.pad(
        vec_here, ((0, 0), (0, 0), (0, rows_own - vec_lines), (LANES - spare, 0))
    ).reshape(each, width, LANES)
    total_attn = block_grads(pairs_own, vec_here, received, staged)
    sum_down, sum_up = scatter_three(two_down), scatter_three(two_up)
    sum_attn = scatter_three(scatter_two(scatter_one(total_attn)))
    sum_qkv = sum_attn[:, : 3 * piece].reshape(rows_own, 3, piece)
    sum_out = sum_attn[:, 3 * piece : width].T
    sum_vector = sum_attn[:vec_lines, width:].reshape(-1)[:vec_count].reshape(vec_shape)

    qkv_m, qkv_v, qkv_w = adamw(
        qkv_weight, sum_qkv, qkv_first, qkv_second, 1.5 * D ** (-0.5), decay_rate
    )
    out_m, out_v, out_w = adamw(
        out_weight, sum_out, out_first, out_second, 1.5 * (D // 64) ** (-0.5), decay_rate
    )
    up_m, up_v, up_w = adamw(up_weight, sum_up, up_first, up_second, 1.5 * D ** (-0.5), decay_rate)
    down_m, down_v, down_w = adamw(
        down_weight, sum_down.T, down_first, down_second, 1.5 * FF ** (-0.5), decay_rate
    )
    vec_m, vec_v, vec_w = adamw(vectors, sum_vector, vectors_first, vectors_second, 0.5, 0.0)
    return (
        layer_out,
        input_grad,
        qkv_m,
        qkv_v,
        qkv_w,
        out_m,
        out_v,
        out_w,
        up_m,
        up_v,
        up_w,
        down_m,
        down_v,
        down_w,
        vec_m,
        vec_v,
        vec_w,
    )


def solution(mesh):
    tokens = P(("dp", "row", "col"), None)
    qkv = P(("dp", "row"), None, "col")
    tall = P("col", ("dp", "row"))
    up = P(("dp", "row"), "col")
    state = (qkv, tall, up, tall, tall)
    return jax.shard_map(
        local,
        mesh=mesh,
        in_specs=(tokens, tokens, P(("dp", "row"), None)) + state * 3,
        out_specs=(tokens, tokens)
        + (qkv,) * 3
        + (tall,) * 3
        + (up,) * 3
        + (tall,) * 3
        + (tall,) * 3,
        check_vma=False,
    )
```

```python
import functools

import jax
import jax.numpy as jnp
from jax import lax
from jax.experimental import pallas as pl
from jax.experimental.pallas import tpu as pltpu
from jax.sharding import PartitionSpec as P

D = 1088
HEAD_DIM = 64
FF = 4352
SEQ = 1024
STEP = 5

LANES = 128


beta_one = 0.9
beta_two = 0.999
epsilon = 1e-08
decay_rate = 0.1
masked_score = -1000000000.0

f32 = jnp.float32
bf16 = jnp.bfloat16


def contract(left, right, left_dim, right_dim):
    return lax.dot_general(
        left, right, (((left_dim,), (right_dim,)), ((), ())), preferred_element_type=f32
    )


def contract_first(left, right):
    return contract(left, right, 0, 0)


def contract_last(left, right):
    return contract(left, right, 1, 1)


def normalize(rows, gain, shift):
    row_mean = jnp.mean(rows, -1, keepdims=True)
    centred = rows - row_mean
    inverse = lax.rsqrt(jnp.mean(centred * centred, -1, keepdims=True) + 1e-05)
    scaled = centred * inverse
    return (scaled * gain + shift, scaled, inverse)


def norm_back(grad_out, scaled, inverse, gain):
    grad_scaled = grad_out * gain
    return inverse * (
        grad_scaled
        - jnp.mean(grad_scaled, -1, keepdims=True)
        - scaled * jnp.mean(grad_scaled * scaled, -1, keepdims=True)
    )


def gelu_tanh(values):
    return jax.nn.gelu(values, approximate=True)


def adamw(weight, gradient, moment_one, moment_two, step_rate, shrink):
    moment_one = beta_one * moment_one + (1.0 - beta_one) * gradient
    moment_two = beta_two * moment_two + (1.0 - beta_two) * gradient * gradient
    update = (
        moment_one
        / (1.0 - beta_one**STEP)
        / (jnp.sqrt(moment_two / (1.0 - beta_two**STEP)) + epsilon)
    )
    return (moment_one, moment_two, weight - step_rate * (update + shrink * weight))


def mask_tables(kseg_own, kseg_oth, qseg, bias_own, bias_oth):
    count = bias_own.shape[0]
    key_place = lax.broadcasted_iota(jnp.int32, (count, count), 0)
    query_place = lax.broadcasted_iota(jnp.int32, (count, count), 1)
    same = kseg_own[...] == qseg[...]
    bias_own[...] = jnp.where(same & (key_place <= query_place), 0.0, masked_score)
    bias_oth[...] = jnp.where(kseg_oth[...] == qseg[...], 0.0, masked_score)


def head_lanes(block, half):
    lane = lax.broadcasted_iota(jnp.int32, block.shape, 1)
    return jnp.where((lane // HEAD_DIM) == half, block, jnp.zeros_like(block))


def attention_forward(
    later, qseg, kseg_own, kseg_oth, q, k_own, v_own, k_oth, v_oth, out, lse, bias_own, bias_oth
):
    pair = pl.program_id(0)
    count = q.shape[0]
    step = count // 2

    @pl.when(pair == 0)
    def _():
        mask_tables(kseg_own, kseg_oth, qseg, bias_own, bias_oth)

    def body(with_other):
        queries = q[...] * jnp.asarray(HEAD_DIM**-0.5, bf16)
        values_own = v_own[...].astype(f32).T.astype(bf16)
        values_oth = v_oth[...].astype(f32).T.astype(bf16) if with_other else None
        for part in range(2):
            cols = slice(part * step, (part + 1) * step)
            seen = (part + 1) * step
            pieces = []
            for half in range(2):
                q_head = head_lanes(queries[cols], half)
                rows = slice(half * HEAD_DIM, (half + 1) * HEAD_DIM)
                s_own = contract_last(k_own[:seen], q_head) + bias_own[:seen, cols]
                top = jnp.max(s_own, 0, keepdims=True)
                if with_other:
                    s_oth = contract_last(k_oth[...], q_head) + bias_oth[:, cols]
                    top = jnp.maximum(top, jnp.max(s_oth, 0, keepdims=True))
                e_own = jnp.exp(s_own - top)
                total = jnp.sum(e_own, 0, keepdims=True)
                mixed = jnp.dot(
                    values_own[rows, :seen], e_own.astype(bf16), preferred_element_type=f32
                )
                if with_other:
                    e_oth = jnp.exp(s_oth - top)
                    total = total + jnp.sum(e_oth, 0, keepdims=True)
                    mixed = mixed + jnp.dot(
                        values_oth[rows], e_oth.astype(bf16), preferred_element_type=f32
                    )
                lse[0, half : half + 1, cols] = top + jnp.log(total)
                pieces.append(mixed / total)
            out[cols] = jnp.concatenate(pieces, 0).T.astype(bf16)

    @pl.when(later[0] == 1)
    def _():
        body(True)

    @pl.when(later[0] == 0)
    def _():
        body(False)


def attention_backward(
    later, qseg, kseg_own, kseg_oth, q, k_own, v_own, k_oth, v_oth, grad, out, lse,
    dq, dk_own, dv_own, dk_oth, dv_oth, bias_own, bias_oth,
):
    pair = pl.program_id(0)
    count = q.shape[0]
    step = count // 2

    @pl.when(pair == 0)
    def _():
        mask_tables(kseg_own, kseg_oth, qseg, bias_own, bias_oth)

    def body(with_other):
        scale = jnp.asarray(HEAD_DIM**-0.5, bf16)
        queries = q[...] * scale
        keys_own = k_own[...].astype(f32).T.astype(bf16)
        keys_oth = k_oth[...].astype(f32).T.astype(bf16) if with_other else None
        products = (grad[...].astype(f32) * out[...].astype(f32)).T
        dk_a = [jnp.zeros((step, LANES), f32) for _ in range(2)]
        dv_a = [jnp.zeros((step, LANES), f32) for _ in range(2)]
        dk_b = jnp.zeros((count, LANES), f32)
        dv_b = jnp.zeros((count, LANES), f32)
        for part in range(2):
            cols = slice(part * step, (part + 1) * step)
            pieces = []
            for half in range(2):
                q_head = head_lanes(queries[cols], half)
                g_head = head_lanes(grad[cols], half)
                rows = slice(half * HEAD_DIM, (half + 1) * HEAD_DIM)
                delta = jnp.sum(products[rows, cols], 0, keepdims=True)
                log_total = lse[0, half : half + 1, cols]

                def block(keys, values, bias):
                    probs = jnp.exp(contract_last(keys, q_head) + bias - log_total)
                    d_probs = contract_last(values, g_head)
                    d_scores = (probs * (d_probs - delta)).astype(bf16)
                    dk = jnp.dot(d_scores, q_head, preferred_element_type=f32)
                    dv = jnp.dot(probs.astype(bf16), g_head, preferred_element_type=f32)
                    return (d_scores, dk, dv)

                d_query = jnp.zeros((HEAD_DIM, step), f32)
                for chunk in range(part + 1):
                    span = slice(chunk * step, (chunk + 1) * step)
                    d_scores, dk, dv = block(k_own[span], v_own[span], bias_own[span, cols])
                    dk_a[chunk] = dk_a[chunk] + dk
                    dv_a[chunk] = dv_a[chunk] + dv
                    d_query = d_query + jnp.dot(
                        keys_own[rows, span], d_scores, preferred_element_type=f32
                    )
                if with_other:
                    d_scores, dk, dv = block(k_oth[...], v_oth[...], bias_oth[:, cols])
                    dk_b = dk_b + dk
                    dv_b = dv_b + dv
                    d_query = d_query + jnp.dot(
                        keys_oth[rows], d_scores, preferred_element_type=f32
                    )
                pieces.append(d_query)
            dq[cols] = (jnp.concatenate(pieces, 0).T * HEAD_DIM**-0.5).astype(bf16)
        for chunk in range(2):
            span = slice(chunk * step, (chunk + 1) * step)
            dk_own[span] = dk_a[chunk].astype(bf16)
            dv_own[span] = dv_a[chunk].astype(bf16)
        dk_oth[...] = dk_b.astype(bf16)
        dv_oth[...] = dv_b.astype(bf16)

    @pl.when(later[0] == 1)
    def _():
        body(True)

    @pl.when(later[0] == 0)
    def _():
        body(False)


def attention_specs(count, pairs):
    def whole(shape):
        return pl.BlockSpec(shape, lambda p, later: (0,) * len(shape))

    def lanes(start):
        return pl.BlockSpec((count, LANES), lambda p, later: (0, start + p))

    segments = [whole((1, count)), whole((count, 1)), whole((count, 1))]
    projected = [lanes(0), lanes(pairs), lanes(2 * pairs), lanes(0), lanes(pairs)]
    totals = pl.BlockSpec((1, 2, count), lambda p, later: (p, 0, 0))
    return segments, projected, lanes(0), totals


def attend(later, labels, projected, others):
    count = projected.shape[0]
    pairs = projected.shape[1] // (3 * LANES)
    segments, blocks, wide, totals = attention_specs(count, pairs)
    work = count * count * LANES * pairs * 2
    return pl.pallas_call(
        attention_forward,
        grid_spec=pltpu.PrefetchScalarGridSpec(
            num_scalar_prefetch=1,
            grid=(pairs,),
            in_specs=segments + blocks,
            out_specs=[wide, totals],
            scratch_shapes=[pltpu.VMEM((count, count), f32), pltpu.VMEM((count, count), f32)],
        ),
        out_shape=[
            jax.ShapeDtypeStruct((count, pairs * LANES), bf16),
            jax.ShapeDtypeStruct((pairs, 2, count), f32),
        ],
        compiler_params=pltpu.CompilerParams(vmem_limit_bytes=48 << 20),
        name="attention_forward",
    )(later, *labels, projected, projected, projected, others, others)


def attend_back(later, labels, projected, others, grad, mixed, log_totals):
    count = projected.shape[0]
    pairs = projected.shape[1] // (3 * LANES)
    segments, blocks, wide, totals = attention_specs(count, pairs)
    work = count * count * LANES * pairs * 2
    return pl.pallas_call(
        attention_backward,
        grid_spec=pltpu.PrefetchScalarGridSpec(
            num_scalar_prefetch=1,
            grid=(pairs,),
            in_specs=segments + blocks + [wide, wide, totals],
            out_specs=[wide] * 5,
            scratch_shapes=[pltpu.VMEM((count, count), f32), pltpu.VMEM((count, count), f32)],
        ),
        out_shape=[jax.ShapeDtypeStruct((count, pairs * LANES), bf16)] * 5,
        compiler_params=pltpu.CompilerParams(vmem_limit_bytes=48 << 20),
        name="attention_backward",
    )(later, *labels, projected, projected, projected, others, others, grad, mixed, log_totals)


def place_kernel(spans, piece, sources, biased, continued, places, x, *refs):
    weights, refs = refs[:sources], refs[sources:]
    bias, refs = (refs[0], refs[1:]) if biased else (None, refs)
    before, refs = (refs[0], refs[1:]) if continued else (None, refs)
    out, whole, product = refs
    step = pl.program_id(0)
    each = pl.num_programs(0) // sources

    @pl.when(step == 0)
    def _():
        whole[...] = before[...].astype(f32) if continued else jnp.zeros_like(whole)

    for k, weight in enumerate(weights):

        @pl.when(step // each == k)
        def _(weight=weight):
            product[...] = jnp.dot(x[...], weight[0], preferred_element_type=f32)

    for place in range(x.shape[1] // piece):

        @pl.when(places[step] == place)
        def _(place=place):
            for source, target in spans:
                start = target + place * piece
                block = product[:, source : source + piece]
                if biased:
                    block = block + bias[:, start : start + piece]
                whole[:, start : start + piece] = block

    @pl.when(step == pl.num_programs(0) - 1)
    def _():
        out[...] = whole[...].astype(bf16)


def multiply_and_place(places, x, weights, lanes, lane_block, spans, piece, out_lanes, bias, before):
    count, depth = x.shape
    each = weights[0].shape[0]
    sources = len(weights)

    def fixed(shape):
        return pl.BlockSpec(shape, lambda j, places: (0, 0))

    in_specs = [fixed((count, depth))]
    for k in range(sources):
        in_specs.append(
            pl.BlockSpec(
                (1, depth, lanes),
                lambda j, places, k=k: (jnp.clip(j - k * each, 0, each - 1), 0, lane_block),
            )
        )
    operands = [x, *weights]
    if bias is not None:
        in_specs.append(fixed(bias.shape))
        operands.append(bias)
    if before is not None:
        in_specs.append(fixed(before.shape))
        operands.append(before)
    return pl.pallas_call(
        functools.partial(
            place_kernel, spans, piece, sources, bias is not None, before is not None
        ),
        grid_spec=pltpu.PrefetchScalarGridSpec(
            num_scalar_prefetch=1,
            grid=(each * sources,),
            in_specs=in_specs,
            out_specs=fixed((count, out_lanes)),
            scratch_shapes=[pltpu.VMEM((count, out_lanes), f32), pltpu.VMEM((count, lanes), f32)],
        ),
        out_shape=jax.ShapeDtypeStruct((count, out_lanes), bf16),
        compiler_params=pltpu.CompilerParams(vmem_limit_bytes=48 << 20),
        name="multiply_and_place",
    )(places, *operands)


def add_product_kernel(each, blocks_own, blocks_oth, own, oth, start, out):
    step = pl.program_id(0)

    @pl.when(step == 0)
    def _():
        out[...] = start[...]

    for k, (blocks, weights) in enumerate(((blocks_own, own), (blocks_oth, oth))):

        @pl.when(step // each == k)
        def _(blocks=blocks, weights=weights):
            out[...] += contract_last(blocks[0], weights[0])


def add_products(start, blocks_own, blocks_oth, own, oth, lane_block):
    each, count, lanes = blocks_own.shape
    width = own.shape[1]

    def stepped(shape, k, lane):
        return pl.BlockSpec(
            (1, *shape), lambda j: (jnp.clip(j - k * each, 0, each - 1), 0, lane)
        )

    whole = pl.BlockSpec((count, width), lambda j: (0, 0))
    return pl.pallas_call(
        functools.partial(add_product_kernel, each),
        grid=(2 * each,),
        in_specs=[stepped((count, lanes), k, 0) for k in range(2)]
        + [stepped((width, lanes), k, lane_block) for k in range(2)]
        + [whole],
        out_specs=whole,
        out_shape=jax.ShapeDtypeStruct((count, width), f32),
        compiler_params=pltpu.CompilerParams(vmem_limit_bytes=48 << 20),
        name="add_products",
    )(blocks_own, blocks_oth, own, oth, start)


def split_all(column, cols, write):
    for here in range(cols):

        @pl.when(column[0] == here)
        def _(here=here):
            for k in range(cols):
                write(k % 2, k // 2, here ^ k)


def split_mixed_kernel(piece, cols, lead, column, mixed, own, oth):
    count, lanes = own.shape[1:]
    values = mixed[...].astype(f32)
    before = jnp.zeros((count, lead), f32)
    after = jnp.zeros((count, lanes - lead - piece), f32)

    def write(which, i, c):
        block = values[:, c * piece : (c + 1) * piece]
        (own, oth)[which][i] = jnp.concatenate([before, block, after], 1).astype(bf16)

    split_all(column, cols, write)


def split_grads_kernel(piece, cols, column, dq, dk, dv, back, own, oth, sums):
    count, lanes = own.shape[1:]
    wide = dq.shape[1]
    grads = [
        dq[...].astype(f32),
        dk[...].astype(f32) + back[:, :wide].astype(f32),
        dv[...].astype(f32) + back[:, wide:].astype(f32),
    ]
    sums[0:1] = jnp.sum(grads[0], 0, keepdims=True)
    sums[1:2] = jnp.sum(grads[2], 0, keepdims=True)
    after = jnp.zeros((count, lanes - 3 * piece), f32)

    def write(which, i, c):
        blocks = [g[:, c * piece : (c + 1) * piece] for g in grads]
        (own, oth)[which][i] = jnp.concatenate([*blocks, after], 1).astype(bf16)

    split_all(column, cols, write)


def whole_specs(shapes):
    return [pl.BlockSpec(s, lambda i, p, n=len(s): (0,) * n) for s in shapes]


def split_call(kernel, column, operands, out_shapes, name):
    moved = sum(x.size * x.dtype.itemsize for x in operands) * 2
    return pl.pallas_call(
        kernel,
        grid_spec=pltpu.PrefetchScalarGridSpec(
            num_scalar_prefetch=1,
            grid=(1,),
            in_specs=whole_specs([x.shape for x in operands]),
            out_specs=whole_specs([s.shape for s in out_shapes]),
        ),
        out_shape=out_shapes,
        compiler_params=pltpu.CompilerParams(vmem_limit_bytes=48 << 20),
        name=name,
    )(column, *operands)


def block_grads_kernel(counts, has_vec, has_received, split, place, *refs):
    refs = list(refs)
    step = pl.program_id(0)
    lefts = [refs.pop(0) for _ in counts]
    rights = [[refs.pop(0) for _ in range(count)] for count in counts]
    vec_part = refs.pop(0) if has_vec else None
    received = refs.pop(0) if has_received else None
    width = lefts[0].shape[0]
    quarter = width // 4

    def value(start):
        rows = pl.ds(start, quarter)
        if len(counts) == 1:
            whole = jnp.dot(lefts[0][rows], rights[0][0][0], preferred_element_type=f32)
        else:
            one, two = [
                jnp.dot(left[rows], right[0][0], preferred_element_type=f32)
                for left, right in zip(lefts, rights)
            ]
            lead = one.shape[1] - LANES
            whole = jnp.concatenate(
                [one[:, :lead], one[:, lead:] + two[:, :LANES], two[:, LANES:]], 1
            )
        if has_vec:
            more = whole[:, -LANES:] + vec_part[0, rows].astype(f32)
            whole = jnp.concatenate([whole[:, :-LANES], more], 1)
        if has_received:
            whole = whole + received[0, rows].astype(f32)
        return whole.astype(bf16)

    for i in range(2):

        @pl.when(step == i)
        def _(i=i):
            if not split:
                for k in range(4):
                    refs[0][0, k * quarter : (k + 1) * quarter] = value(k * quarter)
                return
            first_keep, first_send, second_keep, second_send = refs
            half = width // 2
            first_keep[0] = value(pl.multiple_of(place[0] * half, 16))
            first_send[0] = value(pl.multiple_of((1 - place[0]) * half, 16))
            second = (second_keep, second_send)[i]
            for dp in range(2):
                second[dp] = value(dp * half + quarter)


def block_grads(pairs, vec_part, received, split):
    lefts, rights = zip(*pairs)
    rights = [r if isinstance(r, list) else [r] for r in rights]
    width, count = lefts[0].shape
    each = 2
    lanes = width if len(pairs) == 1 else -(-width // LANES) * LANES
    place = lax.axis_index("dp").reshape(1).astype(jnp.int32)

    def fixed(shape):
        return pl.BlockSpec(shape, lambda i, place: (0,) * len(shape))

    def step(shape):
        return pl.BlockSpec((1, *shape[1:]), lambda i, place: (i, 0, 0))

    flat = [r for right in rights for r in right]
    more = [x for x in (vec_part, received) if x is not None]
    in_specs = [fixed(x.shape) for x in lefts]
    in_specs += [step(x.shape) if x.ndim == 3 else fixed(x.shape) for x in flat]
    in_specs += [step(x.shape) for x in more]
    if split:
        part = (each, width // 4, lanes)
        out_specs = [step(part), step(part), fixed(part), fixed(part)]
        out_shape = [jax.ShapeDtypeStruct(part, bf16)] * 4
    else:
        out_specs = step((each, width, lanes))
        out_shape = jax.ShapeDtypeStruct((each, width, lanes), bf16)
    return pl.pallas_call(
        functools.partial(
            block_grads_kernel,
            [len(r) for r in rights],
            vec_part is not None,
            received is not None,
            split,
        ),
        grid_spec=pltpu.PrefetchScalarGridSpec(
            num_scalar_prefetch=1,
            grid=(each,),
            in_specs=in_specs,
            out_specs=out_specs,
        ),
        out_shape=out_shape,
        compiler_params=pltpu.CompilerParams(vmem_limit_bytes=48 << 20),
        name="block_grads",
    )(place, *lefts, *flat, *more)


def gelu_parts(values):
    scale = (2.0 / jnp.pi) ** 0.5
    square = values * values
    return jnp.tanh(scale * values * (1.0 + 0.044715 * square)), scale * (
        1.0 + (3.0 * 0.044715) * square
    )


def feed_forward_kernel(continued, x, up, bias, down, *refs):
    before, refs = (refs[0], refs[1:]) if continued else (None, refs)
    linear, active, branch = refs
    count = x.shape[0]

    @pl.when(pl.program_id(0) == 0)
    def _():
        branch[...] = before[...] if continued else jnp.zeros_like(branch)

    for k in range(2):
        rows = slice(k * count // 2, (k + 1) * count // 2)
        values = jnp.dot(x[rows], up[0], preferred_element_type=f32) + bias[0]
        linear[0, rows] = values
        low = (0.5 * values * (1.0 + gelu_parts(values)[0])).astype(bf16)
        active[0, rows] = low
        branch[rows] += contract_last(low, down[0])


def feed_backward_kernel(continued, grad, up, down, linear, *refs):
    before, refs = (refs[0], refs[1:]) if continued else (None, refs)
    lows, sums, grad_in = refs
    count = grad.shape[0]

    @pl.when(pl.program_id(0) == 0)
    def _():
        grad_in[...] = before[...] if continued else jnp.zeros_like(grad_in)

    sums[...] = jnp.zeros_like(sums)
    for k in range(2):
        rows = slice(k * count // 2, (k + 1) * count // 2)
        values = linear[0, rows]
        tanh, slope = gelu_parts(values)
        derivative = 0.5 * (1.0 + tanh) + 0.5 * values * (1.0 - tanh * tanh) * slope
        grads = jnp.dot(grad[rows], down[0], preferred_element_type=f32) * derivative
        sums[0] += jnp.sum(grads, 0, keepdims=True)
        low = grads.astype(bf16)
        lows[0, rows] = low
        grad_in[rows] += contract_last(low, up[0])


def feed_call(kernel, fixed, stepped, before, out_stepped, out_fixed, name):
    each = stepped[0].shape[0]

    def whole(x):
        return pl.BlockSpec(x.shape, lambda i: (0,) * len(x.shape))

    def step(x):
        return pl.BlockSpec((1, *x.shape[1:]), lambda i: (i, 0, 0))

    operands = [fixed, *stepped]
    in_specs = [whole(fixed)] + [step(x) for x in stepped]
    if before is not None:
        operands.append(before)
        in_specs.append(whole(before))
    return pl.pallas_call(
        functools.partial(kernel, before is not None),
        grid=(each,),
        in_specs=in_specs,
        out_specs=[step(x) for x in out_stepped] + [whole(out_fixed)],
        out_shape=[*out_stepped, out_fixed],
        compiler_params=pltpu.CompilerParams(vmem_limit_bytes=56 << 20),
        name=name,
    )(*operands)


AXES = ("col", "dp", "row")


def planes():
    owners = lax.axis_size("dp") * lax.axis_size("row")
    cols = lax.axis_size("col")
    return [
        [c * owners + k for c in range(p, cols, 2) for k in range(owners)] for p in range(2)
    ]


def flip_col(block, bit):
    return lax.ppermute(block, "col", [(c, c ^ bit) for c in range(lax.axis_size("col"))])


def partner(block):
    return flip_col(block, 1)


def flip_dp(block):
    return lax.ppermute(block, "dp", [(0, 1), (1, 0)])


def shift_row(block, by):
    count = lax.axis_size("row")
    return lax.ppermute(block, "row", [(i, (i + by) % count) for i in range(count)])


def by_place(blocks):
    column = lax.axis_index("col")
    pairs = blocks.reshape(-1, 2, *blocks.shape[1:])
    pairs = jnp.where(column % 2 == 1, pairs[:, ::-1], pairs)
    return upper_bit(pairs).reshape(blocks.shape)


def upper_bit(blocks):
    return jnp.where(lax.axis_index("col") // 2 == 1, blocks[::-1], blocks)


def short_rows():
    return lax.axis_size("row") == 4 and lax.axis_size("dp") == 2 and lax.axis_size("col") == 4


def assemble_kernel(place, *refs):
    sources, (out, held, sems_in, sems_out) = refs[:-4], refs[-4:]
    dp, row = place[0], place[1]
    order = (
        [(0, 0, 0), (0, 0, 1), (1, 0, 0), (1, 0, 1), (0, 0, 2), (0, 0, 3), (0, 1, 2), (0, 1, 3)]
        + [(0, 1, 0), (0, 1, 1), (1, 1, 0), (1, 1, 1)]
        + [(1, 0, 2), (1, 0, 3), (1, 1, 2), (1, 1, 3)]
    )
    blocks = [source.at[i] for source in sources for i in range(source.shape[0])]
    copies_in, copies_out = [], []
    for k, (block, (over_x, over_y, behind)) in enumerate(zip(blocks, order)):
        target = over_x * 8 + (1 - dp if over_y else dp) * 4 + lax.rem(row + 4 - behind, 4)
        copies_in.append(pltpu.make_async_copy(block, held.at[k], sems_in.at[k]))
        copies_out.append(pltpu.make_async_copy(held.at[k], out.at[target], sems_out.at[k]))
    for copy in copies_in:
        copy.start()
    for copy_in, copy_out in zip(copies_in, copies_out):
        copy_in.wait()
        copy_out.start()
    for copy in copies_out:
        copy.wait()


def assemble(pieces):
    rows, lanes = pieces[0].shape[-2:]
    pieces = [p.reshape(-1, rows, lanes) for p in pieces]
    place = jnp.stack([lax.axis_index("dp"), lax.axis_index("row")]).astype(jnp.int32)
    anywhere = pl.BlockSpec(memory_space=pl.ANY)
    out = pl.pallas_call(
        assemble_kernel,
        grid_spec=pltpu.PrefetchScalarGridSpec(
            num_scalar_prefetch=1,
            grid=(1,),
            in_specs=[anywhere] * len(pieces),
            out_specs=anywhere,
            scratch_shapes=[
                pltpu.VMEM((16, rows, lanes), bf16),
                pltpu.SemaphoreType.DMA((16,)),
                pltpu.SemaphoreType.DMA((16,)),
            ],
        ),
        out_shape=jax.ShapeDtypeStruct((16, rows, lanes), bf16),
        compiler_params=pltpu.CompilerParams(vmem_limit_bytes=48 << 20),
        name="assemble",
    )(place, *pieces)
    return out.reshape(2, -1, lanes)


def spread_rows(block):
    return [block] + [shift_row(block, m) for m in range(1, 4)]


def spread_one(pieces):
    first, second = jnp.stack(pieces[:2]), jnp.stack(pieces[2:])
    return [first, flip_col(first, 2), second, flip_dp(second)]


def spread_two(pieces):
    first_y = flip_dp(jnp.stack(pieces[:2]))
    return [*pieces, first_y, flip_col(jnp.stack(pieces[2:]), 2)]


def gather_groups(block):
    whole = lax.all_gather(block, AXES, axis=0, tiled=False, axis_index_groups=planes())
    return upper_bit(whole.reshape(lax.axis_size("col") // 2, -1, block.shape[-1]))


def together(*arrays):
    return lax.optimization_barrier(arrays)


def added(one, other):
    return (one.astype(f32) + other.astype(f32)).astype(bf16)


def at_place(array, which, axis):
    return lax.dynamic_index_in_dim(array, which, axis, keepdims=False)


def scatter_one(blocks):
    if not short_rows():
        return blocks
    first_keep, first_send, second_keep, second_send = blocks
    first_y, second_x = flip_dp(first_send), flip_col(second_send, 2)
    return added(first_keep, first_y), added(second_keep, second_x)


def scatter_two(halves):
    if not short_rows():
        return halves
    dp = lax.axis_index("dp")
    first, second = halves
    first_x = flip_col(first[1], 2)
    second_y = flip_dp(at_place(second, 1 - dp, 0))
    both = jnp.concatenate(
        [added(first[0], first_x), added(at_place(second, dp, 0), second_y)], 0
    )
    return both.reshape(4, -1, both.shape[-1])


def scatter_three(rows):
    if not short_rows():
        flat = upper_bit(rows).reshape(-1, rows.shape[-1])
        return lax.psum_scatter(
            flat, AXES, scatter_dimension=0, tiled=True, axis_index_groups=planes()
        ).astype(f32)
    row = lax.axis_index("row")
    total = at_place(rows, row, 0).astype(f32)
    for m in range(1, 4):
        total = total + shift_row(at_place(rows, (row + m) % 4, 0), m).astype(f32)
    return total


def local(
    hidden_in,
    cotangent,
    segments,
    qkv_weight,
    out_weight,
    up_weight,
    down_weight,
    vectors,
    qkv_first,
    out_first,
    up_first,
    down_first,
    vectors_first,
    qkv_second,
    out_second,
    up_second,
    down_second,
    vectors_second,
):
    column = lax.axis_index("col")
    cols = lax.axis_size("col")
    here, width = hidden_in.shape
    rows_own = qkv_weight.shape[0]
    owners = lax.axis_size("dp") * lax.axis_size("row")
    piece = qkv_weight.shape[2]
    halves = SEQ // here
    each = cols // 2
    column_word = column.reshape(1).astype(jnp.int32)
    places_own = (column ^ (2 * jnp.arange(each))).astype(jnp.int32)
    places_oth = (column ^ (2 * jnp.arange(each) + 1)).astype(jnp.int32)
    later = lax.rem(column, halves).reshape(1).astype(jnp.int32)
    padded = -(-width // LANES) * LANES
    spare = padded - width
    lanes_qkv = -(-3 * piece // LANES) * LANES
    lead_out = 3 * piece // LANES * LANES
    lanes_out = padded - lead_out

    vec_shape = vectors.shape
    vec_count = vec_shape[0] * vec_shape[1]
    vec_lines = -(-vec_count // spare)
    vec_fill = vec_lines * spare - vec_count
    vec_lanes = jnp.pad(vectors.reshape(vec_count).astype(bf16), (0, vec_fill))
    attn_block = jnp.concatenate(
        [
            qkv_weight.reshape(rows_own, 3 * piece).astype(bf16),
            out_weight.T.astype(bf16),
            jnp.pad(vec_lanes.reshape(vec_lines, spare), ((0, rows_own - vec_lines), (0, 0))),
        ],
        1,
    )
    up_block, down_block = up_weight.astype(bf16), down_weight.T.astype(bf16)
    staged = short_rows()
    if staged:
        attn_rows = spread_rows(attn_block)
        up_block, attn_rows = together(up_block, attn_rows)
        attn_one = spread_one(attn_rows)
        up_rows = spread_rows(up_block)
        down_block, up_rows = together(down_block, up_rows)
        down_rows = spread_rows(down_block)
        attn_two, up_rows = together(spread_two(attn_one), up_rows)
        attn_own = assemble(attn_two)
        up_one = spread_one(up_rows)
    else:
        attn_own, up_own, down_own = [
            gather_groups(b) for b in (attn_block, up_block, down_block)
        ]
    vec_own = attn_own.reshape(each, owners, rows_own, padded)[:, :, :vec_lines, width:]
    vec_oth = partner(vec_own)
    attn_oth = partner(attn_own)

    def vec_rows(lines):
        lines = lines.reshape(each, owners, vec_lines * spare)[:, :, :vec_count]
        lines = lines.reshape(each, owners, *vec_shape).transpose(0, 2, 1, 3)
        return lines.reshape(each, vec_shape[0], width).astype(f32)

    vec = jnp.stack([vec_rows(vec_own), vec_rows(vec_oth)], 1).reshape(cols, -1, width)
    vec = by_place(vec).reshape(-1, width)

    def widen(row):
        return jnp.pad(row, (0, spare))

    inputs = hidden_in.astype(f32)
    normed_one, scaled_one, inverse_one = normalize(inputs, vec[0], vec[1])
    normed_low = normed_one.astype(bf16)
    if staged:
        normed_low, up_one = together(normed_low, up_one)
        up_two = spread_two(up_one)
    bias = jnp.concatenate([widen(vec[2]), jnp.zeros((padded,), f32), widen(vec[3])]).reshape(1, -1)
    spans = tuple((part * piece, part * padded) for part in range(3))
    projected = None
    for places, weights in ((places_own, attn_own), (places_oth, attn_oth)):
        if staged and projected is not None:
            projected, down_rows = together(projected, down_rows)
        projected = multiply_and_place(
            places, normed_low, [weights], lanes_qkv, 0, spans, piece, 3 * padded, bias, projected
        )
    if staged:
        projected, down_one = together(projected, spread_one(down_rows))
        down_two = spread_two(down_one)
    ahead = [(c, c + 1) for c in range(cols - 1) if c % halves + 1 < halves]
    behind = [(b, a) for a, b in ahead]
    others = lax.ppermute(projected[:, padded:], "col", ahead)

    own_half = lax.dynamic_slice_in_dim(segments.reshape(-1), column * here, here, 0)
    first_half = lax.dynamic_slice_in_dim(
        segments.reshape(-1), (column - lax.rem(column, halves)) * here, here, 0
    )
    labels = (own_half.reshape(1, here), own_half.reshape(here, 1), first_half.reshape(here, 1))
    mixed, log_totals = attend(later, labels, projected, others)
    if staged:
        mixed, up_two = together(mixed, up_two)
        up_own = assemble(up_two)
    up_oth = partner(up_own)
    mixed_shape = jax.ShapeDtypeStruct((each, here, lanes_out), bf16)
    lead = 3 * piece - lead_out
    mixed_own, mixed_oth = split_call(
        functools.partial(split_mixed_kernel, piece, cols, lead),
        column_word,
        [mixed],
        [mixed_shape] * 2,
        "split_mixed",
    )
    residual = add_products(
        inputs + vec[4], mixed_own, mixed_oth, attn_own, attn_oth, lead_out // lanes_out
    )
    normed_two, scaled_two, inverse_two = normalize(residual, vec[5], vec[6])
    normed_two_low = normed_two.astype(bf16)

    bias_up = by_place(vec[8:])
    bias_own, bias_oth = bias_up[0::2], bias_up[1::2]

    if staged:
        normed_two_low, down_two = together(normed_two_low, down_two)
        down_own = assemble(down_two)
    down_oth = partner(down_own)
    unit = up_own.shape[2]
    wide_shape = jax.ShapeDtypeStruct((each, here, unit), f32)
    low_shape = jax.ShapeDtypeStruct((each, here, unit), bf16)
    sums_shape = jax.ShapeDtypeStruct((each, 1, unit), f32)
    sum_shape = jax.ShapeDtypeStruct((here, width), f32)

    def forward_part(ups, biases, downs, before):
        return feed_call(
            feed_forward_kernel,
            normed_two_low,
            [ups, biases.reshape(each, 1, unit), downs],
            before,
            [wide_shape, low_shape],
            sum_shape,
            "feed_forward",
        )

    def backward_part(ups, downs, linears, before):
        return feed_call(
            feed_backward_kernel,
            cotangent,
            [ups, downs, linears],
            before,
            [low_shape, sums_shape],
            sum_shape,
            "feed_backward",
        )

    left_down, left_up = cotangent.T, normed_two_low.T
    linear_own, lows_own, branch = forward_part(up_own, bias_own, down_own, None)
    linear_oth, lows_oth, branch = forward_part(up_oth, bias_oth, down_oth, branch)
    layer_out = (residual + branch + vec[7]).astype(bf16)
    sent_down = block_grads([(left_down, lows_oth)], None, None, False)
    linear_oth, sent_down = together(linear_oth, sent_down)
    received_down = partner(sent_down)
    dups_oth, dbias_oth, grad_normed_two = backward_part(up_oth, down_oth, linear_oth, None)
    sent_up = block_grads([(left_up, dups_oth)], None, None, False)
    lows_own, sent_up = together(lows_own, sent_up)
    received_up = partner(sent_up)
    total_down = block_grads([(left_down, lows_own)], None, received_down, staged)
    linear_own, total_down = together(linear_own, total_down)
    dups_own, dbias_own, grad_normed_two = backward_part(
        up_own, down_own, linear_own, grad_normed_two
    )
    one_down = scatter_one(total_down)
    dups_own, grad_normed_two, one_down = together(dups_own, grad_normed_two, one_down)

    grad_residual = cotangent.astype(f32) + norm_back(
        grad_normed_two, scaled_two, inverse_two, vec[5]
    )
    total_up = block_grads([(left_up, dups_own)], None, received_up, staged)
    grad_residual_low = grad_residual.astype(bf16)
    grad_residual_low, total_up = together(grad_residual_low, total_up)
    two_down = scatter_two(one_down)
    grad_mixed = multiply_and_place(
        jnp.concatenate([places_own, places_oth]),
        grad_residual_low,
        [attn_own, attn_oth],
        lanes_out,
        lead_out // lanes_out,
        ((lead, 0),),
        piece,
        padded,
        None,
        None,
    )
    dq, dk_own, dv_own, dk_oth, dv_oth = attend_back(
        later, labels, projected, others, grad_mixed, mixed, log_totals
    )
    one_up = scatter_one(total_up)
    dq, dk_own, dv_own, dk_oth, dv_oth, one_up, two_down = together(
        dq, dk_own, dv_own, dk_oth, dv_oth, one_up, two_down
    )
    back = lax.ppermute(jnp.concatenate([dk_oth, dv_oth], 1), "col", behind)
    grads_shape = jax.ShapeDtypeStruct((each, here, lanes_qkv), bf16)
    grads_own, grads_oth, grad_sums = split_call(
        functools.partial(split_grads_kernel, piece, cols),
        column_word,
        [dq, dk_own, dv_own, back],
        [grads_shape, grads_shape, jax.ShapeDtypeStruct((8, padded), f32)],
        "split_grads",
    )
    two_up = scatter_two(one_up)
    left_one, left_two = normed_low.T, grad_residual_low.T
    pairs_oth = [(left_one, grads_oth), (left_two, mixed_oth)]
    pairs_own = [(left_one, grads_own), (left_two, mixed_own)]
    received = partner(block_grads(pairs_oth, None, None, False))
    grad_normed_one = jnp.zeros((here, width), f32)
    for blocks, weights in ((grads_own, attn_own), (grads_oth, attn_oth)):
        for i in range(each):
            grad_normed_one = grad_normed_one + contract_last(blocks[i], weights[i][:, :lanes_qkv])
    input_grad = grad_residual + norm_back(grad_normed_one, scaled_one, inverse_one, vec[0])

    dbias = jnp.stack([dbias_own, dbias_oth], 1).reshape(cols, width)
    grad_vector = jnp.concatenate(
        [
            jnp.stack(
                [
                    jnp.sum(grad_normed_one * scaled_one, 0),
                    jnp.sum(grad_normed_one, 0),
                    grad_sums[0, :width],
                    grad_sums[1, :width],
                    jnp.sum(grad_residual, 0),
                    jnp.sum(grad_normed_two * scaled_two, 0),
                    jnp.sum(grad_normed_two, 0),
                    jnp.sum(cotangent.astype(f32), 0),
                ]
            ),
            by_place(dbias),
        ],
        0,
    ).astype(bf16)
    vec_part = grad_vector.reshape(cols, vec_shape[0], owners, vec_shape[1]).transpose(0, 2, 1, 3)
    vec_part = jnp.pad(vec_part.reshape(cols, owners, vec_count), ((0, 0), (0, 0), (0, vec_fill)))
    vec_part = by_place(vec_part.reshape(cols, owners, vec_lines, spare))
    vec_here = (vec_part[0::2].astype(f32) + partner(vec_part[1::2]).astype(f32)).astype(bf16)
    vec_here = jnp.pad(
        vec_here, ((0, 0), (0, 0), (0, rows_own - vec_lines), (LANES - spare, 0))
    ).reshape(each, width, LANES)
    total_attn = block_grads(pairs_own, vec_here, received, staged)
    sum_down, sum_up = scatter_three(two_down), scatter_three(two_up)
    one_attn = scatter_one(total_attn)
    sum_down, sum_up, one_attn = together(sum_down, sum_up, one_attn)
    sum_attn = scatter_three(scatter_two(one_attn))
    sum_qkv = sum_attn[:, : 3 * piece].reshape(rows_own, 3, piece)
    sum_out = sum_attn[:, 3 * piece : width].T
    sum_vector = sum_attn[:vec_lines, width:].reshape(-1)[:vec_count].reshape(vec_shape)

    qkv_m, qkv_v, qkv_w = adamw(
        qkv_weight, sum_qkv, qkv_first, qkv_second, 1.5 * D ** (-0.5), decay_rate
    )
    out_m, out_v, out_w = adamw(
        out_weight, sum_out, out_first, out_second, 1.5 * (D // 64) ** (-0.5), decay_rate
    )
    up_m, up_v, up_w = adamw(up_weight, sum_up, up_first, up_second, 1.5 * D ** (-0.5), decay_rate)
    down_m, down_v, down_w = adamw(
        down_weight, sum_down.T, down_first, down_second, 1.5 * FF ** (-0.5), decay_rate
    )
    vec_m, vec_v, vec_w = adamw(vectors, sum_vector, vectors_first, vectors_second, 0.5, 0.0)
    return (
        layer_out,
        input_grad,
        qkv_m,
        qkv_v,
        qkv_w,
        out_m,
        out_v,
        out_w,
        up_m,
        up_v,
        up_w,
        down_m,
        down_v,
        down_w,
        vec_m,
        vec_v,
        vec_w,
    )


def solution(mesh):
    tokens = P(("dp", "row", "col"), None)
    qkv = P(("dp", "row"), None, "col")
    tall = P("col", ("dp", "row"))
    up = P(("dp", "row"), "col")
    state = (qkv, tall, up, tall, tall)
    return jax.shard_map(
        local,
        mesh=mesh,
        in_specs=(tokens, tokens, P(("dp", "row"), None)) + state * 3,
        out_specs=(tokens, tokens)
        + (qkv,) * 3
        + (tall,) * 3
        + (up,) * 3
        + (tall,) * 3
        + (tall,) * 3,
        check_vma=False,
    )
```

```python
import functools

import jax
import jax.numpy as jnp
from jax import lax
from jax.experimental import pallas as pl
from jax.experimental.pallas import tpu as pltpu
from jax.sharding import PartitionSpec as P

D = 1088
HEAD_DIM = 64
FF = 4352
SEQ = 1024
STEP = 5

LANES = 128


beta_one = 0.9
beta_two = 0.999
epsilon = 1e-08
decay_rate = 0.1
masked_score = -1000000000.0

f32 = jnp.float32
bf16 = jnp.bfloat16


def contract(left, right, left_dim, right_dim):
    return lax.dot_general(
        left, right, (((left_dim,), (right_dim,)), ((), ())), preferred_element_type=f32
    )


def contract_first(left, right):
    return contract(left, right, 0, 0)


def contract_last(left, right):
    return contract(left, right, 1, 1)


def normalize(rows, gain, shift):
    row_mean = jnp.mean(rows, -1, keepdims=True)
    centred = rows - row_mean
    inverse = lax.rsqrt(jnp.mean(centred * centred, -1, keepdims=True) + 1e-05)
    scaled = centred * inverse
    return (scaled * gain + shift, scaled, inverse)


def norm_back(grad_out, scaled, inverse, gain):
    grad_scaled = grad_out * gain
    return inverse * (
        grad_scaled
        - jnp.mean(grad_scaled, -1, keepdims=True)
        - scaled * jnp.mean(grad_scaled * scaled, -1, keepdims=True)
    )


def gelu_tanh(values):
    return jax.nn.gelu(values, approximate=True)


def adamw(weight, gradient, moment_one, moment_two, step_rate, shrink):
    moment_one = beta_one * moment_one + (1.0 - beta_one) * gradient
    moment_two = beta_two * moment_two + (1.0 - beta_two) * gradient * gradient
    update = (
        moment_one
        / (1.0 - beta_one**STEP)
        / (jnp.sqrt(moment_two / (1.0 - beta_two**STEP)) + epsilon)
    )
    return (moment_one, moment_two, weight - step_rate * (update + shrink * weight))


def mask_tables(kseg_own, kseg_oth, qseg, bias_own, bias_oth):
    count = bias_own.shape[0]
    key_place = lax.broadcasted_iota(jnp.int32, (count, count), 0)
    query_place = lax.broadcasted_iota(jnp.int32, (count, count), 1)
    same = kseg_own[...] == qseg[...]
    bias_own[...] = jnp.where(same & (key_place <= query_place), 0.0, masked_score)
    bias_oth[...] = jnp.where(kseg_oth[...] == qseg[...], 0.0, masked_score)


def head_lanes(block, half):
    lane = lax.broadcasted_iota(jnp.int32, block.shape, 1)
    return jnp.where((lane // HEAD_DIM) == half, block, jnp.zeros_like(block))


def attention_forward(
    later, qseg, kseg_own, kseg_oth, q, k_own, v_own, k_oth, v_oth, out, lse, bias_own, bias_oth
):
    pair = pl.program_id(0)
    count = q.shape[0]
    step = count // 2

    @pl.when(pair == 0)
    def _():
        mask_tables(kseg_own, kseg_oth, qseg, bias_own, bias_oth)

    def body(with_other):
        queries = q[...] * jnp.asarray(HEAD_DIM**-0.5, bf16)
        values_own = v_own[...].astype(f32).T.astype(bf16)
        values_oth = v_oth[...].astype(f32).T.astype(bf16) if with_other else None
        for part in range(2):
            cols = slice(part * step, (part + 1) * step)
            seen = (part + 1) * step
            pieces = []
            for half in range(2):
                q_head = head_lanes(queries[cols], half)
                rows = slice(half * HEAD_DIM, (half + 1) * HEAD_DIM)
                s_own = contract_last(k_own[:seen], q_head) + bias_own[:seen, cols]
                top = jnp.max(s_own, 0, keepdims=True)
                if with_other:
                    s_oth = contract_last(k_oth[...], q_head) + bias_oth[:, cols]
                    top = jnp.maximum(top, jnp.max(s_oth, 0, keepdims=True))
                e_own = jnp.exp(s_own - top)
                total = jnp.sum(e_own, 0, keepdims=True)
                mixed = jnp.dot(
                    values_own[rows, :seen], e_own.astype(bf16), preferred_element_type=f32
                )
                if with_other:
                    e_oth = jnp.exp(s_oth - top)
                    total = total + jnp.sum(e_oth, 0, keepdims=True)
                    mixed = mixed + jnp.dot(
                        values_oth[rows], e_oth.astype(bf16), preferred_element_type=f32
                    )
                lse[0, half : half + 1, cols] = top + jnp.log(total)
                pieces.append(mixed / total)
            out[cols] = jnp.concatenate(pieces, 0).T.astype(bf16)

    @pl.when(later[0] == 1)
    def _():
        body(True)

    @pl.when(later[0] == 0)
    def _():
        body(False)


def attention_backward(
    later, qseg, kseg_own, kseg_oth, q, k_own, v_own, k_oth, v_oth, grad, out, lse,
    dq, dk_own, dv_own, dk_oth, dv_oth, bias_own, bias_oth,
):
    pair = pl.program_id(0)
    count = q.shape[0]
    step = count // 2

    @pl.when(pair == 0)
    def _():
        mask_tables(kseg_own, kseg_oth, qseg, bias_own, bias_oth)

    def body(with_other):
        scale = jnp.asarray(HEAD_DIM**-0.5, bf16)
        queries = q[...] * scale
        keys_own = k_own[...].astype(f32).T.astype(bf16)
        keys_oth = k_oth[...].astype(f32).T.astype(bf16) if with_other else None
        products = (grad[...].astype(f32) * out[...].astype(f32)).T
        dk_a = [jnp.zeros((step, LANES), f32) for _ in range(2)]
        dv_a = [jnp.zeros((step, LANES), f32) for _ in range(2)]
        dk_b = jnp.zeros((count, LANES), f32)
        dv_b = jnp.zeros((count, LANES), f32)
        for part in range(2):
            cols = slice(part * step, (part + 1) * step)
            pieces = []
            for half in range(2):
                q_head = head_lanes(queries[cols], half)
                g_head = head_lanes(grad[cols], half)
                rows = slice(half * HEAD_DIM, (half + 1) * HEAD_DIM)
                delta = jnp.sum(products[rows, cols], 0, keepdims=True)
                log_total = lse[0, half : half + 1, cols]

                def block(keys, values, bias):
                    probs = jnp.exp(contract_last(keys, q_head) + bias - log_total)
                    d_probs = contract_last(values, g_head)
                    d_scores = (probs * (d_probs - delta)).astype(bf16)
                    dk = jnp.dot(d_scores, q_head, preferred_element_type=f32)
                    dv = jnp.dot(probs.astype(bf16), g_head, preferred_element_type=f32)
                    return (d_scores, dk, dv)

                d_query = jnp.zeros((HEAD_DIM, step), f32)
                for chunk in range(part + 1):
                    span = slice(chunk * step, (chunk + 1) * step)
                    d_scores, dk, dv = block(k_own[span], v_own[span], bias_own[span, cols])
                    dk_a[chunk] = dk_a[chunk] + dk
                    dv_a[chunk] = dv_a[chunk] + dv
                    d_query = d_query + jnp.dot(
                        keys_own[rows, span], d_scores, preferred_element_type=f32
                    )
                if with_other:
                    d_scores, dk, dv = block(k_oth[...], v_oth[...], bias_oth[:, cols])
                    dk_b = dk_b + dk
                    dv_b = dv_b + dv
                    d_query = d_query + jnp.dot(
                        keys_oth[rows], d_scores, preferred_element_type=f32
                    )
                pieces.append(d_query)
            dq[cols] = (jnp.concatenate(pieces, 0).T * HEAD_DIM**-0.5).astype(bf16)
        for chunk in range(2):
            span = slice(chunk * step, (chunk + 1) * step)
            dk_own[span] = dk_a[chunk].astype(bf16)
            dv_own[span] = dv_a[chunk].astype(bf16)
        dk_oth[...] = dk_b.astype(bf16)
        dv_oth[...] = dv_b.astype(bf16)

    @pl.when(later[0] == 1)
    def _():
        body(True)

    @pl.when(later[0] == 0)
    def _():
        body(False)


def attention_specs(count, pairs):
    def whole(shape):
        return pl.BlockSpec(shape, lambda p, later: (0,) * len(shape))

    def lanes(start):
        return pl.BlockSpec((count, LANES), lambda p, later: (0, start + p))

    segments = [whole((1, count)), whole((count, 1)), whole((count, 1))]
    projected = [lanes(0), lanes(pairs), lanes(2 * pairs), lanes(0), lanes(pairs)]
    totals = pl.BlockSpec((1, 2, count), lambda p, later: (p, 0, 0))
    return segments, projected, lanes(0), totals


def attend(later, labels, projected, others):
    count = projected.shape[0]
    pairs = projected.shape[1] // (3 * LANES)
    segments, blocks, wide, totals = attention_specs(count, pairs)
    work = count * count * LANES * pairs * 2
    return pl.pallas_call(
        attention_forward,
        grid_spec=pltpu.PrefetchScalarGridSpec(
            num_scalar_prefetch=1,
            grid=(pairs,),
            in_specs=segments + blocks,
            out_specs=[wide, totals],
            scratch_shapes=[pltpu.VMEM((count, count), f32), pltpu.VMEM((count, count), f32)],
        ),
        out_shape=[
            jax.ShapeDtypeStruct((count, pairs * LANES), bf16),
            jax.ShapeDtypeStruct((pairs, 2, count), f32),
        ],
        compiler_params=pltpu.CompilerParams(vmem_limit_bytes=48 << 20),
        name="attention_forward",
    )(later, *labels, projected, projected, projected, others, others)


def attend_back(later, labels, projected, others, grad, mixed, log_totals):
    count = projected.shape[0]
    pairs = projected.shape[1] // (3 * LANES)
    segments, blocks, wide, totals = attention_specs(count, pairs)
    work = count * count * LANES * pairs * 2
    return pl.pallas_call(
        attention_backward,
        grid_spec=pltpu.PrefetchScalarGridSpec(
            num_scalar_prefetch=1,
            grid=(pairs,),
            in_specs=segments + blocks + [wide, wide, totals],
            out_specs=[wide] * 5,
            scratch_shapes=[pltpu.VMEM((count, count), f32), pltpu.VMEM((count, count), f32)],
        ),
        out_shape=[jax.ShapeDtypeStruct((count, pairs * LANES), bf16)] * 5,
        compiler_params=pltpu.CompilerParams(vmem_limit_bytes=48 << 20),
        name="attention_backward",
    )(later, *labels, projected, projected, projected, others, others, grad, mixed, log_totals)


def place_kernel(spans, piece, sources, biased, continued, places, x, *refs):
    weights, refs = refs[:sources], refs[sources:]
    bias, refs = (refs[0], refs[1:]) if biased else (None, refs)
    before, refs = (refs[0], refs[1:]) if continued else (None, refs)
    out, whole, product = refs
    step = pl.program_id(0)
    each = pl.num_programs(0) // sources

    @pl.when(step == 0)
    def _():
        whole[...] = before[...].astype(f32) if continued else jnp.zeros_like(whole)

    for k, weight in enumerate(weights):

        @pl.when(step // each == k)
        def _(weight=weight):
            product[...] = jnp.dot(x[...], weight[0], preferred_element_type=f32)

    for place in range(x.shape[1] // piece):

        @pl.when(places[step] == place)
        def _(place=place):
            for source, target in spans:
                start = target + place * piece
                block = product[:, source : source + piece]
                if biased:
                    block = block + bias[:, start : start + piece]
                whole[:, start : start + piece] = block

    @pl.when(step == pl.num_programs(0) - 1)
    def _():
        out[...] = whole[...].astype(bf16)


def multiply_and_place(places, x, weights, lanes, lane_block, spans, piece, out_lanes, bias, before):
    count, depth = x.shape
    each = weights[0].shape[0]
    sources = len(weights)

    def fixed(shape):
        return pl.BlockSpec(shape, lambda j, places: (0, 0))

    in_specs = [fixed((count, depth))]
    for k in range(sources):
        in_specs.append(
            pl.BlockSpec(
                (1, depth, lanes),
                lambda j, places, k=k: (jnp.clip(j - k * each, 0, each - 1), 0, lane_block),
            )
        )
    operands = [x, *weights]
    if bias is not None:
        in_specs.append(fixed(bias.shape))
        operands.append(bias)
    if before is not None:
        in_specs.append(fixed(before.shape))
        operands.append(before)
    return pl.pallas_call(
        functools.partial(
            place_kernel, spans, piece, sources, bias is not None, before is not None
        ),
        grid_spec=pltpu.PrefetchScalarGridSpec(
            num_scalar_prefetch=1,
            grid=(each * sources,),
            in_specs=in_specs,
            out_specs=fixed((count, out_lanes)),
            scratch_shapes=[pltpu.VMEM((count, out_lanes), f32), pltpu.VMEM((count, lanes), f32)],
        ),
        out_shape=jax.ShapeDtypeStruct((count, out_lanes), bf16),
        compiler_params=pltpu.CompilerParams(vmem_limit_bytes=48 << 20),
        name="multiply_and_place",
    )(places, *operands)


def split_all(column, cols, write):
    for here in range(cols):

        @pl.when(column[0] == here)
        def _(here=here):
            for k in range(cols):
                write(k % 2, k // 2, here ^ k)


def split_mixed_kernel(piece, cols, lead, column, mixed, own, oth):
    count, lanes = own.shape[1:]
    values = mixed[...].astype(f32)
    before = jnp.zeros((count, lead), f32)
    after = jnp.zeros((count, lanes - lead - piece), f32)

    def write(which, i, c):
        block = values[:, c * piece : (c + 1) * piece]
        (own, oth)[which][i] = jnp.concatenate([before, block, after], 1).astype(bf16)

    split_all(column, cols, write)


def split_grads_kernel(piece, cols, column, dq, dk, dv, back, own, oth, sums):
    count, lanes = own.shape[1:]
    wide = dq.shape[1]
    grads = [
        dq[...].astype(f32),
        dk[...].astype(f32) + back[:, :wide].astype(f32),
        dv[...].astype(f32) + back[:, wide:].astype(f32),
    ]
    sums[0:1] = jnp.sum(grads[0], 0, keepdims=True)
    sums[1:2] = jnp.sum(grads[2], 0, keepdims=True)
    after = jnp.zeros((count, lanes - 3 * piece), f32)

    def write(which, i, c):
        blocks = [g[:, c * piece : (c + 1) * piece] for g in grads]
        (own, oth)[which][i] = jnp.concatenate([*blocks, after], 1).astype(bf16)

    split_all(column, cols, write)


def whole_specs(shapes):
    return [pl.BlockSpec(s, lambda i, p, n=len(s): (0,) * n) for s in shapes]


def split_call(kernel, column, operands, out_shapes, name):
    moved = sum(x.size * x.dtype.itemsize for x in operands) * 2
    return pl.pallas_call(
        kernel,
        grid_spec=pltpu.PrefetchScalarGridSpec(
            num_scalar_prefetch=1,
            grid=(1,),
            in_specs=whole_specs([x.shape for x in operands]),
            out_specs=whole_specs([s.shape for s in out_shapes]),
        ),
        out_shape=out_shapes,
        compiler_params=pltpu.CompilerParams(vmem_limit_bytes=48 << 20),
        name=name,
    )(column, *operands)


def block_grads_kernel(counts, has_vec, has_received, split, place, *refs):
    refs = list(refs)
    step = pl.program_id(0)
    lefts = [refs.pop(0) for _ in counts]
    rights = [[refs.pop(0) for _ in range(count)] for count in counts]
    vec_part = refs.pop(0) if has_vec else None
    received = refs.pop(0) if has_received else None
    width = lefts[0].shape[0]
    quarter = width // 4

    def value(start, which):
        rows = pl.ds(start, quarter)
        if counts[0] > 1:
            whole = contract_last(lefts[0][rows], rights[0][which][...])
        else:
            one, two = [
                jnp.dot(left[rows], right[0][0], preferred_element_type=f32)
                for left, right in zip(lefts, rights)
            ]
            lead = one.shape[1] - LANES
            whole = jnp.concatenate(
                [one[:, :lead], one[:, lead:] + two[:, :LANES], two[:, LANES:]], 1
            )
        if has_vec:
            more = whole[:, -LANES:] + vec_part[0, rows].astype(f32)
            whole = jnp.concatenate([whole[:, :-LANES], more], 1)
        if has_received:
            whole = whole + received[0, rows].astype(f32)
        return whole.astype(bf16)

    for i in range(2):

        @pl.when(step == i)
        def _(i=i):
            if not split:
                for k in range(4):
                    refs[0][0, k * quarter : (k + 1) * quarter] = value(k * quarter, i)
                return
            first_keep, first_send, second_keep, second_send = refs
            half = width // 2
            first_keep[0] = value(pl.multiple_of(place[0] * half, 16), i)
            first_send[0] = value(pl.multiple_of((1 - place[0]) * half, 16), i)
            second = (second_keep, second_send)[i]
            for dp in range(2):
                second[dp] = value(dp * half + quarter, i)


def block_grads(pairs, vec_part, received, split):
    lefts, rights = zip(*pairs)
    rights = [r if isinstance(r, list) else [r] for r in rights]
    width, count = lefts[0].shape
    each = 2
    lanes = width if len(pairs) == 1 else -(-width // LANES) * LANES
    place = lax.axis_index("dp").reshape(1).astype(jnp.int32)

    def fixed(shape):
        return pl.BlockSpec(shape, lambda i, place: (0,) * len(shape))

    def step(shape):
        return pl.BlockSpec((1, *shape[1:]), lambda i, place: (i, 0, 0))

    flat = [r for right in rights for r in right]
    more = [x for x in (vec_part, received) if x is not None]
    in_specs = [fixed(x.shape) for x in lefts]
    in_specs += [step(x.shape) if x.ndim == 3 else fixed(x.shape) for x in flat]
    in_specs += [step(x.shape) for x in more]
    if split:
        part = (each, width // 4, lanes)
        out_specs = [step(part), step(part), fixed(part), fixed(part)]
        out_shape = [jax.ShapeDtypeStruct(part, bf16)] * 4
    else:
        out_specs = step((each, width, lanes))
        out_shape = jax.ShapeDtypeStruct((each, width, lanes), bf16)
    return pl.pallas_call(
        functools.partial(
            block_grads_kernel,
            [len(r) for r in rights],
            vec_part is not None,
            received is not None,
            split,
        ),
        grid_spec=pltpu.PrefetchScalarGridSpec(
            num_scalar_prefetch=1,
            grid=(each,),
            in_specs=in_specs,
            out_specs=out_specs,
        ),
        out_shape=out_shape,
        compiler_params=pltpu.CompilerParams(vmem_limit_bytes=48 << 20),
        name="block_grads",
    )(place, *lefts, *flat, *more)


AXES = ("col", "dp", "row")


def planes():
    owners = lax.axis_size("dp") * lax.axis_size("row")
    cols = lax.axis_size("col")
    return [
        [c * owners + k for c in range(p, cols, 2) for k in range(owners)] for p in range(2)
    ]


def flip_col(block, bit):
    return lax.ppermute(block, "col", [(c, c ^ bit) for c in range(lax.axis_size("col"))])


def partner(block):
    return flip_col(block, 1)


def flip_dp(block):
    return lax.ppermute(block, "dp", [(0, 1), (1, 0)])


def shift_row(block, by):
    count = lax.axis_size("row")
    return lax.ppermute(block, "row", [(i, (i + by) % count) for i in range(count)])


def by_place(blocks):
    column = lax.axis_index("col")
    pairs = blocks.reshape(-1, 2, *blocks.shape[1:])
    pairs = jnp.where(column % 2 == 1, pairs[:, ::-1], pairs)
    return upper_bit(pairs).reshape(blocks.shape)


def upper_bit(blocks):
    return jnp.where(lax.axis_index("col") // 2 == 1, blocks[::-1], blocks)


def short_rows():
    return lax.axis_size("row") == 4 and lax.axis_size("dp") == 2 and lax.axis_size("col") == 4


def assemble_kernel(place, *refs):
    sources, (out, held, sems_in, sems_out) = refs[:-4], refs[-4:]
    dp, row = place[0], place[1]
    order = (
        [(0, 0, 0), (0, 0, 1), (1, 0, 0), (1, 0, 1), (0, 0, 2), (0, 0, 3), (0, 1, 2), (0, 1, 3)]
        + [(0, 1, 0), (0, 1, 1), (1, 1, 0), (1, 1, 1)]
        + [(1, 0, 2), (1, 0, 3), (1, 1, 2), (1, 1, 3)]
    )
    blocks = [source.at[i] for source in sources for i in range(source.shape[0])]
    copies_in, copies_out = [], []
    for k, (block, (over_x, over_y, behind)) in enumerate(zip(blocks, order)):
        target = over_x * 8 + (1 - dp if over_y else dp) * 4 + lax.rem(row + 4 - behind, 4)
        copies_in.append(pltpu.make_async_copy(block, held.at[k], sems_in.at[k]))
        copies_out.append(pltpu.make_async_copy(held.at[k], out.at[target], sems_out.at[k]))
    for copy in copies_in:
        copy.start()
    for copy_in, copy_out in zip(copies_in, copies_out):
        copy_in.wait()
        copy_out.start()
    for copy in copies_out:
        copy.wait()


def assemble(pieces):
    rows, lanes = pieces[0].shape[-2:]
    pieces = [p.reshape(-1, rows, lanes) for p in pieces]
    place = jnp.stack([lax.axis_index("dp"), lax.axis_index("row")]).astype(jnp.int32)
    anywhere = pl.BlockSpec(memory_space=pl.ANY)
    out = pl.pallas_call(
        assemble_kernel,
        grid_spec=pltpu.PrefetchScalarGridSpec(
            num_scalar_prefetch=1,
            grid=(1,),
            in_specs=[anywhere] * len(pieces),
            out_specs=anywhere,
            scratch_shapes=[
                pltpu.VMEM((16, rows, lanes), bf16),
                pltpu.SemaphoreType.DMA((16,)),
                pltpu.SemaphoreType.DMA((16,)),
            ],
        ),
        out_shape=jax.ShapeDtypeStruct((16, rows, lanes), bf16),
        compiler_params=pltpu.CompilerParams(vmem_limit_bytes=48 << 20),
        name="assemble",
    )(place, *pieces)
    return out.reshape(2, -1, lanes)


def spread_rows(block):
    return [block] + [shift_row(block, m) for m in range(1, 4)]


def spread_one(pieces):
    first, second = jnp.stack(pieces[:2]), jnp.stack(pieces[2:])
    return [first, flip_col(first, 2), second, flip_dp(second)]


def spread_two(pieces):
    first_y = flip_dp(jnp.stack(pieces[:2]))
    return [*pieces, first_y, flip_col(jnp.stack(pieces[2:]), 2)]


def gather_groups(block):
    whole = lax.all_gather(block, AXES, axis=0, tiled=False, axis_index_groups=planes())
    return upper_bit(whole.reshape(lax.axis_size("col") // 2, -1, block.shape[-1]))


def together(*arrays):
    return lax.optimization_barrier(arrays)


def added(one, other):
    return (one.astype(f32) + other.astype(f32)).astype(bf16)


def at_place(array, which, axis):
    return lax.dynamic_index_in_dim(array, which, axis, keepdims=False)


def scatter_one(blocks):
    if not short_rows():
        return blocks
    first_keep, first_send, second_keep, second_send = blocks
    first_y, second_x = flip_dp(first_send), flip_col(second_send, 2)
    return added(first_keep, first_y), added(second_keep, second_x)


def scatter_two(halves):
    if not short_rows():
        return halves
    dp = lax.axis_index("dp")
    first, second = halves
    first_x = flip_col(first[1], 2)
    second_y = flip_dp(at_place(second, 1 - dp, 0))
    both = jnp.concatenate(
        [added(first[0], first_x), added(at_place(second, dp, 0), second_y)], 0
    )
    return both.reshape(4, -1, both.shape[-1])


def scatter_three(rows):
    if not short_rows():
        flat = upper_bit(rows).reshape(-1, rows.shape[-1])
        return lax.psum_scatter(
            flat, AXES, scatter_dimension=0, tiled=True, axis_index_groups=planes()
        ).astype(f32)
    row = lax.axis_index("row")
    total = at_place(rows, row, 0).astype(f32)
    for m in range(1, 4):
        total = total + shift_row(at_place(rows, (row + m) % 4, 0), m).astype(f32)
    return total


def local(
    hidden_in,
    cotangent,
    segments,
    qkv_weight,
    out_weight,
    up_weight,
    down_weight,
    vectors,
    qkv_first,
    out_first,
    up_first,
    down_first,
    vectors_first,
    qkv_second,
    out_second,
    up_second,
    down_second,
    vectors_second,
):
    column = lax.axis_index("col")
    cols = lax.axis_size("col")
    here, width = hidden_in.shape
    rows_own = qkv_weight.shape[0]
    owners = lax.axis_size("dp") * lax.axis_size("row")
    piece = qkv_weight.shape[2]
    halves = SEQ // here
    each = cols // 2
    column_word = column.reshape(1).astype(jnp.int32)
    places_own = (column ^ (2 * jnp.arange(each))).astype(jnp.int32)
    places_oth = (column ^ (2 * jnp.arange(each) + 1)).astype(jnp.int32)
    later = lax.rem(column, halves).reshape(1).astype(jnp.int32)
    padded = -(-width // LANES) * LANES
    spare = padded - width
    lanes_qkv = -(-3 * piece // LANES) * LANES
    lead_out = 3 * piece // LANES * LANES
    lanes_out = padded - lead_out

    vec_shape = vectors.shape
    vec_count = vec_shape[0] * vec_shape[1]
    vec_lines = -(-vec_count // spare)
    vec_fill = vec_lines * spare - vec_count
    vec_lanes = jnp.pad(vectors.reshape(vec_count).astype(bf16), (0, vec_fill))
    attn_block = jnp.concatenate(
        [
            qkv_weight.reshape(rows_own, 3 * piece).astype(bf16),
            out_weight.T.astype(bf16),
            jnp.pad(vec_lanes.reshape(vec_lines, spare), ((0, rows_own - vec_lines), (0, 0))),
        ],
        1,
    )
    up_block, down_block = up_weight.astype(bf16), down_weight.T.astype(bf16)
    staged = short_rows()
    if staged:
        attn_rows = spread_rows(attn_block)
        up_block, attn_rows = together(up_block, attn_rows)
        attn_one = spread_one(attn_rows)
        up_rows = spread_rows(up_block)
        down_block, up_rows = together(down_block, up_rows)
        down_rows = spread_rows(down_block)
        attn_own = assemble(spread_two(attn_one))
        up_one = spread_one(up_rows)
    else:
        attn_own, up_own, down_own = [
            gather_groups(b) for b in (attn_block, up_block, down_block)
        ]
    vec_own = attn_own.reshape(each, owners, rows_own, padded)[:, :, :vec_lines, width:]
    vec_oth = partner(vec_own)
    attn_oth = partner(attn_own)

    def vec_rows(lines):
        lines = lines.reshape(each, owners, vec_lines * spare)[:, :, :vec_count]
        lines = lines.reshape(each, owners, *vec_shape).transpose(0, 2, 1, 3)
        return lines.reshape(each, vec_shape[0], width).astype(f32)

    vec = jnp.stack([vec_rows(vec_own), vec_rows(vec_oth)], 1).reshape(cols, -1, width)
    vec = by_place(vec).reshape(-1, width)

    def widen(row):
        return jnp.pad(row, (0, spare))

    inputs = hidden_in.astype(f32)
    normed_one, scaled_one, inverse_one = normalize(inputs, vec[0], vec[1])
    normed_low = normed_one.astype(bf16)
    if staged:
        normed_low, up_one = together(normed_low, up_one)
        up_two = spread_two(up_one)
    bias = jnp.concatenate([widen(vec[2]), jnp.zeros((padded,), f32), widen(vec[3])]).reshape(1, -1)
    spans = tuple((part * piece, part * padded) for part in range(3))
    projected = None
    for places, weights in ((places_own, attn_own), (places_oth, attn_oth)):
        if staged and projected is not None:
            projected, down_rows = together(projected, down_rows)
        projected = multiply_and_place(
            places, normed_low, [weights], lanes_qkv, 0, spans, piece, 3 * padded, bias, projected
        )
    if staged:
        projected, down_one = together(projected, spread_one(down_rows))
        down_two = spread_two(down_one)
    ahead = [(c, c + 1) for c in range(cols - 1) if c % halves + 1 < halves]
    behind = [(b, a) for a, b in ahead]
    others = lax.ppermute(projected[:, padded:], "col", ahead)

    own_half = lax.dynamic_slice_in_dim(segments.reshape(-1), column * here, here, 0)
    first_half = lax.dynamic_slice_in_dim(
        segments.reshape(-1), (column - lax.rem(column, halves)) * here, here, 0
    )
    labels = (own_half.reshape(1, here), own_half.reshape(here, 1), first_half.reshape(here, 1))
    mixed, log_totals = attend(later, labels, projected, others)
    if staged:
        mixed, up_two = together(mixed, up_two)
        up_own = assemble(up_two)
    up_oth = partner(up_own)
    mixed_shape = jax.ShapeDtypeStruct((each, here, lanes_out), bf16)
    lead = 3 * piece - lead_out
    mixed_own, mixed_oth = split_call(
        functools.partial(split_mixed_kernel, piece, cols, lead),
        column_word,
        [mixed],
        [mixed_shape] * 2,
        "split_mixed",
    )
    residual = inputs + vec[4]
    for blocks, weights in ((mixed_own, attn_own), (mixed_oth, attn_oth)):
        for i in range(each):
            residual = residual + contract_last(blocks[i], weights[i][:, lead_out:])
    normed_two, scaled_two, inverse_two = normalize(residual, vec[5], vec[6])
    normed_two_low = normed_two.astype(bf16)

    bias_up = by_place(vec[8:])
    bias_own, bias_oth = bias_up[0::2], bias_up[1::2]

    def up_part(ups, biases):
        return [
            jnp.dot(normed_two_low, ups[i], preferred_element_type=f32) + biases[i]
            for i in range(each)
        ]

    linear_own = up_part(up_own, bias_own)
    if staged:
        linear_own, down_two = together(linear_own, down_two)
        down_own = assemble(down_two)
    down_oth = partner(down_own)
    linear_oth = up_part(up_oth, bias_oth)

    branch = jnp.zeros((here, width), f32)

    def forward_part(linears, downs, branch):
        lows, pullbacks = [], []
        for i in range(each):
            active, pullback = jax.vjp(gelu_tanh, linears[i])
            lows.append(active.astype(bf16))
            pullbacks.append(pullback)
            branch = branch + contract_last(lows[i], downs[i])
        return lows, pullbacks, branch

    left_down, left_up = cotangent.T, normed_two_low.T

    def turned(rights):
        return [r.T for r in rights]

    lows_oth, pull_oth, branch = forward_part(linear_oth, down_oth, branch)
    sent_down = block_grads([(left_down, turned(lows_oth))], None, None, False)
    linear_own, sent_down = together(linear_own, sent_down)
    received_down = partner(sent_down)
    lows_own, pull_own, branch = forward_part(linear_own, down_own, branch)
    total_down = block_grads([(left_down, turned(lows_own))], None, received_down, staged)
    layer_out = (residual + branch + vec[7]).astype(bf16)
    down_oth, total_down = together(down_oth, total_down)
    grad_normed_two = jnp.zeros((here, width), f32)

    def backward_part(ups, downs, pullbacks, grad_normed_two):
        lows, sums = [], []
        for i in range(each):
            grad_active = jnp.dot(cotangent, downs[i], preferred_element_type=f32)
            grad_linear = pullbacks[i](grad_active)[0]
            lows.append(grad_linear.astype(bf16))
            sums.append(jnp.sum(grad_linear, 0))
            grad_normed_two = grad_normed_two + contract_last(lows[i], ups[i])
        return lows, sums, grad_normed_two

    dups_oth, dbias_oth, grad_normed_two = backward_part(
        up_oth, down_oth, pull_oth, grad_normed_two
    )
    one_down = scatter_one(total_down)
    sent_up = block_grads([(left_up, turned(dups_oth))], None, None, False)
    down_own, sent_up = together(down_own, sent_up)
    received_up = partner(sent_up)
    dups_own, dbias_own, grad_normed_two = backward_part(
        up_own, down_own, pull_own, grad_normed_two
    )

    grad_residual = cotangent.astype(f32) + norm_back(
        grad_normed_two, scaled_two, inverse_two, vec[5]
    )
    grad_residual_low = grad_residual.astype(bf16)
    grad_mixed = multiply_and_place(
        jnp.concatenate([places_own, places_oth]),
        grad_residual_low,
        [attn_own, attn_oth],
        lanes_out,
        lead_out // lanes_out,
        ((lead, 0),),
        piece,
        padded,
        None,
        None,
    )
    total_up = block_grads([(left_up, turned(dups_own))], None, received_up, staged)
    grad_mixed, total_up, one_down = together(grad_mixed, total_up, one_down)
    two_down = scatter_two(one_down)
    dq, dk_own, dv_own, dk_oth, dv_oth = attend_back(
        later, labels, projected, others, grad_mixed, mixed, log_totals
    )
    one_up = scatter_one(total_up)
    dq, dk_own, dv_own, dk_oth, dv_oth, one_up, two_down = together(
        dq, dk_own, dv_own, dk_oth, dv_oth, one_up, two_down
    )
    back = lax.ppermute(jnp.concatenate([dk_oth, dv_oth], 1), "col", behind)
    grads_shape = jax.ShapeDtypeStruct((each, here, lanes_qkv), bf16)
    grads_own, grads_oth, grad_sums = split_call(
        functools.partial(split_grads_kernel, piece, cols),
        column_word,
        [dq, dk_own, dv_own, back],
        [grads_shape, grads_shape, jax.ShapeDtypeStruct((8, padded), f32)],
        "split_grads",
    )
    two_up = scatter_two(one_up)
    left_one, left_two = normed_low.T, grad_residual_low.T
    pairs_oth = [(left_one, grads_oth), (left_two, mixed_oth)]
    pairs_own = [(left_one, grads_own), (left_two, mixed_own)]
    received = partner(block_grads(pairs_oth, None, None, False))
    grad_normed_one = jnp.zeros((here, width), f32)
    for blocks, weights in ((grads_own, attn_own), (grads_oth, attn_oth)):
        for i in range(each):
            grad_normed_one = grad_normed_one + contract_last(blocks[i], weights[i][:, :lanes_qkv])
    input_grad = grad_residual + norm_back(grad_normed_one, scaled_one, inverse_one, vec[0])

    dbias = jnp.stack([jnp.stack(dbias_own), jnp.stack(dbias_oth)], 1).reshape(cols, width)
    grad_vector = jnp.concatenate(
        [
            jnp.stack(
                [
                    jnp.sum(grad_normed_one * scaled_one, 0),
                    jnp.sum(grad_normed_one, 0),
                    grad_sums[0, :width],
                    grad_sums[1, :width],
                    jnp.sum(grad_residual, 0),
                    jnp.sum(grad_normed_two * scaled_two, 0),
                    jnp.sum(grad_normed_two, 0),
                    jnp.sum(cotangent.astype(f32), 0),
                ]
            ),
            by_place(dbias),
        ],
        0,
    ).astype(bf16)
    vec_part = grad_vector.reshape(cols, vec_shape[0], owners, vec_shape[1]).transpose(0, 2, 1, 3)
    vec_part = jnp.pad(vec_part.reshape(cols, owners, vec_count), ((0, 0), (0, 0), (0, vec_fill)))
    vec_part = by_place(vec_part.reshape(cols, owners, vec_lines, spare))
    vec_here = (vec_part[0::2].astype(f32) + partner(vec_part[1::2]).astype(f32)).astype(bf16)
    vec_here = jnp.pad(
        vec_here, ((0, 0), (0, 0), (0, rows_own - vec_lines), (LANES - spare, 0))
    ).reshape(each, width, LANES)
    total_attn = block_grads(pairs_own, vec_here, received, staged)
    sum_down, sum_up = scatter_three(two_down), scatter_three(two_up)
    sum_attn = scatter_three(scatter_two(scatter_one(total_attn)))
    sum_qkv = sum_attn[:, : 3 * piece].reshape(rows_own, 3, piece)
    sum_out = sum_attn[:, 3 * piece : width].T
    sum_vector = sum_attn[:vec_lines, width:].reshape(-1)[:vec_count].reshape(vec_shape)

    qkv_m, qkv_v, qkv_w = adamw(
        qkv_weight, sum_qkv, qkv_first, qkv_second, 1.5 * D ** (-0.5), decay_rate
    )
    out_m, out_v, out_w = adamw(
        out_weight, sum_out, out_first, out_second, 1.5 * (D // 64) ** (-0.5), decay_rate
    )
    up_m, up_v, up_w = adamw(up_weight, sum_up, up_first, up_second, 1.5 * D ** (-0.5), decay_rate)
    down_m, down_v, down_w = adamw(
        down_weight, sum_down.T, down_first, down_second, 1.5 * FF ** (-0.5), decay_rate
    )
    vec_m, vec_v, vec_w = adamw(vectors, sum_vector, vectors_first, vectors_second, 0.5, 0.0)
    return (
        layer_out,
        input_grad,
        qkv_m,
        qkv_v,
        qkv_w,
        out_m,
        out_v,
        out_w,
        up_m,
        up_v,
        up_w,
        down_m,
        down_v,
        down_w,
        vec_m,
        vec_v,
        vec_w,
    )


def solution(mesh):
    tokens = P(("dp", "row", "col"), None)
    qkv = P(("dp", "row"), None, "col")
    tall = P("col", ("dp", "row"))
    up = P(("dp", "row"), "col")
    state = (qkv, tall, up, tall, tall)
    return jax.shard_map(
        local,
        mesh=mesh,
        in_specs=(tokens, tokens, P(("dp", "row"), None)) + state * 3,
        out_specs=(tokens, tokens)
        + (qkv,) * 3
        + (tall,) * 3
        + (up,) * 3
        + (tall,) * 3
        + (tall,) * 3,
        check_vma=False,
    )
```
